32 devices in a mesh: ctx: 8 (over z, x), fsdp: 4 (over y, core).
Axes of the slice: x: 2, y: 2, z: 4, core: 2. Of those that a mesh axis runs over, the one named last changes fastest.
Arguments:
- tokens: bfloat16 [12, 8, 2, 128, 1024], P('fsdp', 'ctx'), may hold values from -6 to 6
- cotangent: bfloat16 [12, 8, 2, 128, 1024], P('fsdp', 'ctx'), may hold values from -6 to 6
- query_weight: bfloat16 [1024, 1024], P('fsdp'), may hold values from -0.1875 to 0.1875
- key_weight: bfloat16 [1024, 1024], P('fsdp'), may hold values from -0.1875 to 0.1875
- value_weight: bfloat16 [1024, 1024], P('fsdp'), may hold values from -0.1875 to 0.1875
- output_weight: bfloat16 [1024, 1024], P('fsdp'), may hold values from -3 to 3
- gate_weight: bfloat16 [1024, 2816], P('fsdp'), may hold values from -0.1875 to 0.1875
- up_weight: bfloat16 [1024, 2816], P('fsdp'), may hold values from -0.1875 to 0.1875
- down_weight: bfloat16 [2816, 1024], P('fsdp'), may hold values from -0.109375 to 0.109375
- first_gain: bfloat16 [1024], P('fsdp'), may hold values from 0.099609375 to 1.8984375
- second_gain: bfloat16 [1024], P('fsdp'), may hold values from 0.099609375 to 1.8984375
- cache_keys: bfloat16 [12, 16384, 1024], P('fsdp', 'ctx'), may hold values from -6 to 6
- cache_values: bfloat16 [12, 16384, 1024], P('fsdp', 'ctx'), may hold values from -6 to 6
- block_indices: int32 [12, 8, 2, 2, 8, 4], P('fsdp', 'ctx'), may hold values from 0 to 511, as said below
- partner: int32 [12], P('fsdp'), may hold values from 0 to 2
Outputs:
- layer_output: bfloat16 [12, 8, 2, 128, 1024], P('fsdp', 'ctx')
- input_gradient: float32 [12, 8, 2, 128, 1024], P('fsdp', 'ctx')
- gradient_query: float32 [1024, 1024], P('fsdp')
- gradient_key: float32 [1024, 1024], P('fsdp')
- gradient_value: float32 [1024, 1024], P('fsdp')
- gradient_output: float32 [1024, 1024], P('fsdp')
- gradient_gate: float32 [1024, 2816], P('fsdp')
- gradient_up: float32 [1024, 2816], P('fsdp')
- gradient_down: float32 [2816, 1024], P('fsdp')
- gradient_first: float32 [1024], P('fsdp')
- gradient_second: float32 [1024], P('fsdp')
The draws below stay inside these ranges and needn't reach their ends.
Inputs may be any that keep to these rules, and one draw needn't show every extreme that they name: `block_indices`: entry [s, i, c, n, h, k] is the k-th cache block read by query block n of the piece stored at [s, i, c], head h. A value b below 256 names block b of sequence s's own cache, b - 256 block b - 256 of its partner's; block m of a cache lies on ctx device m // 32. The 128 values of one [s, i] name at most 32 blocks that lie on any one ctx device; in each sequence one ctx device is named exactly 32 times by the values of every [s, i]. Values may repeat. `partner`: index, within the 3 sequences of the same fsdp group, of the sequence whose cache the partner blocks read; it may be the sequence itself.
All inputs are finite; a program needn't handle non-finite values.
Results may differ from the reference program's by a relative error of at most 0.023.
Values may be sent and summed in bfloat16 or wider, within the bound.
A program may use at most 512 MiB of HBM per device.

```python
import math
import jax
import jax.numpy as jnp
from jax import lax

D = 1024
FF = 2816
HEADS = 8
HEAD_DIM = 128
HALF = 128
MICRO = 3
BLOCK = 64
TOPK = 4
CACHE = 16384
LENGTH = 2048
SEQS = 12
QBH = 2
NCB = 256
CB_DEV = 32
REQ = 128
CAP = 32
N_CTX = 8


def draw_block_indices(key, part):
    key = jax.random.fold_in(key, 11)
    sequence_keys = jax.random.split(key, SEQS)

    def one_sequence(sequence_key):
        owner_key, device_key = jax.random.split(sequence_key)
        busiest = jax.random.randint(owner_key, (), 0, N_CTX)
        device_keys = jax.random.split(device_key, N_CTX)

        def one_device(single_key):
            first_key, second_key, third_key, fourth_key = jax.random.split(single_key, 4)
            slots = jnp.arange(N_CTX * CAP, dtype=jnp.int32)
            holder = slots // CAP
            order = jax.random.permutation(first_key, N_CTX * CAP).astype(jnp.int32)
            priority = jnp.where(holder == busiest, order - N_CTX * CAP, order)
            chosen = jnp.argsort(priority, stable=True)[:REQ].astype(jnp.int32)
            owners = jax.random.permutation(second_key, chosen // CAP)
            side = jax.random.randint(third_key, (REQ,), 0, 2)
            within = jax.random.randint(fourth_key, (REQ,), 0, CB_DEV)
            values = side * NCB + owners * CB_DEV + within
            return values.reshape(2, QBH, HEADS, TOPK)
        return jax.vmap(one_device)(device_keys)
    return jax.vmap(one_sequence)(sequence_keys).astype(jnp.int32)


def plant(values, stream_key, least, largest):
    longest = values.shape.index(max(values.shape))
    spots = []
    for shift in (0, 1):
        where = [jax.random.randint(jax.random.fold_in(stream_key, axis), (), 0, length) for axis, length in enumerate(values.shape)]
        where[longest] = (where[longest] + shift) % values.shape[longest]
        spots.append(tuple(where))
    return values.at[spots[0]].set(least).at[spots[1]].set(largest)


def shard_levels(key, dims, shards, low, high):
    def one(dim, blocks):
        draws = jax.random.uniform(jax.random.fold_in(jax.random.fold_in(key, 6), dim), (blocks,), jnp.float32, low / len(shards), high / len(shards))
        return jnp.repeat(jnp.exp(draws), dims[dim] // blocks).reshape((-1,) + (1,) * (len(dims) - dim - 1))

    gain = one(*shards[0])
    for cut in shards[1:]:
        gain = gain * one(*cut)
    return gain


def bell_draw(key, dims, spread, reach, cuts=(), kind=jnp.bfloat16):
    factor_of = shard_levels(key, dims, cuts, -0.22, 0.18) if cuts else 1.0
    drawn = jax.random.normal(key, dims, jnp.float32) * spread * factor_of
    return jnp.minimum(jnp.maximum(drawn, -reach), reach).astype(kind)


def setup_inputs(seed: int = 0) -> dict:
    splits = jax.random.split(jax.random.key(seed), 16)
    tokens = bell_draw(splits[0], (SEQS, N_CTX, 2, HALF, D), 1.0, 6.0, ((0, 4), (1, 8)))
    cotangent = bell_draw(splits[1], (SEQS, N_CTX, 2, HALF, D), 1.0, 6.0, ((0, 4), (1, 8)))
    query_weight = bell_draw(splits[2], (D, D), D ** -0.5, 0.1875, ((0, 4),))
    key_weight = bell_draw(splits[3], (D, D), D ** -0.5, 0.1875, ((0, 4),))
    value_weight = bell_draw(splits[4], (D, D), D ** -0.5, 0.1875, ((0, 4),))
    output_weight = bell_draw(splits[5], (D, D), (max(D // 256, 1)) ** -0.5, 3.0, ((0, 4),))
    gate_weight = bell_draw(splits[6], (D, FF), D ** -0.5, 0.1875, ((0, 4),))
    up_weight = bell_draw(splits[7], (D, FF), D ** -0.5, 0.1875, ((0, 4),))
    down_weight = bell_draw(splits[8], (FF, D), FF ** -0.5, 0.109375, ((0, 4),))
    first_gain = jnp.clip(1.0 + 0.18 * jax.random.normal(splits[9], (D,), jnp.float32), 0.099609375, 1.8984375).astype(jnp.bfloat16)
    second_gain = jnp.clip(1.0 + 0.18 * jax.random.normal(splits[10], (D,), jnp.float32), 0.099609375, 1.8984375).astype(jnp.bfloat16)
    cache_keys = bell_draw(splits[11], (SEQS, CACHE, D), 1.0, 6.0, ((0, 4), (1, 8)))
    cache_values = bell_draw(splits[12], (SEQS, CACHE, D), 1.0, 6.0, ((0, 4), (1, 8)))
    block_indices = draw_block_indices(jax.random.fold_in(splits[15], 71), 0)
    partner = plant(jax.random.randint(splits[14], (SEQS,), 0, MICRO), jax.random.fold_in(splits[14], 1), 0, MICRO - 1).astype(jnp.int32)
    return {"tokens": tokens, "cotangent": cotangent, "query_weight": query_weight, "key_weight": key_weight, "value_weight": value_weight, "output_weight": output_weight, "gate_weight": gate_weight, "up_weight": up_weight, "down_weight": down_weight, "first_gain": first_gain, "second_gain": second_gain, "cache_keys": cache_keys, "cache_values": cache_values, "block_indices": block_indices, "partner": partner}


EPS = 1e-05
EXACT = lax.Precision.HIGHEST

@jax.custom_vjp
def low(v):
    return lax.optimization_barrier(v.astype(jnp.bfloat16)).astype(jnp.float32)

@jax.custom_vjp
def low_back(v):
    return v

def low_keep(v):
    return (low(v), None)

def low_pass(kept, grad):
    return (grad,)

def back_keep(v):
    return (v, None)

def back_low(kept, grad):
    return (low(grad),)
low.defvjp(low_keep, low_pass)
low_back.defvjp(back_keep, back_low)

def natural(array):
    first = array[:, :, 0]
    second = array[:, ::-1, 1]
    joined = jnp.concatenate([first, second], axis=1)
    return joined.reshape((joined.shape[0], -1) + joined.shape[3:])

def dealt(array):
    shaped = array.reshape((array.shape[0], 2 * N_CTX, -1) + array.shape[2:])
    first = shaped[:, :N_CTX]
    second = shaped[:, N_CTX:][:, ::-1]
    return jnp.stack([first, second], axis=2)

def matmul(left, right):
    return jnp.dot(left, right, precision=EXACT)

def normed(value):
    return value * lax.rsqrt(lax.optimization_barrier(jnp.mean(value * value, axis=-1, keepdims=True)) + EPS)

def rotary(value, cosine, sine):
    half = value.shape[-1] // 2
    first = value[..., :half]
    second = value[..., half:]
    return jnp.concatenate([first * cosine - second * sine, second * cosine + first * sine], axis=-1)

def angles(positions):
    inverse = 10000.0 ** (-jnp.arange(HEAD_DIM // 2, dtype=jnp.float32) * 2.0 / HEAD_DIM)
    phase = positions.astype(jnp.float32)[:, None] * inverse[None, :]
    return (jnp.cos(phase)[:, None, :], jnp.sin(phase)[:, None, :])

def attention(query, keys, values, memory_keys, memory_values):
    rows = math.gcd(LENGTH, 512)
    scale = HEAD_DIM ** (-0.5)
    count = rows // BLOCK

    def block(number):
        start = number * rows
        part = lax.dynamic_slice_in_dim(query, start, rows, 0)
        scores = low_back(jnp.einsum('qhd,khd->hqk', part, keys, precision=EXACT) * scale)
        query_place = start + jnp.arange(rows, dtype=jnp.int32)
        key_place = jnp.arange(LENGTH, dtype=jnp.int32)
        visible = query_place[:, None] >= key_place[None, :]
        weights = low(jnp.where(visible[None], jnp.exp(scores), 0.0))
        total = lax.optimization_barrier(jnp.sum(weights, axis=-1))
        weighted = jnp.einsum('hqk,khd->qhd', weights, values, precision=EXACT)
        near_keys = lax.dynamic_slice_in_dim(memory_keys, number * count, count, 0)
        near_values = lax.dynamic_slice_in_dim(memory_values, number * count, count, 0)
        grouped = part.reshape(count, BLOCK, HEADS, HEAD_DIM)
        memory_scores = low_back(jnp.einsum('nqhd,nhmd->nhqm', grouped, near_keys, precision=EXACT) * scale)
        memory_weights = low(jnp.exp(memory_scores))
        total = total + jnp.transpose(lax.optimization_barrier(jnp.sum(memory_weights, axis=-1)), (1, 0, 2)).reshape(HEADS, rows)
        weighted = weighted + jnp.einsum('nhqm,nhmd->nqhd', memory_weights, near_values, precision=EXACT).reshape(rows, HEADS, HEAD_DIM)
        result = low_back(weighted) / jnp.transpose(total)[:, :, None]
        return low(result).reshape(rows, D)
    blocks = lax.map(jax.checkpoint(block), jnp.arange(LENGTH // rows, dtype=jnp.int32))
    return blocks.reshape(LENGTH, D)

def layer(tokens, params, cosine, sine, memory_keys, memory_values):
    query_weight, key_weight, value_weight, output_weight, gate_weight, up_weight, down_weight, first_gain, second_gain = params
    shape = (LENGTH, HEADS, HEAD_DIM)
    normed_in = low(normed(tokens) * first_gain)
    query = low(rotary(low_back(matmul(normed_in, query_weight)).reshape(shape), cosine, sine))
    keys = low(rotary(low_back(matmul(normed_in, key_weight)).reshape(shape), cosine, sine))
    values = low(low_back(matmul(normed_in, value_weight))).reshape(shape)
    mixed = attention(query, keys, values, memory_keys, memory_values)
    middle = tokens + low_back(matmul(mixed, output_weight))
    normed_mid = low(normed(middle) * second_gain)
    gate = low_back(matmul(normed_mid, gate_weight))
    upper = low_back(matmul(normed_mid, up_weight))
    hidden = low(jax.nn.silu(gate) * upper)
    return middle + matmul(hidden, down_weight)

def reference(tokens, cotangent, query_weight, key_weight, value_weight, output_weight, gate_weight, up_weight, down_weight, first_gain, second_gain, cache_keys, cache_values, block_indices, partner):
    weights = tuple((item.astype(jnp.float32) for item in (query_weight, key_weight, value_weight, output_weight, gate_weight, up_weight, down_weight, first_gain, second_gain)))
    inputs = natural(tokens).astype(jnp.float32)
    incoming = natural(cotangent).astype(jnp.float32)
    indices = natural(block_indices)
    cosine, sine = angles(jnp.arange(LENGTH, dtype=jnp.int32))
    key_table = cache_keys.reshape(SEQS, NCB, BLOCK, HEADS, HEAD_DIM)
    value_table = cache_values.reshape(SEQS, NCB, BLOCK, HEADS, HEAD_DIM)
    heads = jnp.arange(HEADS, dtype=jnp.int32)[None, :, None]

    def per_sequence(carry, item):
        number, row, back, index = item
        partner_doc = number // MICRO * MICRO + partner[number]
        side = index // NCB
        block_number = index % NCB
        document = jnp.where(side == 0, number, partner_doc)
        memory_keys = key_table[document, block_number, :, heads, :].astype(jnp.float32).reshape(-1, HEADS, TOPK * BLOCK, HEAD_DIM)
        memory_values = value_table[document, block_number, :, heads, :].astype(jnp.float32).reshape(-1, HEADS, TOPK * BLOCK, HEAD_DIM)

        def forward(row_in, *params):
            return layer(row_in, params, cosine, sine, memory_keys, memory_values)
        result, pull = jax.vjp(forward, row, *weights)
        slopes = pull(back)
        summed = tuple((left + right for left, right in zip(carry, slopes[1:])))
        return (summed, (result.astype(jnp.bfloat16), slopes[0]))
    zeros = tuple((jnp.zeros_like(item) for item in weights))
    totals, (outputs, input_parts) = lax.scan(per_sequence, zeros, (jnp.arange(SEQS, dtype=jnp.int32), inputs, incoming, indices))
    return (dealt(outputs), dealt(input_parts), totals[0], totals[1], totals[2], totals[3], totals[4], totals[5], totals[6], totals[7], totals[8])
```

```python
import functools

import jax
import jax.numpy as jnp
from jax import lax
from jax.experimental import pallas as pl
from jax.experimental.pallas import tpu as pltpu
from jax.sharding import PartitionSpec as P

D = 1024
HEADS = 8
HEAD_DIM = 128
HALF = 128
ROWS = 2 * HALF
BLOCK = 64
TOPK = 4
SIDE = HEADS // 2
SW = SIDE * HEAD_DIM
GROUP = 4
EPS = 1e-05
SCALE = HEAD_DIM**-0.5
LOG2E = 1.4426950408889634
F32 = jnp.float32
BF16 = jnp.bfloat16
EXTRA = 16
SENT = ROWS + EXTRA
VMEM_LIMIT = 56 * 2**20


def nn(a, b):
    return lax.dot_general(a, b, (((1,), (0,)), ((), ())), preferred_element_type=F32)


def nt(a, b):
    return lax.dot_general(a, b, (((1,), (1,)), ((), ())), preferred_element_type=F32)


def tn(a, b):
    return lax.dot_general(a, b, (((0,), (0,)), ((), ())), preferred_element_type=F32)


def params(**more):
    return pltpu.CompilerParams(vmem_limit_bytes=VMEM_LIMIT, **more)


def ring_order(count):
    if count == 8:
        return [0, 2, 4, 6, 7, 5, 3, 1]
    half = count // 2
    return list(range(half)) + [count - 1 - i for i in range(count - half)]


def list_base(count):
    return 1 + 2 * count


def list_at(owner, micro, side, micros, cap):
    return ((owner * micros + micro) * 2 + side) * (cap + 1)


def make_meta(indices, partner, cb_dev, count):
    micros = indices.shape[0]
    here = lax.axis_index("ctx")
    order = ring_order(count)
    place = sum(jnp.where(here == d, p, 0) for p, d in enumerate(order))
    steps = jnp.arange(count, dtype=jnp.int32)
    at = jnp.stack([(place - steps) % count, (place + steps) % count], axis=1)
    owners = sum(jnp.where(at == p, d, 0) for p, d in enumerate(order))
    blocks = cb_dev * count
    cap = 2 * 128 // count
    side_shape = (micros, count, 2 * ROWS // (2 * BLOCK), 2, SIDE, TOPK)
    index = indices.reshape(side_shape).transpose(1, 0, 3, 2, 4, 5)
    index = index.reshape(count, micros, 2, -1)
    number = index % blocks
    mine = (number // cb_dev) == here
    own = jnp.arange(micros, dtype=jnp.int32)[None, :, None, None]
    document = jnp.where(index < blocks, own, partner[None, :, None, None])
    entries = index.shape[-1]
    entry = jnp.arange(entries, dtype=jnp.int32)
    query_block = entry // (SIDE * TOPK)
    head = entry // TOPK % SIDE
    code = ((document * cb_dev + number % cb_dev) * 4 + query_block) * SIDE + head
    before = (entry[:, None] < entry[None, :]).astype(F32)
    flags = mine.astype(F32)
    rank = jnp.dot(flags.reshape(-1, entries), before, preferred_element_type=F32).reshape(flags.shape)
    rank = rank.astype(jnp.int32)
    slot = jnp.arange(cap, dtype=jnp.int32)
    hit = mine[..., None, :] & (rank[..., None, :] == slot[:, None])
    codes = jnp.sum(jnp.where(hit, code[..., None, :], 0), axis=-1)
    length = jnp.sum(mine.astype(jnp.int32), axis=-1, keepdims=True)
    lists = jnp.concatenate([length, codes], axis=-1).reshape(-1)
    return jnp.concatenate([here.reshape(1), owners.reshape(-1), lists]).astype(jnp.int32), cap


def collect_kernel(meta, ck, cv, mk, mv, sem_k, sem_v, *, micros, count, cap):
    owner = pl.program_id(0)

    def groups(i):
        base = list_base(count) + (owner * 2 * micros + i) * (cap + 1)
        return base, (meta[base] + GROUP - 1) // GROUP

    def start(i, carry):
        base, rounds = groups(i)

        def one(g, c):
            for u in range(GROUP):
                j = g * GROUP + u
                code = meta[base + 1 + j]
                head = (i & 1) * SIDE + (code & (SIDE - 1))
                rows = pl.ds(pl.multiple_of((code >> 4) << 6, BLOCK), BLOCK)
                cols = pl.ds(pl.multiple_of(head << 7, HEAD_DIM), HEAD_DIM)
                pltpu.make_async_copy(ck.at[rows, cols], mk.at[i >> 1, 0, i & 1, j], sem_k).start()
                pltpu.make_async_copy(cv.at[rows, cols], mv.at[i >> 1, 0, i & 1, j], sem_v).start()
            return c

        return lax.fori_loop(0, rounds, one, carry)

    def finish(i, carry):
        _, rounds = groups(i)

        def one(g, c):
            some = pl.ds(g * GROUP, GROUP)
            for place, sem in ((mk, sem_k), (mv, sem_v)):
                whole = place.at[i >> 1, 0, i & 1, some]
                pltpu.make_async_copy(whole, whole, sem).wait()
            return c

        return lax.fori_loop(0, rounds, one, carry)

    lax.fori_loop(0, 2 * micros, start, 0)
    lax.fori_loop(0, 2 * micros, finish, 0)


def collect(meta, cache_keys, cache_values, count, cap):
    micros = cache_keys.shape[0]
    shape = jax.ShapeDtypeStruct((micros, count, 2, cap, BLOCK, HEAD_DIM), BF16)
    anywhere = pl.BlockSpec(memory_space=pl.ANY)
    block = pl.BlockSpec((micros, 1, 2, cap, BLOCK, HEAD_DIM), lambda o, meta: (0, o, 0, 0, 0, 0))
    return pl.pallas_call(
        functools.partial(collect_kernel, micros=micros, count=count, cap=cap),
        grid_spec=pltpu.PrefetchScalarGridSpec(
            num_scalar_prefetch=1,
            grid=(count,),
            in_specs=[anywhere, anywhere],
            out_specs=[block, block],
            scratch_shapes=[pltpu.SemaphoreType.DMA, pltpu.SemaphoreType.DMA],
        ),
        out_shape=[shape, shape],
        compiler_params=params(),
        name="collect",
        cost_estimate=pl.CostEstimate(flops=0, bytes_accessed=90_000_000, transcendentals=0),
    )(meta, cache_keys.reshape(-1, D), cache_values.reshape(-1, D))


def turn(value, cosine, sine):
    return value * cosine + pltpu.roll(value, HEAD_DIM // 2, 1) * sine


def first_kernel(x, gain, weight, cosine, sine, normed, qa, qb):
    value = x[0].astype(F32)
    scale = lax.rsqrt(jnp.mean(value * value, axis=-1, keepdims=True) + EPS)
    low = (value * scale * gain[...]).astype(BF16)
    normed[0] = low
    product = nn(low, weight[...])
    for h in range(HEADS):
        cols = slice(h * HEAD_DIM, (h + 1) * HEAD_DIM)
        out = qa if h < SIDE else qb
        place = slice((h % SIDE) * HEAD_DIM, (h % SIDE + 1) * HEAD_DIM)
        out[0, :, place] = turn(product[:, cols], cosine[...], sine[...]).astype(BF16)


def second_kernel(normed, key_weight, value_weight, cosine, sine, keys, values):
    low = normed[0]
    product = nn(low, key_weight[...])
    for h in range(HEADS):
        cols = slice(h * HEAD_DIM, (h + 1) * HEAD_DIM)
        keys[0, :, cols] = turn(product[:, cols], cosine[...], sine[...]).astype(BF16)
    values[0] = nn(low, value_weight[...]).astype(BF16)


def seq_spec(*shape):
    return pl.BlockSpec((1,) + shape, lambda m, *_: (m,) + (0,) * len(shape))


def full_spec(*shape):
    return pl.BlockSpec(shape, lambda m, *_: (0,) * len(shape))


def seq_shape(micros, *shape, dtype=BF16):
    return jax.ShapeDtypeStruct((micros,) + shape, dtype)


def project_query(x, gain, weight, cosine, sine):
    micros = x.shape[0]
    return pl.pallas_call(
        first_kernel,
        grid=(micros,),
        in_specs=[
            seq_spec(ROWS, D),
            full_spec(1, D),
            full_spec(D, D),
            full_spec(ROWS, HEAD_DIM),
            full_spec(ROWS, HEAD_DIM),
        ],
        out_specs=[seq_spec(ROWS, D), seq_spec(ROWS, SW), seq_spec(ROWS, SW)],
        out_shape=[seq_shape(micros, ROWS, D), seq_shape(micros, ROWS, SW), seq_shape(micros, ROWS, SW)],
        compiler_params=params(),
        name="project_query",
        cost_estimate=pl.CostEstimate(flops=2 * micros * ROWS * D * D, bytes_accessed=8_000_000, transcendentals=0),
    )(x, gain, weight, cosine, sine)


def project_pairs(normed, key_weight, value_weight, cosine, sine):
    micros = normed.shape[0]
    return pl.pallas_call(
        second_kernel,
        grid=(micros,),
        in_specs=[
            seq_spec(ROWS, D),
            full_spec(D, D),
            full_spec(D, D),
            full_spec(ROWS, HEAD_DIM),
            full_spec(ROWS, HEAD_DIM),
        ],
        out_specs=[seq_spec(ROWS, D), seq_spec(ROWS, D)],
        out_shape=[seq_shape(micros, ROWS, D), seq_shape(micros, ROWS, D)],
        compiler_params=params(),
        name="project_pairs",
        cost_estimate=pl.CostEstimate(flops=4 * micros * ROWS * D * D, bytes_accessed=10_000_000, transcendentals=0),
    )(normed, key_weight, value_weight, cosine, sine)


def causal_mask():
    row = lax.broadcasted_iota(jnp.int32, (ROWS, ROWS), 0)
    col = lax.broadcasted_iota(jnp.int32, (ROWS, ROWS), 1)
    return row >= col


def to_lanes(wide):
    lane = lax.broadcasted_iota(jnp.int32, (ROWS, HEAD_DIM), 1)
    packed = jnp.zeros((ROWS, HEAD_DIM), F32)
    for h in range(SIDE):
        packed = jnp.where(lane == h, wide[:, h * HEAD_DIM : (h + 1) * HEAD_DIM], packed)
    return packed.T[:8]


def to_columns(lanes):
    return jnp.concatenate([lanes, jnp.zeros((HEAD_DIM - 8, ROWS), F32)], axis=0).T


def split3(value):
    high = value.astype(BF16).astype(F32)
    middle = (value - high).astype(BF16).astype(F32)
    return high, middle, value - high - middle


def pack_lanes(lanes):
    high, middle, low = split3(lanes)
    rows = jnp.concatenate(
        [jnp.concatenate([high, middle], axis=1), jnp.concatenate([low, jnp.zeros_like(low)], axis=1)],
        axis=0,
    )
    return rows.astype(BF16)


def unpack_lanes(rows):
    value = rows.astype(F32)
    return value[:8, :ROWS] + value[:8, ROWS:] + value[8:, :ROWS]


def forward_kernel(meta, qa, qb, k, v, mka, mkb, mva, mvb, pa, pb, ta, tb, wide, *, step, count, cap, micros):
    micro = pl.program_id(0)
    here = meta[0]
    for side, (q, mk, mv, part, total) in enumerate(
        ((qa, mka, mva, pa, ta), (qb, mkb, mvb, pb, tb))
    ):
        owner = meta[1 + 2 * step + side]

        def local(qrows, krows, masked):
            for h in range(SIDE):
                cols = slice(h * HEAD_DIM, (h + 1) * HEAD_DIM)
                kcols = slice((side * SIDE + h) * HEAD_DIM, (side * SIDE + h + 1) * HEAD_DIM)
                keys = k[0, krows, kcols]
                values = v[0, krows, kcols]
                score = nt(q[0, qrows, cols], keys)
                weight = jnp.exp2(score * (SCALE * LOG2E))
                if masked:
                    weight = jnp.where(causal_mask(), weight, 0.0)
                more = jnp.concatenate([values, jnp.ones_like(values)], axis=1)
                out = nn(weight.astype(BF16), more)
                part[0, qrows, cols] = out[:, :HEAD_DIM]
                wide[qrows, cols] = out[:, HEAD_DIM:]

        everything = slice(0, ROWS)
        low = slice(0, HALF)
        high = slice(HALF, ROWS)
        if step == 0:
            local(everything, everything, True)
        else:

            @pl.when(owner < here)
            def _():
                part[0, low, :] = jnp.zeros((HALF, SW), F32)
                wide[low, :] = jnp.zeros((HALF, SW), F32)
                local(high, everything, False)

            @pl.when(owner > here)
            def _():
                local(everything, low, False)

        base = list_base(count) + list_at(owner, micro, side, micros, cap)
        length = meta[base]

        def group(i, carry):
            for j in range(GROUP):
                slot = i * GROUP + j
                code = meta[base + 1 + slot]
                rows = pl.ds(pl.multiple_of(code // SIDE % 4 * BLOCK, BLOCK), BLOCK)
                cols = pl.ds(pl.multiple_of(code % SIDE * HEAD_DIM, HEAD_DIM), HEAD_DIM)
                keys = mk[0, 0, 0, slot]
                values = mv[0, 0, 0, slot]
                score = nt(q[0, rows, cols], keys)
                weight = jnp.exp2(score * (SCALE * LOG2E))
                weight = jnp.where(slot < length, weight, 0.0).astype(BF16)
                more = jnp.concatenate([values, jnp.ones_like(values)], axis=1)
                out = nn(weight, more)
                part[0, rows, cols] += out[:, :HEAD_DIM]
                wide[rows, cols] += out[:, HEAD_DIM:]
            return carry

        lax.fori_loop(0, (length + GROUP - 1) // GROUP, group, 0)
        total[0] = to_lanes(wide[...])


def memory_specs(step, cap):
    def spec(side):
        return pl.BlockSpec(
            (1, 1, 1, cap, BLOCK, HEAD_DIM),
            lambda m, meta: (m, meta[1 + 2 * step + side], side, 0, 0, 0),
        )

    return [spec(0), spec(1), spec(0), spec(1)]


def attend(meta, qa, qb, keys, values, memory_keys, memory_values, step, count, cap):
    micros = qa.shape[0]
    return pl.pallas_call(
        functools.partial(forward_kernel, step=step, count=count, cap=cap, micros=micros),
        grid_spec=pltpu.PrefetchScalarGridSpec(
            num_scalar_prefetch=1,
            grid=(micros,),
            in_specs=[seq_spec(ROWS, SW), seq_spec(ROWS, SW), seq_spec(ROWS, D), seq_spec(ROWS, D)]
            + memory_specs(step, cap),
            out_specs=[seq_spec(ROWS, SW), seq_spec(ROWS, SW), seq_spec(8, ROWS), seq_spec(8, ROWS)],
            scratch_shapes=[pltpu.VMEM((ROWS, SW), F32)],
        ),
        out_shape=[
            seq_shape(micros, ROWS, SW, dtype=F32),
            seq_shape(micros, ROWS, SW, dtype=F32),
            seq_shape(micros, 8, ROWS, dtype=F32),
            seq_shape(micros, 8, ROWS, dtype=F32),
        ],
        compiler_params=params(),
        name="attend",
        cost_estimate=pl.CostEstimate(flops=8_000_000_000, bytes_accessed=14_000_000, transcendentals=0),
    )(meta, qa, qb, keys, values, memory_keys, memory_keys, memory_values, memory_values)


def combine_kernel(*refs, carried, sums):
    refs = list(refs)
    received = [refs.pop(0), refs.pop(0)] if carried else [None, None]
    parts = [refs.pop(0), refs.pop(0)]
    totals = [refs.pop(0), refs.pop(0)] if sums else [None, None]
    for got, part, total, out in zip(received, parts, totals, refs):
        value = part[0]
        if carried:
            value = value + got[0, :ROWS].astype(F32)
        out[0, :ROWS] = value.astype(BF16)
        if sums:
            lanes = total[0]
            if carried:
                lanes = lanes + unpack_lanes(got[0, ROWS:])
            out[0, ROWS:] = pack_lanes(lanes)


def combine(received, parts, totals=()):
    micros = parts[0].shape[0]
    sent = SENT if totals else ROWS
    half, lanes, packed = seq_spec(ROWS, SW), seq_spec(8, ROWS), seq_spec(sent, SW)
    return pl.pallas_call(
        functools.partial(combine_kernel, carried=bool(received), sums=bool(totals)),
        grid=(micros,),
        in_specs=[packed] * len(received) + [half] * 2 + [lanes] * len(totals),
        out_specs=[packed, packed],
        out_shape=[seq_shape(micros, sent, SW)] * 2,
        compiler_params=params(),
        name="combine",
        cost_estimate=pl.CostEstimate(flops=2_000_000, bytes_accessed=7_000_000, transcendentals=0),
    )(*received, *parts, *totals)


def finish_kernel(acc_a, acc_b, pa, pb, ta, tb, mixed, low, total):
    for side, (acc, part, own) in enumerate(((acc_a, pa, ta), (acc_b, pb, tb))):
        lanes = unpack_lanes(acc[0, ROWS:]) + own[0]
        total[0, side] = lanes
        columns = to_columns(lanes)
        for h in range(SIDE):
            cols = slice(h * HEAD_DIM, (h + 1) * HEAD_DIM)
            place = slice((side * SIDE + h) * HEAD_DIM, (side * SIDE + h + 1) * HEAD_DIM)
            weighted = acc[0, :ROWS, cols].astype(F32) + part[0, :, cols]
            value = weighted / columns[:, h : h + 1]
            mixed[0, :, place] = value
            low[0, :, place] = value.astype(BF16)


def finish(acc_a, acc_b, pa, pb, ta, tb):
    micros = acc_a.shape[0]
    packed, half, lanes = seq_spec(SENT, SW), seq_spec(ROWS, SW), seq_spec(8, ROWS)
    return pl.pallas_call(
        finish_kernel,
        grid=(micros,),
        in_specs=[packed, packed, half, half, lanes, lanes],
        out_specs=[seq_spec(ROWS, D), seq_spec(ROWS, D), seq_spec(2, 8, ROWS)],
        out_shape=[
            seq_shape(micros, ROWS, D, dtype=F32),
            seq_shape(micros, ROWS, D),
            seq_shape(micros, 2, 8, ROWS, dtype=F32),
        ],
        compiler_params=params(),
        name="finish",
        cost_estimate=pl.CostEstimate(flops=3_000_000, bytes_accessed=10_000_000, transcendentals=0),
    )(acc_a, acc_b, pa, pb, ta, tb)


def prepare_kernel(back_attn, weight, mixed, total, da, db):
    lane = lax.broadcasted_iota(jnp.int32, (ROWS, HEAD_DIM), 1)
    for side, out in enumerate((da, db)):
        columns = to_columns(total[0, side])
        packed = jnp.zeros((ROWS, HEAD_DIM), F32)
        back = nt(back_attn[0], weight[side * SW : (side + 1) * SW, :])
        for h in range(SIDE):
            cols = slice(h * HEAD_DIM, (h + 1) * HEAD_DIM)
            place = slice((side * SIDE + h) * HEAD_DIM, (side * SIDE + h + 1) * HEAD_DIM)
            part = back[:, cols]
            divisor = columns[:, h : h + 1]
            out[0, :ROWS, cols] = (part / divisor).astype(BF16)
            product = jnp.sum(part * mixed[0, :, place], axis=1, keepdims=True)
            packed = jnp.where(lane == h, -product / divisor, packed)
        out[0, ROWS:] = pack_lanes(packed.T[:8])


def prepare(back_attn, weight, mixed, total):
    micros = back_attn.shape[0]
    return pl.pallas_call(
        prepare_kernel,
        grid=(micros,),
        in_specs=[seq_spec(ROWS, D), full_spec(D, D), seq_spec(ROWS, D), seq_spec(2, 8, ROWS)],
        out_specs=[seq_spec(SENT, SW), seq_spec(SENT, SW)],
        out_shape=[seq_shape(micros, SENT, SW)] * 2,
        compiler_params=params(),
        name="prepare",
        cost_estimate=pl.CostEstimate(flops=2 * micros * ROWS * D * D, bytes_accessed=10_000_000, transcendentals=0),
    )(back_attn, weight, mixed, total)


def backward_kernel(
    meta, qa, qb, da, db, k, v, mka, mkb, mva, mvb, *rest, step, count, cap, micros
):
    if step == 0:
        dqa, dqb, dk, dv, wide = rest
    else:
        dk_in, dv_in, dqa, dqb, dk, dv, wide = rest
    micro = pl.program_id(0)
    here = meta[0]
    if step == 0:
        dk[...] = jnp.zeros_like(dk)
        dv[...] = jnp.zeros_like(dv)
    else:
        dk[...] = dk_in[...]
        dv[...] = dv_in[...]
    for side, (q, d, mk, mv, dq) in enumerate(
        ((qa, da, mka, mva, dqa), (qb, db, mkb, mvb, dqb))
    ):
        owner = meta[1 + 2 * step + side]
        columns = to_columns(unpack_lanes(d[0, ROWS:]))
        for h in range(SIDE):
            cols = slice(h * HEAD_DIM, (h + 1) * HEAD_DIM)
            wide[:, cols] = jnp.broadcast_to(columns[:, h : h + 1], (ROWS, HEAD_DIM))

        def local(qrows, krows, masked):
            for h in range(SIDE):
                cols = slice(h * HEAD_DIM, (h + 1) * HEAD_DIM)
                kcols = slice((side * SIDE + h) * HEAD_DIM, (side * SIDE + h + 1) * HEAD_DIM)
                keys = k[0, krows, kcols]
                values = v[0, krows, kcols]
                query = q[0, qrows, cols]
                back = d[0, qrows, cols]
                score = nt(query, keys)
                weight = jnp.exp2(score * (SCALE * LOG2E))
                if masked:
                    weight = jnp.where(causal_mask(), weight, 0.0)
                slope = nt(back, values) + wide[qrows, cols][:, :1]
                slope = (weight * slope).astype(BF16)
                dq[0, qrows, cols] = nn(slope, keys)
                dk[0, krows, kcols] += tn(slope, query)
                dv[0, krows, kcols] += tn(weight.astype(BF16), back)

        everything = slice(0, ROWS)
        low = slice(0, HALF)
        high = slice(HALF, ROWS)
        if step == 0:
            local(everything, everything, True)
        else:

            @pl.when(owner < here)
            def _():
                dq[0, low, :] = jnp.zeros((HALF, SW), F32)
                local(high, everything, False)

            @pl.when(owner > here)
            def _():
                local(everything, low, False)

        base = list_base(count) + list_at(owner, micro, side, micros, cap)
        length = meta[base]

        def group(i, carry):
            for j in range(GROUP):
                slot = i * GROUP + j
                code = meta[base + 1 + slot]
                rows = pl.ds(pl.multiple_of(code // SIDE % 4 * BLOCK, BLOCK), BLOCK)
                cols = pl.ds(pl.multiple_of(code % SIDE * HEAD_DIM, HEAD_DIM), HEAD_DIM)
                keys = mk[0, 0, 0, slot]
                values = mv[0, 0, 0, slot]
                score = nt(q[0, rows, cols], keys)
                weight = jnp.exp2(score * (SCALE * LOG2E))
                slope = nt(d[0, rows, cols], values) + wide[rows, cols][:, :BLOCK]
                slope = jnp.where(slot < length, weight * slope, 0.0).astype(BF16)
                dq[0, rows, cols] += nn(slope, keys)
            return carry

        lax.fori_loop(0, (length + GROUP - 1) // GROUP, group, 0)


def unattend(meta, qa, qb, da, db, keys, values, memory_keys, memory_values, sums, step, count, cap):
    micros = qa.shape[0]
    half, packed, whole = seq_spec(ROWS, SW), seq_spec(SENT, SW), seq_spec(ROWS, D)
    carried = [] if sums is None else list(sums)
    first = 11
    return pl.pallas_call(
        functools.partial(backward_kernel, step=step, count=count, cap=cap, micros=micros),
        grid_spec=pltpu.PrefetchScalarGridSpec(
            num_scalar_prefetch=1,
            grid=(micros,),
            in_specs=[half, half, packed, packed, whole, whole]
            + memory_specs(step, cap)
            + [whole] * len(carried),
            out_specs=[half, half, whole, whole],
            scratch_shapes=[pltpu.VMEM((ROWS, SW), F32)],
        ),
        out_shape=[
            seq_shape(micros, ROWS, SW, dtype=F32),
            seq_shape(micros, ROWS, SW, dtype=F32),
            seq_shape(micros, ROWS, D, dtype=F32),
            seq_shape(micros, ROWS, D, dtype=F32),
        ],
        input_output_aliases={first: 2, first + 1: 3} if carried else {},
        compiler_params=params(),
        name="unattend",
        cost_estimate=pl.CostEstimate(flops=16_000_000_000, bytes_accessed=30_000_000, transcendentals=0),
    )(
        meta,
        qa,
        qb,
        da,
        db,
        keys,
        values,
        memory_keys,
        memory_keys,
        memory_values,
        memory_values,
        *carried,
    )


def unturn_kernel(acc_a, acc_b, pa, pb, dk, dv, cosine, sine, back):
    for h in range(HEADS):
        acc, part = (acc_a, pa) if h < SIDE else (acc_b, pb)
        cols = slice(h % SIDE * HEAD_DIM, (h % SIDE + 1) * HEAD_DIM)
        place = slice(h * HEAD_DIM, (h + 1) * HEAD_DIM)
        value = (acc[0, :, cols].astype(F32) + part[0, :, cols]) * SCALE
        key_place = slice(D + h * HEAD_DIM, D + (h + 1) * HEAD_DIM)
        back[0, :, place] = turn(value, cosine[...], -sine[...]).astype(BF16)
        back[0, :, key_place] = turn(dk[0, :, place] * SCALE, cosine[...], -sine[...]).astype(BF16)
    back[0, :, 2 * D :] = dv[0].astype(BF16)


def unturn(acc_a, acc_b, pa, pb, dk, dv, cosine, sine):
    micros = acc_a.shape[0]
    half, whole, angle = seq_spec(ROWS, SW), seq_spec(ROWS, D), full_spec(ROWS, HEAD_DIM)
    return pl.pallas_call(
        unturn_kernel,
        grid=(micros,),
        in_specs=[half, half, half, half, whole, whole, angle, angle],
        out_specs=seq_spec(ROWS, 3 * D),
        out_shape=seq_shape(micros, ROWS, 3 * D),
        compiler_params=params(),
        name="unturn",
        cost_estimate=pl.CostEstimate(flops=10_000_000, bytes_accessed=16_000_000, transcendentals=0),
    )(acc_a, acc_b, pa, pb, dk, dv, cosine, sine)


def norm_parts(value):
    scale = lax.rsqrt(jnp.mean(value * value, axis=-1, keepdims=True) + EPS)
    return value * scale, scale


def norm_back(hat, scale, back, gain):
    slope = back * gain
    return scale * (slope - hat * jnp.mean(slope * hat, axis=-1, keepdims=True))


def body(
    tokens,
    cotangent,
    query_weight,
    key_weight,
    value_weight,
    output_weight,
    gate_weight,
    up_weight,
    down_weight,
    first_gain,
    second_gain,
    cache_keys,
    cache_values,
    block_indices,
    partner,
):
    count = lax.axis_size("ctx")
    here = lax.axis_index("ctx")
    micros = tokens.shape[0]
    rows = micros * ROWS
    order = ring_order(count)
    onward = [(order[i], order[(i + 1) % count]) for i in range(count)]
    backward = [(b, a) for a, b in onward]

    def gather(value):
        return lax.all_gather(value, "fsdp", axis=0, tiled=True)

    indices = lax.all_gather(block_indices, "ctx", axis=1, tiled=True)
    gains = lax.all_gather(jnp.stack([first_gain, second_gain]), "fsdp", axis=1, tiled=True)
    full_query = gather(query_weight)
    full_key = gather(key_weight)
    full_value = gather(value_weight)
    full_output = gather(output_weight)
    full_gate = gather(gate_weight)
    full_up = gather(up_weight)
    full_down = gather(down_weight)
    gain_one = gains[0:1].astype(F32)
    gain_two = gains[1:2].astype(F32)

    pieces_at = jnp.stack([here, 2 * count - 1 - here])
    positions = (pieces_at[:, None] * HALF + jnp.arange(HALF, dtype=jnp.int32)[None, :]).reshape(ROWS)
    inverse = 10000.0 ** (-jnp.arange(HEAD_DIM // 2, dtype=F32) * 2.0 / HEAD_DIM)
    phase = positions.astype(F32)[:, None] * inverse[None, :]
    cosine = jnp.tile(jnp.cos(phase), (1, 2))
    sine = jnp.sin(phase)
    sine = jnp.concatenate([-sine, sine], axis=1)

    meta, cap = make_meta(indices, partner, cache_keys.shape[1] // BLOCK, count)
    memory_keys, memory_values = collect(meta, cache_keys, cache_values, count, cap)

    x = tokens.reshape(micros, ROWS, D)
    normed_low, qa, qb = project_query(x, gain_one, full_query, cosine, sine)
    keys, values = project_pairs(normed_low, full_key, full_value, cosine, sine)

    queries = [(qa, qb)]
    for _ in range(count - 1):
        qa, qb = lax.ppermute(qa, "ctx", onward), lax.ppermute(qb, "ctx", backward)
        queries.append((qa, qb))

    acc = ()
    for step in list(range(1, count)) + [0]:
        pa, pb, ta, tb = attend(
            meta, *queries[step], keys, values, memory_keys, memory_values, step, count, cap
        )
        if acc:
            acc = (lax.ppermute(acc[0], "ctx", onward), lax.ppermute(acc[1], "ctx", backward))
        if step == 0:
            mixed, mixed_low, total = finish(*acc, pa, pb, ta, tb)
        else:
            acc = combine(acc, (pa, pb), (ta, tb))

    inputs = tokens.reshape(rows, D).astype(F32)
    mixed_low = mixed_low.reshape(rows, D)
    middle = inputs + jnp.dot(mixed_low, full_output, preferred_element_type=F32)
    mid_hat, mid_scale = norm_parts(middle)
    middle_low = (mid_hat * gain_two).astype(BF16)
    gate = jnp.dot(middle_low, full_gate, preferred_element_type=F32)
    upper = jnp.dot(middle_low, full_up, preferred_element_type=F32)
    sigma = jax.nn.sigmoid(gate)
    silu = gate * sigma
    hidden = (silu * upper).astype(BF16)
    layer_output = (middle + jnp.dot(hidden, full_down, preferred_element_type=F32)).astype(BF16)
    incoming = cotangent.reshape(rows, D)
    gradient_down = jnp.einsum("tf,td->fd", hidden, incoming, preferred_element_type=F32).astype(BF16)
    back_hidden = jnp.einsum("td,fd->tf", incoming, full_down, preferred_element_type=F32)
    back_gate = (back_hidden * upper * (sigma * (1.0 + gate * (1.0 - sigma)))).astype(BF16)
    back_upper = (back_hidden * silu).astype(BF16)
    gradient_gate = jnp.einsum("td,tf->df", middle_low, back_gate, preferred_element_type=F32).astype(BF16)
    gradient_up = jnp.einsum("td,tf->df", middle_low, back_upper, preferred_element_type=F32).astype(BF16)
    back_mid_normed = jnp.einsum(
        "tf,df->td", back_gate, full_gate, preferred_element_type=F32
    ) + jnp.einsum("tf,df->td", back_upper, full_up, preferred_element_type=F32)
    gradient_second = jnp.sum(back_mid_normed * mid_hat, axis=0)
    back_middle = incoming.astype(F32) + norm_back(mid_hat, mid_scale, back_mid_normed, gain_two)
    back_attn = back_middle.astype(BF16)
    gradient_output = jnp.einsum("tc,td->cd", mixed_low, back_attn, preferred_element_type=F32).astype(BF16)

    slopes = [prepare(back_attn.reshape(micros, ROWS, D), full_output, mixed, total)]
    for _ in range(count - 1):
        da, db = slopes[-1]
        slopes.append((lax.ppermute(da, "ctx", onward), lax.ppermute(db, "ctx", backward)))
    slopes[1], (gradient_down, gradient_gate, gradient_up, gradient_output) = lax.optimization_barrier(
        (slopes[1], (gradient_down, gradient_gate, gradient_up, gradient_output))
    )

    sums = None
    acc = ()
    for step in range(count):
        dqa, dqb, dk, dv = unattend(
            meta,
            *queries[step],
            *slopes[step],
            keys,
            values,
            memory_keys,
            memory_values,
            sums,
            step,
            count,
            cap,
        )
        sums = (dk, dv)
        if step == 0:
            own = (dqa, dqb)
            continue
        if acc:
            acc = (lax.ppermute(acc[0], "ctx", onward), lax.ppermute(acc[1], "ctx", backward))
        acc = combine(acc, (dqa, dqb))
    ra, rb = lax.ppermute(acc[0], "ctx", onward), lax.ppermute(acc[1], "ctx", backward)
    back = unturn(ra, rb, *own, *sums, cosine, sine).reshape(rows, 3 * D)
    normed_low = normed_low.reshape(rows, D)
    gradient_three = jnp.einsum("tc,td->cd", normed_low, back, preferred_element_type=F32).astype(BF16)
    back_in_normed = (
        jnp.einsum("td,cd->tc", back[:, :D], full_query, preferred_element_type=F32)
        + jnp.einsum("td,cd->tc", back[:, D : 2 * D], full_key, preferred_element_type=F32)
        + jnp.einsum("td,cd->tc", back[:, 2 * D :], full_value, preferred_element_type=F32)
    )
    in_hat, in_scale = norm_parts(inputs)
    gradient_first = jnp.sum(back_in_normed * in_hat, axis=0)
    input_gradient = back_middle + norm_back(in_hat, in_scale, back_in_normed, gain_one)

    def scatter(part):
        return lax.psum_scatter(part, "fsdp", scatter_dimension=0, tiled=True)

    early = [
        scatter(part) for part in (gradient_down, gradient_gate, gradient_up, gradient_output)
    ]
    early, three = lax.optimization_barrier((lax.psum(early, "ctx"), scatter(gradient_three)))
    early = [part.astype(F32) for part in early]
    three = lax.psum(three, "ctx").astype(F32)
    gain_changes = lax.psum(jnp.stack([gradient_first, gradient_second]), ("ctx", "fsdp"))
    own_rows = D // lax.axis_size("fsdp")
    gain_changes = lax.dynamic_slice_in_dim(
        gain_changes, lax.axis_index("fsdp") * own_rows, own_rows, axis=1
    )
    return (
        layer_output.reshape(tokens.shape),
        input_gradient.reshape(tokens.shape),
        three[:, :D],
        three[:, D : 2 * D],
        three[:, 2 * D :],
        early[3],
        early[1],
        early[2],
        early[0],
        gain_changes[0],
        gain_changes[1],
    )


def solution(mesh):
    split = P("fsdp", "ctx", None, None, None)
    shard = P("fsdp", None)
    return jax.shard_map(
        body,
        mesh=mesh,
        in_specs=(
            split,
            split,
            *([shard] * 7),
            P("fsdp"),
            P("fsdp"),
            P("fsdp", "ctx", None),
            P("fsdp", "ctx", None),
            P("fsdp", "ctx", None, None, None, None),
            P("fsdp"),
        ),
        out_specs=(split, split, *([shard] * 7), P("fsdp"), P("fsdp")),
        check_vma=False,
    )
```

```python
import functools

import jax
import jax.numpy as jnp
from jax import lax
from jax.experimental import pallas as pl
from jax.experimental.pallas import tpu as pltpu
from jax.sharding import PartitionSpec as P

D = 1024
HEADS = 8
HEAD_DIM = 128
HALF = 128
ROWS = 2 * HALF
BLOCK = 64
TOPK = 4
SIDE = HEADS // 2
SW = SIDE * HEAD_DIM
GROUP = 8
EPS = 1e-05
SCALE = HEAD_DIM**-0.5
LOG2E = 1.4426950408889634
F32 = jnp.float32
BF16 = jnp.bfloat16
EXTRA = 16
SENT = ROWS + EXTRA


def nn(a, b):
    return lax.dot_general(a, b, (((1,), (0,)), ((), ())), preferred_element_type=F32)


def nt(a, b):
    return lax.dot_general(a, b, (((1,), (1,)), ((), ())), preferred_element_type=F32)


def tn(a, b):
    return lax.dot_general(a, b, (((0,), (0,)), ((), ())), preferred_element_type=F32)


def params(mib=56):
    return pltpu.CompilerParams(vmem_limit_bytes=mib * 2**20)


def ring_order(count):
    if count == 8:
        return [0, 2, 4, 6, 7, 5, 3, 1]
    half = count // 2
    return list(range(half)) + [count - 1 - i for i in range(count - half)]


def ring_place(count):
    here = lax.axis_index("ctx")
    half = count // 2
    if count == 8:
        turned = here % 2
        return (1 - turned) * (here // 2) + turned * (count - 1 - here // 2)
    turned = here // half
    return (1 - turned) * here + turned * (count - 1 + half - here)


def ring_index(place, count):
    half = count // 2
    place = place % count
    turned = place // half
    if count == 8:
        return (1 - turned) * 2 * place + turned * (2 * count - 1 - 2 * place)
    return (1 - turned) * place + turned * (count - 1 + half - place)


def ring_pairs(count):
    order = ring_order(count)
    onward = [(order[i], order[(i + 1) % count]) for i in range(count)]
    return onward, [(b, a) for a, b in onward]


def list_base(count):
    return 1 + 2 * count


def list_at(owner, micro, side, micros, cap):
    return ((owner * micros + micro) * 2 + side) * (cap + 1)


def make_meta(indices, partner, cb_dev, count):
    micros = indices.shape[0]
    here = lax.axis_index("ctx")
    order = ring_order(count)
    place = ring_place(count)
    steps = jnp.arange(count, dtype=jnp.int32)
    at = jnp.stack([(place - steps) % count, (place + steps) % count], axis=1)
    owners = sum(jnp.where(at == p, d, 0) for p, d in enumerate(order))
    blocks = cb_dev * count
    cap = 2 * 128 // count
    side_shape = (micros, count, 2 * ROWS // (2 * BLOCK), 2, SIDE, TOPK)
    index = indices.reshape(side_shape).transpose(1, 0, 3, 2, 4, 5)
    index = index.reshape(count, micros, 2, -1)
    number = index % blocks
    mine = (number // cb_dev) == here
    own = jnp.arange(micros, dtype=jnp.int32)[None, :, None, None]
    document = jnp.where(index < blocks, own, partner[None, :, None, None])
    entries = index.shape[-1]
    entry = jnp.arange(entries, dtype=jnp.int32)
    query_block = entry // (SIDE * TOPK)
    head = entry // TOPK % SIDE
    code = ((document * cb_dev + number % cb_dev) * 4 + query_block) * SIDE + head
    before = (entry[:, None] < entry[None, :]).astype(F32)
    flags = mine.astype(F32)
    rank = jnp.dot(flags.reshape(-1, entries), before, preferred_element_type=F32).reshape(flags.shape)
    rank = rank.astype(jnp.int32)
    slot = jnp.arange(cap, dtype=jnp.int32)
    hit = mine[..., None, :] & (rank[..., None, :] == slot[:, None])
    codes = jnp.sum(jnp.where(hit, code[..., None, :], 0), axis=-1)
    length = jnp.sum(mine.astype(jnp.int32), axis=-1, keepdims=True)
    lists = jnp.concatenate([length, codes], axis=-1).reshape(-1)
    return jnp.concatenate([here.reshape(1), owners.reshape(-1), lists]).astype(jnp.int32), cap


def collect_kernel(meta, ck, cv, mk, mv, sem_k, sem_v, *, micros, count, cap):
    owner = pl.program_id(0)

    def list_of(i):
        base = list_base(count) + (owner * 2 * micros + i) * (cap + 1)
        return base, meta[base]

    def start(i, carry):
        base, length = list_of(i)

        def one(j, c):
            code = meta[base + 1 + j]
            head = (i & 1) * SIDE + (code & (SIDE - 1))
            rows = pl.ds(pl.multiple_of((code >> 4) << 6, BLOCK), BLOCK)
            cols = pl.ds(pl.multiple_of(head << 7, HEAD_DIM), HEAD_DIM)
            pltpu.make_async_copy(ck.at[rows, cols], mk.at[i >> 1, 0, i & 1, j], sem_k).start()
            pltpu.make_async_copy(cv.at[rows, cols], mv.at[i >> 1, 0, i & 1, j], sem_v).start()
            return c

        def clear(j, c):
            mk[i >> 1, 0, i & 1, j] = jnp.zeros((BLOCK, HEAD_DIM), BF16)
            mv[i >> 1, 0, i & 1, j] = jnp.zeros((BLOCK, HEAD_DIM), BF16)
            return c

        lax.fori_loop(0, length, one, carry)
        return lax.fori_loop(length, (length + GROUP - 1) // GROUP * GROUP, clear, carry)

    def finish(i, carry):
        _, length = list_of(i)
        rounds = length // GROUP

        def many(g, c):
            some = pl.ds(g * GROUP, GROUP)
            for place, sem in ((mk, sem_k), (mv, sem_v)):
                whole = place.at[i >> 1, 0, i & 1, some]
                pltpu.make_async_copy(whole, whole, sem).wait()
            return c

        def one(j, c):
            for place, sem in ((mk, sem_k), (mv, sem_v)):
                whole = place.at[i >> 1, 0, i & 1, j]
                pltpu.make_async_copy(whole, whole, sem).wait()
            return c

        lax.fori_loop(0, rounds, many, carry)
        return lax.fori_loop(rounds * GROUP, length, one, carry)

    lax.fori_loop(0, 2 * micros, start, 0)
    lax.fori_loop(0, 2 * micros, finish, 0)


def collect(meta, cache_keys, cache_values, count, cap):
    micros = cache_keys.shape[0]
    shape = jax.ShapeDtypeStruct((micros, count, 2, cap, BLOCK, HEAD_DIM), BF16)
    anywhere = pl.BlockSpec(memory_space=pl.ANY)
    block = pl.BlockSpec((micros, 1, 2, cap, BLOCK, HEAD_DIM), lambda o, meta: (0, o, 0, 0, 0, 0))
    return pl.pallas_call(
        functools.partial(collect_kernel, micros=micros, count=count, cap=cap),
        grid_spec=pltpu.PrefetchScalarGridSpec(
            num_scalar_prefetch=1,
            grid=(count,),
            in_specs=[anywhere, anywhere],
            out_specs=[block, block],
            scratch_shapes=[pltpu.SemaphoreType.DMA, pltpu.SemaphoreType.DMA],
        ),
        out_shape=[shape, shape],
        compiler_params=params(),
        name="collect",
        cost_estimate=pl.CostEstimate(flops=0, bytes_accessed=90_000_000, transcendentals=0),
    )(meta, cache_keys.reshape(-1, D), cache_values.reshape(-1, D))


def turn(value, cosine, sine):
    return value * cosine + pltpu.roll(value, HEAD_DIM // 2, 1) * sine


def first_kernel(x, gain, weight, cosine, sine, normed, qa, qb):
    value = x[0].astype(F32)
    scale = lax.rsqrt(jnp.mean(value * value, axis=-1, keepdims=True) + EPS)
    low = (value * scale * gain[...]).astype(BF16)
    normed[0] = low
    product = nn(low, weight[...])
    for h in range(HEADS):
        cols = slice(h * HEAD_DIM, (h + 1) * HEAD_DIM)
        out = qa if h < SIDE else qb
        place = slice((h % SIDE) * HEAD_DIM, (h % SIDE + 1) * HEAD_DIM)
        out[0, :, place] = turn(product[:, cols], cosine[...], sine[...]).astype(BF16)


def second_kernel(normed, key_weight, value_weight, cosine, sine, keys, values):
    low = normed[0]
    product = nn(low, key_weight[...])
    for h in range(HEADS):
        cols = slice(h * HEAD_DIM, (h + 1) * HEAD_DIM)
        keys[0, :, cols] = turn(product[:, cols], cosine[...], sine[...]).astype(BF16)
    values[0] = nn(low, value_weight[...]).astype(BF16)


def seq_spec(*shape):
    return pl.BlockSpec((1,) + shape, lambda m, *_: (m,) + (0,) * len(shape))


def full_spec(*shape):
    return pl.BlockSpec(shape, lambda m, *_: (0,) * len(shape))


def seq_shape(micros, *shape, dtype=BF16):
    return jax.ShapeDtypeStruct((micros,) + shape, dtype)


def project_query(x, gain, weight, cosine, sine):
    micros = x.shape[0]
    return pl.pallas_call(
        first_kernel,
        grid=(micros,),
        in_specs=[
            seq_spec(ROWS, D),
            full_spec(1, D),
            full_spec(D, D),
            full_spec(ROWS, HEAD_DIM),
            full_spec(ROWS, HEAD_DIM),
        ],
        out_specs=[seq_spec(ROWS, D), seq_spec(ROWS, SW), seq_spec(ROWS, SW)],
        out_shape=[seq_shape(micros, ROWS, D), seq_shape(micros, ROWS, SW), seq_shape(micros, ROWS, SW)],
        compiler_params=params(),
        name="project_query",
        cost_estimate=pl.CostEstimate(flops=2 * micros * ROWS * D * D, bytes_accessed=8_000_000, transcendentals=0),
    )(x, gain, weight, cosine, sine)


def project_pairs(normed, key_weight, value_weight, cosine, sine):
    micros = normed.shape[0]
    return pl.pallas_call(
        second_kernel,
        grid=(micros,),
        in_specs=[
            seq_spec(ROWS, D),
            full_spec(D, D),
            full_spec(D, D),
            full_spec(ROWS, HEAD_DIM),
            full_spec(ROWS, HEAD_DIM),
        ],
        out_specs=[seq_spec(ROWS, D), seq_spec(ROWS, D)],
        out_shape=[seq_shape(micros, ROWS, D), seq_shape(micros, ROWS, D)],
        compiler_params=params(),
        name="project_pairs",
        cost_estimate=pl.CostEstimate(flops=4 * micros * ROWS * D * D, bytes_accessed=10_000_000, transcendentals=0),
    )(normed, key_weight, value_weight, cosine, sine)


def causal_mask(turned=False):
    row = lax.broadcasted_iota(jnp.int32, (ROWS, ROWS), 0)
    col = lax.broadcasted_iota(jnp.int32, (ROWS, ROWS), 1)
    return row <= col if turned else row >= col


def to_lanes(wide):
    lane = lax.broadcasted_iota(jnp.int32, (ROWS, HEAD_DIM), 1)
    packed = jnp.zeros((ROWS, HEAD_DIM), F32)
    for h in range(SIDE):
        packed = jnp.where(lane == h, wide[:, h * HEAD_DIM : (h + 1) * HEAD_DIM], packed)
    return packed.T[:8]


def to_columns(lanes):
    return jnp.concatenate([lanes, jnp.zeros((HEAD_DIM - 8, ROWS), F32)], axis=0).T


def split3(value):
    high = value.astype(BF16).astype(F32)
    middle = (value - high).astype(BF16).astype(F32)
    return high, middle, value - high - middle


def pack_lanes(lanes):
    high, middle, low = split3(lanes)
    rows = jnp.concatenate(
        [jnp.concatenate([high, middle], axis=1), jnp.concatenate([low, jnp.zeros_like(low)], axis=1)],
        axis=0,
    )
    return rows.astype(BF16)


def unpack_lanes(rows):
    value = rows.astype(F32)
    return value[:8, :ROWS] + value[:8, ROWS:] + value[8:, :ROWS]


def requests(meta, mk, mv, kbuf, vbuf, sem, micro, act, *, step, count, cap, micros):
    slot = micro % 2
    for side in range(2):
        owner = meta[1 + 2 * step + side]
        length = meta[list_base(count) + list_at(owner, micro, side, micros, cap)]

        def one(g, carry):
            some = pl.ds(g * GROUP, GROUP)
            for source, place in ((mk, kbuf), (mv, vbuf)):
                copy = pltpu.make_async_copy(
                    source.at[micro, owner, side, some], place.at[slot, side, some], sem.at[slot]
                )
                if act == "start":
                    copy.start()
                else:
                    copy.wait()
            return carry

        lax.fori_loop(0, (length + GROUP - 1) // GROUP, one, 0)


def request_ahead(fetch, micro, micros):
    @pl.when(micro == 0)
    def _():
        fetch(micro, "start")

    @pl.when(micro + 1 < micros)
    def _():
        fetch(micro + 1, "start")


def request_scratch(cap):
    return [
        pltpu.VMEM((2, 2, cap, BLOCK, HEAD_DIM), BF16),
        pltpu.VMEM((2, 2, cap, BLOCK, HEAD_DIM), BF16),
        pltpu.SemaphoreType.DMA((2,)),
    ]


EVERYTHING, LOW, HIGH = slice(0, ROWS), slice(0, HALF), slice(HALF, ROWS)


def tiles(side):
    return [
        (
            slice(h * HEAD_DIM, (h + 1) * HEAD_DIM),
            slice((side * SIDE + h) * HEAD_DIM, (side * SIDE + h + 1) * HEAD_DIM),
        )
        for h in range(SIDE)
    ]


def forward_kernel(
    meta, qa, qb, k, v, mk, mv, pa, pb, ta, tb, part, wide, kbuf, vbuf, sem, *, step, count, cap, micros
):
    micro = pl.program_id(0)
    here = meta[0]
    fetch = functools.partial(
        requests, meta, mk, mv, kbuf, vbuf, sem, step=step, count=count, cap=cap, micros=micros
    )
    request_ahead(fetch, micro, micros)
    for side, q in enumerate((qa, qb)):
        owner = meta[1 + 2 * step + side]

        def local(qrows, krows, masked):
            spots = tiles(side)
            scores = [nt(q[0, qrows, cols], k[0, krows, kcols]) for cols, kcols in spots]
            weights = [jnp.exp2(score * (SCALE * LOG2E)) for score in scores]
            if masked:
                weights = [jnp.where(causal_mask(), weight, 0.0) for weight in weights]
            for weight, (cols, kcols) in zip(weights, spots):
                values = v[0, krows, kcols]
                more = jnp.concatenate([values, jnp.ones_like(values)], axis=1)
                out = nn(weight.astype(BF16), more)
                part[qrows, kcols] = out[:, :HEAD_DIM]
                wide[qrows, kcols] = out[:, HEAD_DIM:]

        if step == 0:
            local(EVERYTHING, EVERYTHING, True)
        else:

            @pl.when(owner < here)
            def _():
                zeros = jnp.zeros((HALF, SW), F32)
                part[LOW, side * SW : (side + 1) * SW] = zeros
                wide[LOW, side * SW : (side + 1) * SW] = zeros
                local(HIGH, EVERYTHING, False)

            @pl.when(owner > here)
            def _():
                local(EVERYTHING, LOW, False)

    fetch(micro, "wait")
    slot = micro % 2
    for side, (q, out, total) in enumerate(((qa, pa, ta), (qb, pb, tb))):
        owner = meta[1 + 2 * step + side]
        base = list_base(count) + list_at(owner, micro, side, micros, cap)
        length = meta[base]

        def group(i, carry):
            numbers = [i * GROUP + j for j in range(GROUP)]
            places = [request_place(meta[base + 1 + number]) for number in numbers]
            scores = [
                nt(q[0, rows, cols], kbuf[slot, side, number])
                for number, (rows, cols) in zip(numbers, places)
            ]
            weights = [
                jnp.where(number < length, jnp.exp2(score * (SCALE * LOG2E)), 0.0).astype(BF16)
                for number, score in zip(numbers, scores)
            ]
            outs = []
            for number, weight in zip(numbers, weights):
                values = vbuf[slot, side, number]
                outs.append(nn(weight, jnp.concatenate([values, jnp.ones_like(values)], axis=1)))
            for o, (rows, cols) in zip(outs, places):
                cols = pl.ds(pl.multiple_of(cols.start + side * SW, HEAD_DIM), HEAD_DIM)
                part[rows, cols] += o[:, :HEAD_DIM]
                wide[rows, cols] += o[:, HEAD_DIM:]
            return carry

        lax.fori_loop(0, (length + GROUP - 1) // GROUP, group, 0)
        out[0] = part[:, side * SW : (side + 1) * SW].astype(BF16)
        total[0] = to_lanes(wide[:, side * SW : (side + 1) * SW])


def request_place(code):
    return (
        pl.ds(pl.multiple_of(((code >> 2) & 3) << 6, BLOCK), BLOCK),
        pl.ds(pl.multiple_of((code & 3) << 7, HEAD_DIM), HEAD_DIM),
    )


def attend(meta, qa, qb, keys, values, memory_keys, memory_values, step, count, cap):
    micros = qa.shape[0]
    half, whole, lanes = seq_spec(ROWS, SW), seq_spec(ROWS, D), seq_spec(8, ROWS)
    anywhere = pl.BlockSpec(memory_space=pl.ANY)
    return pl.pallas_call(
        functools.partial(forward_kernel, step=step, count=count, cap=cap, micros=micros),
        grid_spec=pltpu.PrefetchScalarGridSpec(
            num_scalar_prefetch=1,
            grid=(micros,),
            in_specs=[half, half, whole, whole, anywhere, anywhere],
            out_specs=[half, half, lanes, lanes],
            scratch_shapes=[pltpu.VMEM((ROWS, D), F32), pltpu.VMEM((ROWS, D), F32)]
            + request_scratch(cap),
        ),
        out_shape=[
            seq_shape(micros, ROWS, SW),
            seq_shape(micros, ROWS, SW),
            seq_shape(micros, 8, ROWS, dtype=F32),
            seq_shape(micros, 8, ROWS, dtype=F32),
        ],
        compiler_params=params(24),
        name="attend",
        cost_estimate=pl.CostEstimate(flops=6_000_000_000, bytes_accessed=10_000_000, transcendentals=0),
    )(meta, qa, qb, keys, values, memory_keys, memory_values)


def combine_kernel(*refs, carried, sums):
    refs = list(refs)
    received = [refs.pop(0), refs.pop(0)] if carried else [None, None]
    parts = [refs.pop(0), refs.pop(0)]
    totals = [refs.pop(0), refs.pop(0)] if sums else [None, None]
    for got, part, total, out in zip(received, parts, totals, refs):
        value = part[0].astype(F32)
        if carried:
            value = value + got[0, :ROWS].astype(F32)
        out[0, :ROWS] = value.astype(BF16)
        if sums:
            lanes = total[0]
            if carried:
                lanes = lanes + unpack_lanes(got[0, ROWS:])
            out[0, ROWS:] = pack_lanes(lanes)


def combine(received, parts, totals=()):
    micros = parts[0].shape[0]
    sent = SENT if totals else ROWS
    half, lanes, packed = seq_spec(ROWS, SW), seq_spec(8, ROWS), seq_spec(sent, SW)
    return pl.pallas_call(
        functools.partial(combine_kernel, carried=bool(received), sums=bool(totals)),
        grid=(micros,),
        in_specs=[packed] * len(received) + [half] * 2 + [lanes] * len(totals),
        out_specs=[packed, packed],
        out_shape=[seq_shape(micros, sent, SW)] * 2,
        compiler_params=params(16),
        name="combine",
        cost_estimate=pl.CostEstimate(flops=2_000_000, bytes_accessed=7_000_000, transcendentals=0),
    )(*received, *parts, *totals)


def finish_kernel(acc_a, acc_b, pa, pb, ta, tb, x, weight, gain, mixed, low, total, middle, normed):
    for side, (acc, part, own) in enumerate(((acc_a, pa, ta), (acc_b, pb, tb))):
        lanes = unpack_lanes(acc[0, ROWS:]) + own[0]
        total[0, side] = lanes
        columns = to_columns(lanes)
        for h in range(SIDE):
            cols = slice(h * HEAD_DIM, (h + 1) * HEAD_DIM)
            place = slice((side * SIDE + h) * HEAD_DIM, (side * SIDE + h + 1) * HEAD_DIM)
            weighted = acc[0, :ROWS, cols].astype(F32) + part[0, :, cols].astype(F32)
            value = weighted / columns[:, h : h + 1]
            mixed[0, :, place] = value
            low[0, :, place] = value.astype(BF16)
    value = x[0].astype(F32) + nn(low[0], weight[...])
    middle[0] = value
    scale = lax.rsqrt(jnp.mean(value * value, axis=-1, keepdims=True) + EPS)
    normed[0] = (value * scale * gain[...]).astype(BF16)


def finish(acc_a, acc_b, pa, pb, ta, tb, x, weight, gain):
    micros = acc_a.shape[0]
    packed, half, lanes = seq_spec(SENT, SW), seq_spec(ROWS, SW), seq_spec(8, ROWS)
    whole = seq_spec(ROWS, D)
    return pl.pallas_call(
        finish_kernel,
        grid=(micros,),
        in_specs=[packed, packed, half, half, lanes, lanes, whole, full_spec(D, D), full_spec(1, D)],
        out_specs=[whole, whole, seq_spec(2, 8, ROWS), whole, whole],
        out_shape=[
            seq_shape(micros, ROWS, D, dtype=F32),
            seq_shape(micros, ROWS, D),
            seq_shape(micros, 2, 8, ROWS, dtype=F32),
            seq_shape(micros, ROWS, D, dtype=F32),
            seq_shape(micros, ROWS, D),
        ],
        compiler_params=params(),
        name="finish",
        cost_estimate=pl.CostEstimate(flops=2 * micros * ROWS * D * D, bytes_accessed=16_000_000, transcendentals=0),
    )(acc_a, acc_b, pa, pb, ta, tb, x, weight, gain)


TILE = 256


def feed_kernel(
    normed, incoming, middle, gate_weight, up_weight, down_weight, out, back, dg, du, dd, turned, acc, hid, bg, bu
):
    step = pl.program_id(0)
    micros = normed.shape[0]

    @pl.when(step == 0)
    def _():
        for m in range(micros):
            turned[:, m * ROWS : (m + 1) * ROWS] = normed[m].T
            acc[m] = middle[m]
            back[m] = jnp.zeros((ROWS, D), F32)

    wg, wu, wd = gate_weight[...], up_weight[...], down_weight[...]
    for m in range(micros):
        rows = slice(m * ROWS, (m + 1) * ROWS)
        gate = nn(normed[m], wg)
        upper = nn(normed[m], wu)
        slope = nt(incoming[m], wd)
        sigma = 1.0 / (1.0 + jnp.exp(-gate))
        silu = gate * sigma
        hid[rows] = (silu * upper).astype(BF16)
        bg[rows] = (slope * upper * (sigma * (1.0 + gate * (1.0 - sigma)))).astype(BF16)
        bu[rows] = (slope * silu).astype(BF16)
        acc[m] += nn(hid[rows], wd)
        back[m] += nt(bg[rows], wg) + nt(bu[rows], wu)
    dg[...] = nn(turned[...], bg[...]).astype(BF16)
    du[...] = nn(turned[...], bu[...]).astype(BF16)
    dd[...] = tn(hid[...], incoming[...].reshape(micros * ROWS, D)).astype(BF16)

    @pl.when(step == pl.num_programs(0) - 1)
    def _():
        out[...] = acc[...].astype(BF16)


def feed(normed, incoming, middle, gate_weight, up_weight, down_weight):
    micros = normed.shape[0]
    units = gate_weight.shape[1]
    whole = full_spec(micros, ROWS, D)
    wide = pl.BlockSpec((D, TILE), lambda f: (0, f))
    tall = pl.BlockSpec((TILE, D), lambda f: (f, 0))
    return pl.pallas_call(
        feed_kernel,
        grid=(units // TILE,),
        in_specs=[whole, whole, whole, wide, wide, tall],
        out_specs=[whole, whole, wide, wide, tall],
        out_shape=[
            seq_shape(micros, ROWS, D),
            seq_shape(micros, ROWS, D, dtype=F32),
            jax.ShapeDtypeStruct((D, units), BF16),
            jax.ShapeDtypeStruct((D, units), BF16),
            jax.ShapeDtypeStruct((units, D), BF16),
        ],
        scratch_shapes=[
            pltpu.VMEM((D, micros * ROWS), BF16),
            pltpu.VMEM((micros, ROWS, D), F32),
            pltpu.VMEM((micros * ROWS, TILE), BF16),
            pltpu.VMEM((micros * ROWS, TILE), BF16),
            pltpu.VMEM((micros * ROWS, TILE), BF16),
        ],
        compiler_params=params(),
        name="feed",
        cost_estimate=pl.CostEstimate(
            flops=18 * micros * ROWS * D * units, bytes_accessed=50_000_000, transcendentals=0
        ),
    )(normed, incoming, middle, gate_weight, up_weight, down_weight)


def prepare_kernel(back_normed, middle, incoming, gain, weight, mixed, total, da, db, back_middle, back_attn, dgain):
    value = middle[0]
    scale = lax.rsqrt(jnp.mean(value * value, axis=-1, keepdims=True) + EPS)
    hat = value * scale
    slope = back_normed[0] * gain[...]
    slope = incoming[0].astype(F32) + scale * (
        slope - hat * jnp.mean(slope * hat, axis=-1, keepdims=True)
    )
    back_middle[0] = slope
    back_attn[0] = slope.astype(BF16)
    dgain[0] = jnp.sum((back_normed[0] * hat).reshape(ROWS // 8, 8, D), axis=0)
    lane = lax.broadcasted_iota(jnp.int32, (ROWS, HEAD_DIM), 1)
    for side, out in enumerate((da, db)):
        columns = to_columns(total[0, side])
        packed = jnp.zeros((ROWS, HEAD_DIM), F32)
        back = nt(back_attn[0], weight[side * SW : (side + 1) * SW, :])
        for h in range(SIDE):
            cols = slice(h * HEAD_DIM, (h + 1) * HEAD_DIM)
            place = slice((side * SIDE + h) * HEAD_DIM, (side * SIDE + h + 1) * HEAD_DIM)
            part = back[:, cols]
            divisor = columns[:, h : h + 1]
            out[0, :ROWS, cols] = (part / divisor).astype(BF16)
            product = jnp.sum(part * mixed[0, :, place], axis=1, keepdims=True)
            packed = jnp.where(lane == h, -product / divisor, packed)
        out[0, ROWS:] = pack_lanes(packed.T[:8])


def prepare(back_normed, middle, incoming, gain, weight, mixed, total):
    micros = middle.shape[0]
    whole = seq_spec(ROWS, D)
    return pl.pallas_call(
        prepare_kernel,
        grid=(micros,),
        in_specs=[whole, whole, whole, full_spec(1, D), full_spec(D, D), whole, seq_spec(2, 8, ROWS)],
        out_specs=[seq_spec(SENT, SW), seq_spec(SENT, SW), whole, whole, seq_spec(8, D)],
        out_shape=[
            seq_shape(micros, SENT, SW),
            seq_shape(micros, SENT, SW),
            seq_shape(micros, ROWS, D, dtype=F32),
            seq_shape(micros, ROWS, D),
            seq_shape(micros, 8, D, dtype=F32),
        ],
        compiler_params=params(),
        name="prepare",
        cost_estimate=pl.CostEstimate(flops=2 * micros * ROWS * D * D, bytes_accessed=22_000_000, transcendentals=0),
    )(back_normed, middle, incoming, gain, weight, mixed, total)


def backward_kernel(
    meta, qa, qb, da, db, k, v, mk, mv, dqa, dqb, part, wide, kbuf, vbuf, sem, *, step, count, cap, micros
):
    micro = pl.program_id(0)
    here = meta[0]
    fetch = functools.partial(
        requests, meta, mk, mv, kbuf, vbuf, sem, step=step, count=count, cap=cap, micros=micros
    )
    request_ahead(fetch, micro, micros)
    for side, (q, d) in enumerate(((qa, da), (qb, db))):
        owner = meta[1 + 2 * step + side]
        columns = to_columns(unpack_lanes(d[0, ROWS:]))
        for h, (_, place) in enumerate(tiles(side)):
            wide[:, place] = jnp.broadcast_to(columns[:, h : h + 1], (ROWS, HEAD_DIM))

        def local(qrows, krows, masked):
            spots = tiles(side)
            scores = [nt(q[0, qrows, cols], k[0, krows, kcols]) for cols, kcols in spots]
            slopes = [nt(d[0, qrows, cols], v[0, krows, kcols]) for cols, kcols in spots]
            weights = [jnp.exp2(score * (SCALE * LOG2E)) for score in scores]
            if masked:
                weights = [jnp.where(causal_mask(), weight, 0.0) for weight in weights]
            slopes = [
                (weight * (slope + wide[qrows, kcols][:, :1])).astype(BF16)
                for weight, slope, (_, kcols) in zip(weights, slopes, spots)
            ]
            for slope, (_, kcols) in zip(slopes, spots):
                part[qrows, kcols] = nn(slope, k[0, krows, kcols])

        if step == 0:
            local(EVERYTHING, EVERYTHING, True)
        else:

            @pl.when(owner < here)
            def _():
                part[LOW, side * SW : (side + 1) * SW] = jnp.zeros((HALF, SW), F32)
                local(HIGH, EVERYTHING, False)

            @pl.when(owner > here)
            def _():
                local(EVERYTHING, LOW, False)

    fetch(micro, "wait")
    slot = micro % 2
    for side, (q, d, out) in enumerate(((qa, da, dqa), (qb, db, dqb))):
        owner = meta[1 + 2 * step + side]
        base = list_base(count) + list_at(owner, micro, side, micros, cap)
        length = meta[base]

        def group(i, carry):
            numbers = [i * GROUP + j for j in range(GROUP)]
            places = [request_place(meta[base + 1 + number]) for number in numbers]
            shifted = [
                (rows, pl.ds(pl.multiple_of(cols.start + side * SW, HEAD_DIM), HEAD_DIM))
                for rows, cols in places
            ]
            scores = [
                nt(q[0, rows, cols], kbuf[slot, side, number])
                for number, (rows, cols) in zip(numbers, places)
            ]
            slopes = [
                nt(d[0, rows, cols], vbuf[slot, side, number])
                for number, (rows, cols) in zip(numbers, places)
            ]
            weights = [jnp.exp2(score * (SCALE * LOG2E)) for score in scores]
            slopes = [
                jnp.where(
                    number < length, weight * (slope + wide[rows, cols][:, :BLOCK]), 0.0
                ).astype(BF16)
                for number, weight, slope, (rows, cols) in zip(numbers, weights, slopes, shifted)
            ]
            outs = [nn(slope, kbuf[slot, side, number]) for number, slope in zip(numbers, slopes)]
            for o, (rows, cols) in zip(outs, shifted):
                part[rows, cols] += o
            return carry

        lax.fori_loop(0, (length + GROUP - 1) // GROUP, group, 0)
        out[0] = part[:, side * SW : (side + 1) * SW].astype(BF16)


def unattend(meta, qa, qb, da, db, keys, values, memory_keys, memory_values, step, count, cap):
    micros = qa.shape[0]
    half, packed, whole = seq_spec(ROWS, SW), seq_spec(SENT, SW), seq_spec(ROWS, D)
    anywhere = pl.BlockSpec(memory_space=pl.ANY)
    return pl.pallas_call(
        functools.partial(backward_kernel, step=step, count=count, cap=cap, micros=micros),
        grid_spec=pltpu.PrefetchScalarGridSpec(
            num_scalar_prefetch=1,
            grid=(micros,),
            in_specs=[half, half, packed, packed, whole, whole, anywhere, anywhere],
            out_specs=[half, half],
            scratch_shapes=[pltpu.VMEM((ROWS, D), F32), pltpu.VMEM((ROWS, D), F32)]
            + request_scratch(cap),
        ),
        out_shape=[seq_shape(micros, ROWS, SW), seq_shape(micros, ROWS, SW)],
        compiler_params=params(24),
        name="unattend",
        cost_estimate=pl.CostEstimate(flops=8_000_000_000, bytes_accessed=12_000_000, transcendentals=0),
    )(meta, qa, qb, da, db, keys, values, memory_keys, memory_values)


def key_kernel(meta, k, v, *refs, steps, micros):
    number = len(steps)
    sources, (dk, dv, qbuf, dbuf, sem) = refs[: 4 * number], refs[4 * number :]
    micro = pl.program_id(0)
    here = meta[0]

    def fetch(m, act):
        slot = m % 2
        for i in range(number):
            for side in range(2):
                for source, place in (
                    (sources[4 * i + side], qbuf.at[slot, side, i]),
                    (sources[4 * i + 2 + side], dbuf.at[slot, side, i]),
                ):
                    copy = pltpu.make_async_copy(source.at[m], place, sem.at[slot])
                    if act == "start":
                        copy.start()
                    else:
                        copy.wait()

    request_ahead(fetch, micro, micros)
    fetch(micro, "wait")
    dk[0] = jnp.zeros((ROWS, D), F32)
    dv[0] = jnp.zeros((ROWS, D), F32)
    slot = micro % 2
    for side in range(2):
        spots = tiles(side)

        def one(i, step, own):
            q, d = qbuf.at[slot, side, i], dbuf.at[slot, side, i]
            shift = unpack_lanes(d[ROWS:, :])

            def local(qrows, krows, masked):
                scores = [nt(k[0, krows, kcols], q[qrows, cols]) for cols, kcols in spots]
                slopes = [nt(v[0, krows, kcols], d[qrows, cols]) for cols, kcols in spots]
                weights = [jnp.exp2(score * (SCALE * LOG2E)) for score in scores]
                if masked:
                    weights = [jnp.where(causal_mask(True), weight, 0.0) for weight in weights]
                slopes = [
                    (weight * (slope + shift[h : h + 1, qrows])).astype(BF16)
                    for h, (weight, slope) in enumerate(zip(weights, slopes))
                ]
                for weight, slope, (cols, kcols) in zip(weights, slopes, spots):
                    dk[0, krows, kcols] += nn(slope, q[qrows, cols])
                    dv[0, krows, kcols] += nn(weight.astype(BF16), d[qrows, cols])

            if own:
                local(EVERYTHING, EVERYTHING, True)
                return
            owner = meta[1 + 2 * step + side]

            @pl.when(owner < here)
            def _():
                local(HIGH, EVERYTHING, False)

            @pl.when(owner > here)
            def _():
                local(EVERYTHING, LOW, False)

        first = 0
        if steps[0] == 0:
            one(0, 0, True)
            first = 1

        def loop(i, carry):
            one(i, steps[0] + i, False)
            return carry

        lax.fori_loop(first, number, loop, 0)


def key_gradients(meta, keys, values, queries, slopes, steps):
    micros = keys.shape[0]
    whole = seq_spec(ROWS, D)
    anywhere = pl.BlockSpec(memory_space=pl.ANY)
    sources = []
    for step in steps:
        sources += [*queries[step], *slopes[step]]
    return pl.pallas_call(
        functools.partial(key_kernel, steps=steps, micros=micros),
        grid_spec=pltpu.PrefetchScalarGridSpec(
            num_scalar_prefetch=1,
            grid=(micros,),
            in_specs=[whole, whole] + [anywhere] * len(sources),
            out_specs=[whole, whole],
            scratch_shapes=[
                pltpu.VMEM((2, 2, len(steps), ROWS, SW), BF16),
                pltpu.VMEM((2, 2, len(steps), SENT, SW), BF16),
                pltpu.SemaphoreType.DMA((2,)),
            ],
        ),
        out_shape=[
            seq_shape(micros, ROWS, D, dtype=F32),
            seq_shape(micros, ROWS, D, dtype=F32),
        ],
        compiler_params=params(40),
        name="key_gradients",
        cost_estimate=pl.CostEstimate(
            flops=3_000_000_000 * len(steps), bytes_accessed=20_000_000, transcendentals=0
        ),
    )(meta, keys, values, *sources)


def unturn_kernel(acc_a, acc_b, pa, pb, dk, dv, dk_more, dv_more, cosine, sine, back):
    for h in range(HEADS):
        acc, part = (acc_a, pa) if h < SIDE else (acc_b, pb)
        cols = slice(h % SIDE * HEAD_DIM, (h % SIDE + 1) * HEAD_DIM)
        place = slice(h * HEAD_DIM, (h + 1) * HEAD_DIM)
        value = (acc[0, :, cols].astype(F32) + part[0, :, cols].astype(F32)) * SCALE
        key_place = slice(D + h * HEAD_DIM, D + (h + 1) * HEAD_DIM)
        back[0, :, place] = turn(value, cosine[...], -sine[...]).astype(BF16)
        back[0, :, key_place] = turn((dk[0, :, place] + dk_more[0, :, place]) * SCALE, cosine[...], -sine[...]).astype(BF16)
    back[0, :, 2 * D :] = (dv[0] + dv_more[0]).astype(BF16)


def unturn(acc_a, acc_b, pa, pb, key_parts, cosine, sine):
    micros = acc_a.shape[0]
    half, whole, angle = seq_spec(ROWS, SW), seq_spec(ROWS, D), full_spec(ROWS, HEAD_DIM)
    return pl.pallas_call(
        unturn_kernel,
        grid=(micros,),
        in_specs=[half, half, half, half, whole, whole, whole, whole, angle, angle],
        out_specs=seq_spec(ROWS, 3 * D),
        out_shape=seq_shape(micros, ROWS, 3 * D),
        compiler_params=params(),
        name="unturn",
        cost_estimate=pl.CostEstimate(flops=10_000_000, bytes_accessed=16_000_000, transcendentals=0),
    )(acc_a, acc_b, pa, pb, *key_parts, cosine, sine)


def bits(size):
    return [1 << i for i in range(size.bit_length() - 1)]


def sums_kernel(
    early,
    late,
    gains,
    early_out,
    late_out,
    gains_out,
    *scratch,
    count,
    shards,
):
    scratch = list(scratch)
    halves = [scratch.pop(0) for _ in bits(shards)]
    early_slots, late_slots, gain_in, gain_sum = (scratch.pop(0) for _ in range(4))
    ring_send, ring_recv, half_send, half_recv, gain_send, gain_recv = scratch
    here, shard = lax.axis_index("ctx"), lax.axis_index("fsdp")
    place = ring_place(count)
    neighbour = (ring_index(place + 1, count), ring_index(place + count - 1, count))
    partners = [("fsdp", shard, bit) for bit in bits(shards)] + [("ctx", here, bit) for bit in bits(count)]

    def partner(axis, index, bit):
        return {axis: index + bit * (1 - 2 * ((index // bit) % 2))}

    barrier = pltpu.get_barrier_semaphore()
    known = [{"ctx": neighbour[0]}, {"ctx": neighbour[1]}] + [partner(*p) for p in partners]
    for device in known:
        pl.semaphore_signal(barrier, inc=1, device_id=device, device_id_type=pl.DeviceIdType.MESH)
    pl.semaphore_wait(barrier, len(known))

    sent = []

    def send(source, target, send_sem, recv_sem, device):
        copy = pltpu.make_async_remote_copy(
            source, target, send_sem, recv_sem, device_id=device, device_id_type=pl.DeviceIdType.MESH
        )
        copy.start()
        sent.append(copy)
        return copy

    def halve_start(i):
        held = late if i == 0 else halves[i - 1]
        bit = (shard // (1 << i)) % 2
        return [
            send(
                held.at[2 * j + 1 - bit],
                halves[i].at[j],
                half_send.at[i, j],
                half_recv.at[i, j],
                partner("fsdp", shard, 1 << i),
            )
            for j in range(shards >> (i + 1))
        ]

    def halve_finish(i, copies):
        held = late if i == 0 else halves[i - 1]
        bit = (shard // (1 << i)) % 2
        for j, copy in enumerate(copies):
            copy.wait_recv()

            def add(c, carry):
                halves[i][j, c] = (
                    halves[i][j, c].astype(F32) + held[2 * j + bit, c].astype(F32)
                ).astype(BF16)
                return carry

            lax.fori_loop(0, 2 * count, add, 0)

    def gain_start(i):
        return send(gain_sum.at[i], gain_in.at[i], gain_send.at[i], gain_recv.at[i], partner(*partners[i]))

    def gain_finish(i, copy):
        copy.wait_recv()
        gain_sum[i + 1] = gain_sum[i] + gain_in[i]

    def flow(number, source, slots, out):
        def home(side, hop):
            sign = 1 - 2 * side
            return side * count + (place - sign * hop + 2 * count) % count

        def sum_start(hop):
            copies = []
            for side in range(2):
                held = source.at[home(side, 1)] if hop == 1 else slots.at[side, hop - 2]
                copies.append(
                    send(
                        held,
                        slots.at[side, hop - 1],
                        ring_send.at[number, side, hop - 1],
                        ring_recv.at[number, side, hop - 1],
                        {"ctx": neighbour[side]},
                    )
                )
            return copies

        def sum_finish(hop, copies):
            for side in range(2):
                copies[side].wait_recv()
                total = slots[side, hop - 1].astype(F32) + source[home(side, 1 + hop)].astype(F32)
                if hop == count - 1:
                    out[home(side, 0)] = total.astype(BF16)
                else:
                    slots[side, hop - 1] = total.astype(BF16)

        def copy_start(hop):
            copies = []
            for side in range(2):
                chunk = home(side, hop - 1)
                copies.append(
                    send(
                        out.at[chunk],
                        out.at[chunk],
                        ring_send.at[number, side, count - 2 + hop],
                        ring_recv.at[number, side, count - 2 + hop],
                        {"ctx": neighbour[side]},
                    )
                )
            return copies

        def copy_finish(copies):
            for copy in copies:
                copy.wait_recv()

        return sum_start, sum_finish, copy_start, copy_finish

    early_flow = flow(0, early, early_slots, early_out)
    late_flow = flow(1, halves[-1].at[0], late_slots, late_out)
    gain_sum[0] = gains[...]
    stages, exchanges = len(halves), len(partners)
    half = halve_start(0)
    gain = gain_start(0)
    stage, exchange = 0, 0
    ring = early_flow[0](1)
    for hop in range(1, count):
        early_flow[1](hop, ring)
        if hop < count - 1:
            ring = early_flow[0](hop + 1)
        if stage < stages - 1:
            halve_finish(stage, half)
            stage += 1
            half = halve_start(stage)
        if exchange < exchanges:
            gain_finish(exchange, gain)
            exchange += 1
            if exchange < exchanges:
                gain = gain_start(exchange)
    ring = early_flow[2](1)
    halve_finish(stage, half)
    late_ring = late_flow[0](1)
    for hop in range(1, count):
        early_flow[3](ring)
        if hop < count - 1:
            ring = early_flow[2](hop + 1)
        late_flow[1](hop, late_ring)
        if hop < count - 1:
            late_ring = late_flow[0](hop + 1)
        if exchange < exchanges:
            gain_finish(exchange, gain)
            exchange += 1
            if exchange < exchanges:
                gain = gain_start(exchange)
    for hop in range(1, count):
        late_flow[3](late_flow[2](hop))
    gains_out[...] = gain_sum[exchanges]
    for copy in sent:
        copy.wait_send()


def sums(early, late, gains):
    shards, chunks, rows, width = late.shape
    count = chunks // 2
    more = early.shape[-1]
    exchanges = len(bits(shards)) + len(bits(count))
    vmem = pl.BlockSpec(memory_space=pltpu.VMEM)
    return pl.pallas_call(
        functools.partial(sums_kernel, count=count, shards=shards),
        in_specs=[vmem] * 3,
        out_specs=[vmem] * 3,
        out_shape=[
            jax.ShapeDtypeStruct(early.shape, BF16),
            jax.ShapeDtypeStruct(late.shape[1:], BF16),
            jax.ShapeDtypeStruct(gains.shape, F32),
        ],
        scratch_shapes=[pltpu.VMEM((bit and shards // (2 * bit), chunks, rows, width), BF16) for bit in bits(shards)]
        + [
            pltpu.VMEM((2, count - 1, early.shape[1], more), BF16),
            pltpu.VMEM((2, count - 1, rows, width), BF16),
            pltpu.VMEM((exchanges,) + gains.shape, F32),
            pltpu.VMEM((exchanges + 1,) + gains.shape, F32),
            pltpu.SemaphoreType.DMA((2, 2, 2 * count - 2)),
            pltpu.SemaphoreType.DMA((2, 2, 2 * count - 2)),
            pltpu.SemaphoreType.DMA((len(bits(shards)), shards // 2)),
            pltpu.SemaphoreType.DMA((len(bits(shards)), shards // 2)),
            pltpu.SemaphoreType.DMA((exchanges,)),
            pltpu.SemaphoreType.DMA((exchanges,)),
        ],
        compiler_params=pltpu.CompilerParams(
            vmem_limit_bytes=48 * 2**20, collective_id=0, has_side_effects=True
        ),
        name="sums",
        cost_estimate=pl.CostEstimate(flops=50_000_000, bytes_accessed=400_000_000, transcendentals=0),
    )(early, late, gains)


def to_chunks(value, count):
    rows, width = value.shape[-2:]
    lead = value.shape[:-2]
    chunks = 2 * count
    if rows % (16 * chunks) == 0:
        return value.reshape(lead + (chunks, rows // chunks, width))
    step = -(-width // (chunks * HEAD_DIM)) * HEAD_DIM
    value = jnp.pad(value, [(0, 0)] * len(lead) + [(0, 0), (0, step * chunks - width)])
    return jnp.moveaxis(value.reshape(lead + (rows, chunks, step)), -2, -3)


def from_chunks(value, rows, width):
    if value.shape[0] * value.shape[1] == rows:
        return value.reshape(rows, width)
    return jnp.moveaxis(value, 0, 1).reshape(rows, -1)[:, :width]


def norm_parts(value):
    scale = lax.rsqrt(jnp.mean(value * value, axis=-1, keepdims=True) + EPS)
    return value * scale, scale


def norm_back(hat, scale, back, gain):
    slope = back * gain
    return scale * (slope - hat * jnp.mean(slope * hat, axis=-1, keepdims=True))


def body(
    tokens,
    cotangent,
    query_weight,
    key_weight,
    value_weight,
    output_weight,
    gate_weight,
    up_weight,
    down_weight,
    first_gain,
    second_gain,
    cache_keys,
    cache_values,
    block_indices,
    partner,
):
    count = lax.axis_size("ctx")
    here = lax.axis_index("ctx")
    micros = tokens.shape[0]
    rows = micros * ROWS
    onward, backward = ring_pairs(count)

    def gather(value):
        return lax.all_gather(value, "fsdp", axis=0, tiled=True)

    indices = lax.all_gather(block_indices, "ctx", axis=1, tiled=True)
    gains = lax.all_gather(jnp.stack([first_gain, second_gain]), "fsdp", axis=1, tiled=True)
    full_query = gather(query_weight)
    full_key = gather(key_weight)
    full_value = gather(value_weight)
    full_output = gather(output_weight)
    full_gate = gather(gate_weight)
    full_up = gather(up_weight)
    full_down = gather(down_weight)
    gain_one = gains[0:1].astype(F32)
    gain_two = gains[1:2].astype(F32)

    pieces_at = jnp.stack([here, 2 * count - 1 - here])
    positions = (pieces_at[:, None] * HALF + jnp.arange(HALF, dtype=jnp.int32)[None, :]).reshape(ROWS)
    inverse = 10000.0 ** (-jnp.arange(HEAD_DIM // 2, dtype=F32) * 2.0 / HEAD_DIM)
    phase = positions.astype(F32)[:, None] * inverse[None, :]
    cosine = jnp.tile(jnp.cos(phase), (1, 2))
    sine = jnp.sin(phase)
    sine = jnp.concatenate([-sine, sine], axis=1)

    meta, cap = make_meta(indices, partner, cache_keys.shape[1] // BLOCK, count)
    memory_keys, memory_values = collect(meta, cache_keys, cache_values, count, cap)

    x = tokens.reshape(micros, ROWS, D)
    normed_low, qa, qb = project_query(x, gain_one, full_query, cosine, sine)
    keys, values = project_pairs(normed_low, full_key, full_value, cosine, sine)

    queries = [(qa, qb)]
    for _ in range(count - 1):
        qa, qb = lax.ppermute(qa, "ctx", onward), lax.ppermute(qb, "ctx", backward)
        queries.append((qa, qb))

    acc = ()
    for step in list(range(1, count)) + [0]:
        pa, pb, ta, tb = attend(
            meta, *queries[step], keys, values, memory_keys, memory_values, step, count, cap
        )
        if acc:
            acc = (lax.ppermute(acc[0], "ctx", onward), lax.ppermute(acc[1], "ctx", backward))
        if step == 0:
            mixed, mixed_low, total, middle, middle_low = finish(
                *acc, pa, pb, ta, tb, x, full_output, gain_two
            )
        else:
            acc = combine(acc, (pa, pb), (ta, tb))

    incoming = cotangent.reshape(micros, ROWS, D)
    layer_output, back_mid_normed, gradient_gate, gradient_up, gradient_down = feed(
        middle_low, incoming, middle, full_gate, full_up, full_down
    )
    da, db, back_middle, back_attn, gain_part = prepare(
        back_mid_normed, middle, incoming, gain_two, full_output, mixed, total
    )
    gradient_second = jnp.sum(gain_part, axis=(0, 1))
    gradient_output = jnp.einsum(
        "tc,td->cd", mixed_low.reshape(rows, D), back_attn.reshape(rows, D), preferred_element_type=F32
    ).astype(BF16)
    back_middle = back_middle.reshape(rows, D)
    inputs = tokens.reshape(rows, D).astype(F32)

    slopes = [(da, db)]
    for _ in range(count - 1):
        da, db = slopes[-1]
        slopes.append((lax.ppermute(da, "ctx", onward), lax.ppermute(db, "ctx", backward)))
    slopes[1], gradient_output = lax.optimization_barrier((slopes[1], gradient_output))

    acc = ()
    for step in range(count):
        part = unattend(
            meta, *queries[step], *slopes[step], keys, values, memory_keys, memory_values, step, count, cap
        )
        if step == 0:
            own = part
            continue
        if acc:
            acc = (lax.ppermute(acc[0], "ctx", onward), lax.ppermute(acc[1], "ctx", backward))
        acc = combine(acc, part)
    key_parts = [
        part
        for steps in (range(count // 2), range(count // 2, count))
        for part in key_gradients(meta, keys, values, queries, slopes, steps)
    ]
    ra, rb = lax.ppermute(acc[0], "ctx", onward), lax.ppermute(acc[1], "ctx", backward)
    back = unturn(ra, rb, *own, key_parts, cosine, sine).reshape(rows, 3 * D)
    normed_low = normed_low.reshape(rows, D)
    late = jnp.einsum("tc,td->cd", normed_low, back, preferred_element_type=F32).astype(BF16)
    back_in_normed = (
        jnp.einsum("td,cd->tc", back[:, :D], full_query, preferred_element_type=F32)
        + jnp.einsum("td,cd->tc", back[:, D : 2 * D], full_key, preferred_element_type=F32)
        + jnp.einsum("td,cd->tc", back[:, 2 * D :], full_value, preferred_element_type=F32)
    )
    in_hat, in_scale = norm_parts(inputs)
    gradient_first = jnp.sum(back_in_normed * in_hat, axis=0)
    input_gradient = back_middle + norm_back(in_hat, in_scale, back_in_normed, gain_one)

    def scatter(part):
        return lax.psum_scatter(part, "fsdp", scatter_dimension=0, tiled=True)

    early = jnp.concatenate(
        [
            scatter(part).reshape(D // lax.axis_size("fsdp"), -1)
            for part in (gradient_down, gradient_gate, gradient_up, gradient_output)
        ],
        axis=1,
    )
    shards = lax.axis_size("fsdp")
    late = late.reshape(shards, D // shards, 3 * D)
    gains_part = jnp.concatenate(
        [gradient_first[None], gradient_second[None], jnp.zeros((6, D), F32)], axis=0
    )
    early_sum, late_sum, gain_changes = sums(to_chunks(early, count), to_chunks(late, count), gains_part)
    early = from_chunks(early_sum, *early.shape).astype(F32)
    three = from_chunks(late_sum, *late.shape[1:]).astype(F32)
    units = gate_weight.shape[1]
    own_rows = D // lax.axis_size("fsdp")
    gain_changes = lax.dynamic_slice_in_dim(
        gain_changes, lax.axis_index("fsdp") * own_rows, own_rows, axis=1
    )
    return (
        layer_output.reshape(tokens.shape),
        input_gradient.reshape(tokens.shape),
        three[:, :D],
        three[:, D : 2 * D],
        three[:, 2 * D :],
        early[:, 3 * units :],
        early[:, units : 2 * units],
        early[:, 2 * units : 3 * units],
        early[:, :units].reshape(down_weight.shape),
        gain_changes[0],
        gain_changes[1],
    )


def solution(mesh):
    split = P("fsdp", "ctx", None, None, None)
    shard = P("fsdp", None)
    return jax.shard_map(
        body,
        mesh=mesh,
        in_specs=(
            split,
            split,
            *([shard] * 7),
            P("fsdp"),
            P("fsdp"),
            P("fsdp", "ctx", None),
            P("fsdp", "ctx", None),
            P("fsdp", "ctx", None, None, None, None),
            P("fsdp"),
        ),
        out_specs=(split, split, *([shard] * 7), P("fsdp"), P("fsdp")),
        check_vma=False,
    )
```

```python
import functools

import jax
import jax.numpy as jnp
from jax import lax
from jax.experimental import pallas as pl
from jax.experimental.pallas import tpu as pltpu
from jax.sharding import PartitionSpec as P

D = 1024
HEADS = 8
HEAD_DIM = 128
HALF = 128
ROWS = 2 * HALF
BLOCK = 64
TOPK = 4
SIDE = HEADS // 2
SW = SIDE * HEAD_DIM
GROUP = 8
EPS = 1e-05
SCALE = HEAD_DIM**-0.5
LOG2E = 1.4426950408889634
F32 = jnp.float32
BF16 = jnp.bfloat16
EXTRA = 16
SENT = ROWS + EXTRA


def nn(a, b):
    return lax.dot_general(a, b, (((1,), (0,)), ((), ())), preferred_element_type=F32)


def nt(a, b):
    return lax.dot_general(a, b, (((1,), (1,)), ((), ())), preferred_element_type=F32)


def tn(a, b):
    return lax.dot_general(a, b, (((0,), (0,)), ((), ())), preferred_element_type=F32)


def params(mib=56):
    return pltpu.CompilerParams(vmem_limit_bytes=mib * 2**20)


def ring_order(count):
    if count == 8:
        return [0, 2, 4, 6, 7, 5, 3, 1]
    half = count // 2
    return list(range(half)) + [count - 1 - i for i in range(count - half)]


def ring_place(count):
    here = lax.axis_index("ctx")
    half = count // 2
    if count == 8:
        turned = here % 2
        return (1 - turned) * (here // 2) + turned * (count - 1 - here // 2)
    turned = here // half
    return (1 - turned) * here + turned * (count - 1 + half - here)


def ring_index(place, count):
    half = count // 2
    place = place % count
    turned = place // half
    if count == 8:
        return (1 - turned) * 2 * place + turned * (2 * count - 1 - 2 * place)
    return (1 - turned) * place + turned * (count - 1 + half - place)


def ring_pairs(count):
    order = ring_order(count)
    onward = [(order[i], order[(i + 1) % count]) for i in range(count)]
    return onward, [(b, a) for a, b in onward]


def list_base(count):
    return 1 + 2 * count


def list_at(owner, micro, side, micros, cap):
    return ((owner * micros + micro) * 2 + side) * (cap + 1)


def make_meta(indices, partner, cb_dev, count):
    micros = indices.shape[0]
    here = lax.axis_index("ctx")
    order = ring_order(count)
    place = ring_place(count)
    steps = jnp.arange(count, dtype=jnp.int32)
    at = jnp.stack([(place - steps) % count, (place + steps) % count], axis=1)
    owners = sum(jnp.where(at == p, d, 0) for p, d in enumerate(order))
    blocks = cb_dev * count
    cap = 2 * 128 // count
    side_shape = (micros, count, 2 * ROWS // (2 * BLOCK), 2, SIDE, TOPK)
    index = indices.reshape(side_shape).transpose(1, 0, 3, 2, 4, 5)
    index = index.reshape(count, micros, 2, -1)
    number = index % blocks
    mine = (number // cb_dev) == here
    own = jnp.arange(micros, dtype=jnp.int32)[None, :, None, None]
    document = jnp.where(index < blocks, own, partner[None, :, None, None])
    entries = index.shape[-1]
    entry = jnp.arange(entries, dtype=jnp.int32)
    query_block = entry // (SIDE * TOPK)
    head = entry // TOPK % SIDE
    code = ((document * cb_dev + number % cb_dev) * 4 + query_block) * SIDE + head
    before = (entry[:, None] < entry[None, :]).astype(F32)
    flags = mine.astype(F32)
    rank = jnp.dot(flags.reshape(-1, entries), before, preferred_element_type=F32).reshape(flags.shape)
    rank = rank.astype(jnp.int32)
    slot = jnp.arange(cap, dtype=jnp.int32)
    hit = mine[..., None, :] & (rank[..., None, :] == slot[:, None])
    codes = jnp.sum(jnp.where(hit, code[..., None, :], 0), axis=-1)
    length = jnp.sum(mine.astype(jnp.int32), axis=-1, keepdims=True)
    lists = jnp.concatenate([length, codes], axis=-1).reshape(-1)
    return jnp.concatenate([here.reshape(1), owners.reshape(-1), lists]).astype(jnp.int32), cap


def share_kernel(indices, gains, all_indices, all_gains, send_sem, recv_sem, *, count, shards):
    here, shard = lax.axis_index("ctx"), lax.axis_index("fsdp")
    groups = (("ctx", here, count, indices, all_indices), ("fsdp", shard, shards, gains, all_gains))
    barrier = pltpu.get_barrier_semaphore()
    for axis, index, size, _, _ in groups:
        for k in range(1, size):
            pl.semaphore_signal(
                barrier, inc=1, device_id={axis: (index + k) % size}, device_id_type=pl.DeviceIdType.MESH
            )
    pl.semaphore_wait(barrier, count + shards - 2)
    copies = []
    for number, (axis, index, size, source, target) in enumerate(groups):
        for k in range(1, size):
            copy = pltpu.make_async_remote_copy(
                source,
                target.at[index],
                send_sem.at[number, k],
                recv_sem.at[number, k],
                device_id={axis: (index + k) % size},
                device_id_type=pl.DeviceIdType.MESH,
            )
            copy.start()
            copies.append(copy)
        target[index] = source[...]
    for copy in copies:
        copy.wait()


def share(indices, gains, count, shards):
    vmem = pl.BlockSpec(memory_space=pltpu.VMEM)
    most = max(count, shards)
    return pl.pallas_call(
        functools.partial(share_kernel, count=count, shards=shards),
        in_specs=[vmem, vmem],
        out_specs=[vmem, vmem],
        out_shape=[
            jax.ShapeDtypeStruct((count,) + indices.shape, indices.dtype),
            jax.ShapeDtypeStruct((shards,) + gains.shape, gains.dtype),
        ],
        scratch_shapes=[pltpu.SemaphoreType.DMA((2, most)), pltpu.SemaphoreType.DMA((2, most))],
        compiler_params=pltpu.CompilerParams(
            vmem_limit_bytes=8 * 2**20, collective_id=1, has_side_effects=True
        ),
        name="share",
        cost_estimate=pl.CostEstimate(flops=0, bytes_accessed=20_000_000, transcendentals=0),
    )(indices, gains)


def collect_kernel(meta, ck, cv, mk, mv, sem_k, sem_v, *, micros, count, cap):
    owner = pl.program_id(0)

    def list_of(i):
        base = list_base(count) + (owner * 2 * micros + i) * (cap + 1)
        return base, meta[base]

    def start(i, carry):
        base, length = list_of(i)

        def one(j, c):
            code = meta[base + 1 + j]
            head = (i & 1) * SIDE + (code & (SIDE - 1))
            rows = pl.ds(pl.multiple_of((code >> 4) << 6, BLOCK), BLOCK)
            cols = pl.ds(pl.multiple_of(head << 7, HEAD_DIM), HEAD_DIM)
            pltpu.make_async_copy(ck.at[rows, cols], mk.at[i >> 1, 0, i & 1, j], sem_k).start()
            pltpu.make_async_copy(cv.at[rows, cols], mv.at[i >> 1, 0, i & 1, j], sem_v).start()
            return c

        def clear(j, c):
            mk[i >> 1, 0, i & 1, j] = jnp.zeros((BLOCK, HEAD_DIM), BF16)
            mv[i >> 1, 0, i & 1, j] = jnp.zeros((BLOCK, HEAD_DIM), BF16)
            return c

        lax.fori_loop(0, length, one, carry)
        return lax.fori_loop(length, (length + GROUP - 1) // GROUP * GROUP, clear, carry)

    def finish(i, carry):
        _, length = list_of(i)
        rounds = length // GROUP

        def many(g, c):
            some = pl.ds(g * GROUP, GROUP)
            for place, sem in ((mk, sem_k), (mv, sem_v)):
                whole = place.at[i >> 1, 0, i & 1, some]
                pltpu.make_async_copy(whole, whole, sem).wait()
            return c

        def one(j, c):
            for place, sem in ((mk, sem_k), (mv, sem_v)):
                whole = place.at[i >> 1, 0, i & 1, j]
                pltpu.make_async_copy(whole, whole, sem).wait()
            return c

        lax.fori_loop(0, rounds, many, carry)
        return lax.fori_loop(rounds * GROUP, length, one, carry)

    lax.fori_loop(0, 2 * micros, start, 0)
    lax.fori_loop(0, 2 * micros, finish, 0)


def collect(meta, cache_keys, cache_values, count, cap):
    micros = cache_keys.shape[0]
    shape = jax.ShapeDtypeStruct((micros, count, 2, cap, BLOCK, HEAD_DIM), BF16)
    anywhere = pl.BlockSpec(memory_space=pl.ANY)
    block = pl.BlockSpec((micros, 1, 2, cap, BLOCK, HEAD_DIM), lambda o, meta: (0, o, 0, 0, 0, 0))
    return pl.pallas_call(
        functools.partial(collect_kernel, micros=micros, count=count, cap=cap),
        grid_spec=pltpu.PrefetchScalarGridSpec(
            num_scalar_prefetch=1,
            grid=(count,),
            in_specs=[anywhere, anywhere],
            out_specs=[block, block],
            scratch_shapes=[pltpu.SemaphoreType.DMA, pltpu.SemaphoreType.DMA],
        ),
        out_shape=[shape, shape],
        compiler_params=params(),
        name="collect",
        cost_estimate=pl.CostEstimate(flops=0, bytes_accessed=90_000_000, transcendentals=0),
    )(meta, cache_keys.reshape(-1, D), cache_values.reshape(-1, D))


def turn(value, cosine, sine):
    return value * cosine + pltpu.roll(value, HEAD_DIM // 2, 1) * sine


def first_kernel(x, gain, weight, cosine, sine, normed, qa, qb):
    value = x[0].astype(F32)
    scale = lax.rsqrt(jnp.mean(value * value, axis=-1, keepdims=True) + EPS)
    low = (value * scale * gain[...]).astype(BF16)
    normed[0] = low
    product = nn(low, weight[...])
    for h in range(HEADS):
        cols = slice(h * HEAD_DIM, (h + 1) * HEAD_DIM)
        out = qa if h < SIDE else qb
        place = slice((h % SIDE) * HEAD_DIM, (h % SIDE + 1) * HEAD_DIM)
        out[0, :, place] = turn(product[:, cols], cosine[...], sine[...]).astype(BF16)


def second_kernel(normed, weights, cosine, sine, keys, values, turned):
    low = normed[0]
    turned[...] = low.T
    product = nn(low, weights[0])
    for h in range(HEADS):
        cols = slice(h * HEAD_DIM, (h + 1) * HEAD_DIM)
        keys[0, :, cols] = turn(product[:, cols], cosine[...], sine[...]).astype(BF16)
    values[0] = nn(low, weights[1]).astype(BF16)


def seq_spec(*shape):
    return pl.BlockSpec((1,) + shape, lambda m, *_: (m,) + (0,) * len(shape))


def full_spec(*shape):
    return pl.BlockSpec(shape, lambda m, *_: (0,) * len(shape))


def seq_shape(micros, *shape, dtype=BF16):
    return jax.ShapeDtypeStruct((micros,) + shape, dtype)


def project_query(x, gain, weight, cosine, sine):
    micros = x.shape[0]
    return pl.pallas_call(
        first_kernel,
        grid=(micros,),
        in_specs=[
            seq_spec(ROWS, D),
            full_spec(1, D),
            full_spec(D, D),
            full_spec(ROWS, HEAD_DIM),
            full_spec(ROWS, HEAD_DIM),
        ],
        out_specs=[seq_spec(ROWS, D), seq_spec(ROWS, SW), seq_spec(ROWS, SW)],
        out_shape=[seq_shape(micros, ROWS, D), seq_shape(micros, ROWS, SW), seq_shape(micros, ROWS, SW)],
        compiler_params=params(),
        name="project_query",
        cost_estimate=pl.CostEstimate(flops=2 * micros * ROWS * D * D, bytes_accessed=8_000_000, transcendentals=0),
    )(x, gain, weight, cosine, sine)


def project_pairs(normed, weights, cosine, sine):
    micros = normed.shape[0]
    return pl.pallas_call(
        second_kernel,
        grid=(micros,),
        in_specs=[
            seq_spec(ROWS, D),
            full_spec(2, D, D),
            full_spec(ROWS, HEAD_DIM),
            full_spec(ROWS, HEAD_DIM),
        ],
        out_specs=[seq_spec(ROWS, D), seq_spec(ROWS, D), pl.BlockSpec((D, ROWS), lambda m: (0, m))],
        out_shape=[
            seq_shape(micros, ROWS, D),
            seq_shape(micros, ROWS, D),
            jax.ShapeDtypeStruct((D, micros * ROWS), BF16),
        ],
        compiler_params=params(),
        name="project_pairs",
        cost_estimate=pl.CostEstimate(flops=4 * micros * ROWS * D * D, bytes_accessed=10_000_000, transcendentals=0),
    )(normed, weights, cosine, sine)


def causal_mask(turned=False):
    row = lax.broadcasted_iota(jnp.int32, (ROWS, ROWS), 0)
    col = lax.broadcasted_iota(jnp.int32, (ROWS, ROWS), 1)
    return row <= col if turned else row >= col


def to_lanes(wide):
    lane = lax.broadcasted_iota(jnp.int32, (ROWS, HEAD_DIM), 1)
    packed = jnp.zeros((ROWS, HEAD_DIM), F32)
    for h in range(SIDE):
        packed = jnp.where(lane == h, wide[:, h * HEAD_DIM : (h + 1) * HEAD_DIM], packed)
    return packed.T[:8]


def to_columns(lanes):
    return jnp.concatenate([lanes, jnp.zeros((HEAD_DIM - 8, ROWS), F32)], axis=0).T


def split3(value):
    high = value.astype(BF16).astype(F32)
    middle = (value - high).astype(BF16).astype(F32)
    return high, middle, value - high - middle


def pack_lanes(lanes):
    high, middle, low = split3(lanes)
    rows = jnp.concatenate(
        [jnp.concatenate([high, middle], axis=1), jnp.concatenate([low, jnp.zeros_like(low)], axis=1)],
        axis=0,
    )
    return rows.astype(BF16)


def unpack_lanes(rows):
    value = rows.astype(F32)
    return value[:8, :ROWS] + value[:8, ROWS:] + value[8:, :ROWS]


def requests(meta, mk, mv, kbuf, vbuf, sem, micro, act, *, step, count, cap, micros):
    slot = micro % 2
    for side in range(2):
        owner = meta[1 + 2 * step + side]
        length = meta[list_base(count) + list_at(owner, micro, side, micros, cap)]

        def one(g, carry):
            some = pl.ds(g * GROUP, GROUP)
            for source, place in ((mk, kbuf), (mv, vbuf)):
                copy = pltpu.make_async_copy(
                    source.at[micro, owner, side, some], place.at[slot, side, some], sem.at[slot]
                )
                if act == "start":
                    copy.start()
                else:
                    copy.wait()
            return carry

        lax.fori_loop(0, (length + GROUP - 1) // GROUP, one, 0)


def request_ahead(fetch, micro, micros):
    @pl.when(micro == 0)
    def _():
        fetch(micro, "start")

    @pl.when(micro + 1 < micros)
    def _():
        fetch(micro + 1, "start")


def request_scratch(cap):
    return [
        pltpu.VMEM((2, 2, cap, BLOCK, HEAD_DIM), BF16),
        pltpu.VMEM((2, 2, cap, BLOCK, HEAD_DIM), BF16),
        pltpu.SemaphoreType.DMA((2,)),
    ]


EVERYTHING, LOW, HIGH = slice(0, ROWS), slice(0, HALF), slice(HALF, ROWS)


def tiles(side):
    return [
        (
            slice(h * HEAD_DIM, (h + 1) * HEAD_DIM),
            slice((side * SIDE + h) * HEAD_DIM, (side * SIDE + h + 1) * HEAD_DIM),
        )
        for h in range(SIDE)
    ]


def forward_kernel(
    meta, qa, qb, k, v, mk, mv, pa, pb, ta, tb, part, wide, kbuf, vbuf, sem, *, step, count, cap, micros
):
    micro = pl.program_id(0)
    here = meta[0]
    fetch = functools.partial(
        requests, meta, mk, mv, kbuf, vbuf, sem, step=step, count=count, cap=cap, micros=micros
    )
    request_ahead(fetch, micro, micros)
    for side, q in enumerate((qa, qb)):
        owner = meta[1 + 2 * step + side]

        def local(qrows, krows, masked):
            spots = tiles(side)
            scores = [nt(q[0, qrows, cols], k[0, krows, kcols]) for cols, kcols in spots]
            weights = [jnp.exp2(score * (SCALE * LOG2E)) for score in scores]
            if masked:
                weights = [jnp.where(causal_mask(), weight, 0.0) for weight in weights]
            for weight, (cols, kcols) in zip(weights, spots):
                values = v[0, krows, kcols]
                more = jnp.concatenate([values, jnp.ones_like(values)], axis=1)
                out = nn(weight.astype(BF16), more)
                part[qrows, kcols] = out[:, :HEAD_DIM]
                wide[qrows, kcols] = out[:, HEAD_DIM:]

        if step == 0:
            local(EVERYTHING, EVERYTHING, True)
        else:

            @pl.when(owner < here)
            def _():
                zeros = jnp.zeros((HALF, SW), F32)
                part[LOW, side * SW : (side + 1) * SW] = zeros
                wide[LOW, side * SW : (side + 1) * SW] = zeros
                local(HIGH, EVERYTHING, False)

            @pl.when(owner > here)
            def _():
                local(EVERYTHING, LOW, False)

    fetch(micro, "wait")
    slot = micro % 2
    for side, (q, out, total) in enumerate(((qa, pa, ta), (qb, pb, tb))):
        owner = meta[1 + 2 * step + side]
        base = list_base(count) + list_at(owner, micro, side, micros, cap)
        length = meta[base]

        def group(i, carry):
            numbers = [i * GROUP + j for j in range(GROUP)]
            places = [request_place(meta[base + 1 + number]) for number in numbers]
            scores = [
                nt(q[0, rows, cols], kbuf[slot, side, number])
                for number, (rows, cols) in zip(numbers, places)
            ]
            weights = [
                jnp.where(number < length, jnp.exp2(score * (SCALE * LOG2E)), 0.0).astype(BF16)
                for number, score in zip(numbers, scores)
            ]
            outs = []
            for number, weight in zip(numbers, weights):
                values = vbuf[slot, side, number]
                outs.append(nn(weight, jnp.concatenate([values, jnp.ones_like(values)], axis=1)))
            for o, (rows, cols) in zip(outs, places):
                cols = pl.ds(pl.multiple_of(cols.start + side * SW, HEAD_DIM), HEAD_DIM)
                part[rows, cols] += o[:, :HEAD_DIM]
                wide[rows, cols] += o[:, HEAD_DIM:]
            return carry

        lax.fori_loop(0, (length + GROUP - 1) // GROUP, group, 0)
        out[0] = part[:, side * SW : (side + 1) * SW].astype(BF16)
        total[0] = to_lanes(wide[:, side * SW : (side + 1) * SW])


def request_place(code):
    return (
        pl.ds(pl.multiple_of(((code >> 2) & 3) << 6, BLOCK), BLOCK),
        pl.ds(pl.multiple_of((code & 3) << 7, HEAD_DIM), HEAD_DIM),
    )


def attend(meta, qa, qb, keys, values, memory_keys, memory_values, step, count, cap):
    micros = qa.shape[0]
    half, whole, lanes = seq_spec(ROWS, SW), seq_spec(ROWS, D), seq_spec(8, ROWS)
    anywhere = pl.BlockSpec(memory_space=pl.ANY)
    return pl.pallas_call(
        functools.partial(forward_kernel, step=step, count=count, cap=cap, micros=micros),
        grid_spec=pltpu.PrefetchScalarGridSpec(
            num_scalar_prefetch=1,
            grid=(micros,),
            in_specs=[half, half, whole, whole, anywhere, anywhere],
            out_specs=[half, half, lanes, lanes],
            scratch_shapes=[pltpu.VMEM((ROWS, D), F32), pltpu.VMEM((ROWS, D), F32)]
            + request_scratch(cap),
        ),
        out_shape=[
            seq_shape(micros, ROWS, SW),
            seq_shape(micros, ROWS, SW),
            seq_shape(micros, 8, ROWS, dtype=F32),
            seq_shape(micros, 8, ROWS, dtype=F32),
        ],
        compiler_params=params(24),
        name="attend",
        cost_estimate=pl.CostEstimate(flops=6_000_000_000, bytes_accessed=10_000_000, transcendentals=0),
    )(meta, qa, qb, keys, values, memory_keys, memory_values)


def combine_kernel(*refs, carried, sums):
    refs = list(refs)
    received = [refs.pop(0), refs.pop(0)] if carried else [None, None]
    parts = [refs.pop(0), refs.pop(0)]
    totals = [refs.pop(0), refs.pop(0)] if sums else [None, None]
    for got, part, total, out in zip(received, parts, totals, refs):
        value = part[0].astype(F32)
        if carried:
            value = value + got[0, :ROWS].astype(F32)
        out[0, :ROWS] = value.astype(BF16)
        if sums:
            lanes = total[0]
            if carried:
                lanes = lanes + unpack_lanes(got[0, ROWS:])
            out[0, ROWS:] = pack_lanes(lanes)


def combine(received, parts, totals=()):
    micros = parts[0].shape[0]
    sent = SENT if totals else ROWS
    half, lanes, packed = seq_spec(ROWS, SW), seq_spec(8, ROWS), seq_spec(sent, SW)
    return pl.pallas_call(
        functools.partial(combine_kernel, carried=bool(received), sums=bool(totals)),
        grid=(micros,),
        in_specs=[packed] * len(received) + [half] * 2 + [lanes] * len(totals),
        out_specs=[packed, packed],
        out_shape=[seq_shape(micros, sent, SW)] * 2,
        compiler_params=params(16),
        name="combine",
        cost_estimate=pl.CostEstimate(flops=2_000_000, bytes_accessed=7_000_000, transcendentals=0),
    )(*received, *parts, *totals)


def finish_kernel(acc_a, acc_b, pa, pb, ta, tb, x, weight, gain, mixed, low, total, middle, normed):
    for side, (acc, part, own) in enumerate(((acc_a, pa, ta), (acc_b, pb, tb))):
        lanes = unpack_lanes(acc[0, ROWS:]) + own[0]
        total[0, side] = lanes
        columns = to_columns(lanes)
        for h in range(SIDE):
            cols = slice(h * HEAD_DIM, (h + 1) * HEAD_DIM)
            place = slice((side * SIDE + h) * HEAD_DIM, (side * SIDE + h + 1) * HEAD_DIM)
            weighted = acc[0, :ROWS, cols].astype(F32) + part[0, :, cols].astype(F32)
            value = weighted / columns[:, h : h + 1]
            mixed[0, :, place] = value
            low[0, :, place] = value.astype(BF16)
    value = x[0].astype(F32) + nn(low[0], weight[...])
    middle[0] = value
    scale = lax.rsqrt(jnp.mean(value * value, axis=-1, keepdims=True) + EPS)
    normed[0] = (value * scale * gain[...]).astype(BF16)


def finish(acc_a, acc_b, pa, pb, ta, tb, x, weight, gain):
    micros = acc_a.shape[0]
    packed, half, lanes = seq_spec(SENT, SW), seq_spec(ROWS, SW), seq_spec(8, ROWS)
    whole = seq_spec(ROWS, D)
    return pl.pallas_call(
        finish_kernel,
        grid=(micros,),
        in_specs=[packed, packed, half, half, lanes, lanes, whole, full_spec(D, D), full_spec(1, D)],
        out_specs=[whole, whole, seq_spec(2, 8, ROWS), whole, whole],
        out_shape=[
            seq_shape(micros, ROWS, D, dtype=F32),
            seq_shape(micros, ROWS, D),
            seq_shape(micros, 2, 8, ROWS, dtype=F32),
            seq_shape(micros, ROWS, D, dtype=F32),
            seq_shape(micros, ROWS, D),
        ],
        compiler_params=params(),
        name="finish",
        cost_estimate=pl.CostEstimate(flops=2 * micros * ROWS * D * D, bytes_accessed=16_000_000, transcendentals=0),
    )(acc_a, acc_b, pa, pb, ta, tb, x, weight, gain)


TILE = 256


def feed_kernel(
    normed, incoming, middle, gate_weight, up_weight, down_weight, out, back, dg, du, dd, turned, acc, hid, bg, bu
):
    step = pl.program_id(0)
    micros = normed.shape[0]

    @pl.when(step == 0)
    def _():
        for m in range(micros):
            turned[:, m * ROWS : (m + 1) * ROWS] = normed[m].T
            acc[m] = middle[m]
            back[m] = jnp.zeros((ROWS, D), F32)

    wg, wu, wd = gate_weight[...], up_weight[...], down_weight[...]
    for m in range(micros):
        rows = slice(m * ROWS, (m + 1) * ROWS)
        gate = nn(normed[m], wg)
        upper = nn(normed[m], wu)
        slope = nt(incoming[m], wd)
        sigma = 1.0 / (1.0 + jnp.exp(-gate))
        silu = gate * sigma
        hid[rows] = (silu * upper).astype(BF16)
        bg[rows] = (slope * upper * (sigma * (1.0 + gate * (1.0 - sigma)))).astype(BF16)
        bu[rows] = (slope * silu).astype(BF16)
        acc[m] += nn(hid[rows], wd)
        back[m] += nt(bg[rows], wg) + nt(bu[rows], wu)
    dg[...] = nn(turned[...], bg[...]).astype(BF16)
    du[...] = nn(turned[...], bu[...]).astype(BF16)
    dd[...] = tn(hid[...], incoming[...].reshape(micros * ROWS, D)).astype(BF16)

    @pl.when(step == pl.num_programs(0) - 1)
    def _():
        out[...] = acc[...].astype(BF16)


def feed(normed, incoming, middle, gate_weight, up_weight, down_weight):
    micros = normed.shape[0]
    units = gate_weight.shape[1]
    whole = full_spec(micros, ROWS, D)
    wide = pl.BlockSpec((D, TILE), lambda f: (0, f))
    tall = pl.BlockSpec((TILE, D), lambda f: (f, 0))
    return pl.pallas_call(
        feed_kernel,
        grid=(units // TILE,),
        in_specs=[whole, whole, whole, wide, wide, tall],
        out_specs=[whole, whole, wide, wide, tall],
        out_shape=[
            seq_shape(micros, ROWS, D),
            seq_shape(micros, ROWS, D, dtype=F32),
            jax.ShapeDtypeStruct((D, units), BF16),
            jax.ShapeDtypeStruct((D, units), BF16),
            jax.ShapeDtypeStruct((units, D), BF16),
        ],
        scratch_shapes=[
            pltpu.VMEM((D, micros * ROWS), BF16),
            pltpu.VMEM((micros, ROWS, D), F32),
            pltpu.VMEM((micros * ROWS, TILE), BF16),
            pltpu.VMEM((micros * ROWS, TILE), BF16),
            pltpu.VMEM((micros * ROWS, TILE), BF16),
        ],
        compiler_params=params(),
        name="feed",
        cost_estimate=pl.CostEstimate(
            flops=18 * micros * ROWS * D * units, bytes_accessed=50_000_000, transcendentals=0
        ),
    )(normed, incoming, middle, gate_weight, up_weight, down_weight)


def prepare_kernel(back_normed, middle, incoming, gain, weight, mixed, total, da, db, back_middle, back_attn, dgain):
    value = middle[0]
    scale = lax.rsqrt(jnp.mean(value * value, axis=-1, keepdims=True) + EPS)
    hat = value * scale
    slope = back_normed[0] * gain[...]
    slope = incoming[0].astype(F32) + scale * (
        slope - hat * jnp.mean(slope * hat, axis=-1, keepdims=True)
    )
    back_middle[0] = slope
    back_attn[0] = slope.astype(BF16)
    dgain[0] = jnp.sum((back_normed[0] * hat).reshape(ROWS // 8, 8, D), axis=0)
    lane = lax.broadcasted_iota(jnp.int32, (ROWS, HEAD_DIM), 1)
    for side, out in enumerate((da, db)):
        columns = to_columns(total[0, side])
        packed = jnp.zeros((ROWS, HEAD_DIM), F32)
        back = nt(back_attn[0], weight[side * SW : (side + 1) * SW, :])
        for h in range(SIDE):
            cols = slice(h * HEAD_DIM, (h + 1) * HEAD_DIM)
            place = slice((side * SIDE + h) * HEAD_DIM, (side * SIDE + h + 1) * HEAD_DIM)
            part = back[:, cols]
            divisor = columns[:, h : h + 1]
            out[0, :ROWS, cols] = (part / divisor).astype(BF16)
            product = jnp.sum(part * mixed[0, :, place], axis=1, keepdims=True)
            packed = jnp.where(lane == h, -product / divisor, packed)
        out[0, ROWS:] = pack_lanes(packed.T[:8])


def prepare(back_normed, middle, incoming, gain, weight, mixed, total):
    micros = middle.shape[0]
    whole = seq_spec(ROWS, D)
    return pl.pallas_call(
        prepare_kernel,
        grid=(micros,),
        in_specs=[whole, whole, whole, full_spec(1, D), full_spec(D, D), whole, seq_spec(2, 8, ROWS)],
        out_specs=[seq_spec(SENT, SW), seq_spec(SENT, SW), whole, whole, seq_spec(8, D)],
        out_shape=[
            seq_shape(micros, SENT, SW),
            seq_shape(micros, SENT, SW),
            seq_shape(micros, ROWS, D, dtype=F32),
            seq_shape(micros, ROWS, D),
            seq_shape(micros, 8, D, dtype=F32),
        ],
        compiler_params=params(),
        name="prepare",
        cost_estimate=pl.CostEstimate(flops=2 * micros * ROWS * D * D, bytes_accessed=22_000_000, transcendentals=0),
    )(back_normed, middle, incoming, gain, weight, mixed, total)


def backward_kernel(
    meta, qa, qb, da, db, k, v, mk, mv, dqa, dqb, part, wide, kbuf, vbuf, sem, *, step, count, cap, micros
):
    micro = pl.program_id(0)
    here = meta[0]
    fetch = functools.partial(
        requests, meta, mk, mv, kbuf, vbuf, sem, step=step, count=count, cap=cap, micros=micros
    )
    request_ahead(fetch, micro, micros)
    for side, (q, d) in enumerate(((qa, da), (qb, db))):
        owner = meta[1 + 2 * step + side]
        columns = to_columns(unpack_lanes(d[0, ROWS:]))
        for h, (_, place) in enumerate(tiles(side)):
            wide[:, place] = jnp.broadcast_to(columns[:, h : h + 1], (ROWS, HEAD_DIM))

        def local(qrows, krows, masked):
            spots = tiles(side)
            scores = [nt(q[0, qrows, cols], k[0, krows, kcols]) for cols, kcols in spots]
            slopes = [nt(d[0, qrows, cols], v[0, krows, kcols]) for cols, kcols in spots]
            weights = [jnp.exp2(score * (SCALE * LOG2E)) for score in scores]
            if masked:
                weights = [jnp.where(causal_mask(), weight, 0.0) for weight in weights]
            slopes = [
                (weight * (slope + wide[qrows, kcols][:, :1])).astype(BF16)
                for weight, slope, (_, kcols) in zip(weights, slopes, spots)
            ]
            for slope, (_, kcols) in zip(slopes, spots):
                part[qrows, kcols] = nn(slope, k[0, krows, kcols])

        if step == 0:
            local(EVERYTHING, EVERYTHING, True)
        else:

            @pl.when(owner < here)
            def _():
                part[LOW, side * SW : (side + 1) * SW] = jnp.zeros((HALF, SW), F32)
                local(HIGH, EVERYTHING, False)

            @pl.when(owner > here)
            def _():
                local(EVERYTHING, LOW, False)

    fetch(micro, "wait")
    slot = micro % 2
    for side, (q, d, out) in enumerate(((qa, da, dqa), (qb, db, dqb))):
        owner = meta[1 + 2 * step + side]
        base = list_base(count) + list_at(owner, micro, side, micros, cap)
        length = meta[base]

        def group(i, carry):
            numbers = [i * GROUP + j for j in range(GROUP)]
            places = [request_place(meta[base + 1 + number]) for number in numbers]
            shifted = [
                (rows, pl.ds(pl.multiple_of(cols.start + side * SW, HEAD_DIM), HEAD_DIM))
                for rows, cols in places
            ]
            scores = [
                nt(q[0, rows, cols], kbuf[slot, side, number])
                for number, (rows, cols) in zip(numbers, places)
            ]
            slopes = [
                nt(d[0, rows, cols], vbuf[slot, side, number])
                for number, (rows, cols) in zip(numbers, places)
            ]
            weights = [jnp.exp2(score * (SCALE * LOG2E)) for score in scores]
            slopes = [
                jnp.where(
                    number < length, weight * (slope + wide[rows, cols][:, :BLOCK]), 0.0
                ).astype(BF16)
                for number, weight, slope, (rows, cols) in zip(numbers, weights, slopes, shifted)
            ]
            outs = [nn(slope, kbuf[slot, side, number]) for number, slope in zip(numbers, slopes)]
            for o, (rows, cols) in zip(outs, shifted):
                part[rows, cols] += o
            return carry

        lax.fori_loop(0, (length + GROUP - 1) // GROUP, group, 0)
        out[0] = part[:, side * SW : (side + 1) * SW].astype(BF16)


def unattend(meta, qa, qb, da, db, keys, values, memory_keys, memory_values, step, count, cap):
    micros = qa.shape[0]
    half, packed, whole = seq_spec(ROWS, SW), seq_spec(SENT, SW), seq_spec(ROWS, D)
    anywhere = pl.BlockSpec(memory_space=pl.ANY)
    return pl.pallas_call(
        functools.partial(backward_kernel, step=step, count=count, cap=cap, micros=micros),
        grid_spec=pltpu.PrefetchScalarGridSpec(
            num_scalar_prefetch=1,
            grid=(micros,),
            in_specs=[half, half, packed, packed, whole, whole, anywhere, anywhere],
            out_specs=[half, half],
            scratch_shapes=[pltpu.VMEM((ROWS, D), F32), pltpu.VMEM((ROWS, D), F32)]
            + request_scratch(cap),
        ),
        out_shape=[seq_shape(micros, ROWS, SW), seq_shape(micros, ROWS, SW)],
        compiler_params=params(24),
        name="unattend",
        cost_estimate=pl.CostEstimate(flops=8_000_000_000, bytes_accessed=12_000_000, transcendentals=0),
    )(meta, qa, qb, da, db, keys, values, memory_keys, memory_values)


def key_kernel(meta, k, v, *refs, steps, micros, last):
    number = len(steps)
    sources, refs = refs[: 4 * number], refs[4 * number :]
    if last:
        dk_first, dv_first, cosine, sine, back_key, back_value, dk, dv, qbuf, dbuf, sem = refs
    else:
        dk, dv, qbuf, dbuf, sem = refs
    micro = pl.program_id(0)
    here = meta[0]

    def fetch(m, act):
        slot = m % 2
        for i in range(number):
            for side in range(2):
                for source, place in (
                    (sources[4 * i + side], qbuf.at[slot, side, i]),
                    (sources[4 * i + 2 + side], dbuf.at[slot, side, i]),
                ):
                    copy = pltpu.make_async_copy(source.at[m], place, sem.at[slot])
                    if act == "start":
                        copy.start()
                    else:
                        copy.wait()

    request_ahead(fetch, micro, micros)
    fetch(micro, "wait")
    dk[0] = dk_first[0] if last else jnp.zeros((ROWS, D), F32)
    dv[0] = dv_first[0] if last else jnp.zeros((ROWS, D), F32)
    slot = micro % 2
    for side in range(2):
        spots = tiles(side)

        def one(i, step, own):
            q, d = qbuf.at[slot, side, i], dbuf.at[slot, side, i]
            shift = unpack_lanes(d[ROWS:, :])

            def local(qrows, krows, masked):
                scores = [nt(k[0, krows, kcols], q[qrows, cols]) for cols, kcols in spots]
                slopes = [nt(v[0, krows, kcols], d[qrows, cols]) for cols, kcols in spots]
                weights = [jnp.exp2(score * (SCALE * LOG2E)) for score in scores]
                if masked:
                    weights = [jnp.where(causal_mask(True), weight, 0.0) for weight in weights]
                slopes = [
                    (weight * (slope + shift[h : h + 1, qrows])).astype(BF16)
                    for h, (weight, slope) in enumerate(zip(weights, slopes))
                ]
                for weight, slope, (cols, kcols) in zip(weights, slopes, spots):
                    dk[0, krows, kcols] += nn(slope, q[qrows, cols])
                    dv[0, krows, kcols] += nn(weight.astype(BF16), d[qrows, cols])

            if own:
                local(EVERYTHING, EVERYTHING, True)
                return
            owner = meta[1 + 2 * step + side]

            @pl.when(owner < here)
            def _():
                local(HIGH, EVERYTHING, False)

            @pl.when(owner > here)
            def _():
                local(EVERYTHING, LOW, False)

        first = 0
        if steps[0] == 0:
            one(0, 0, True)
            first = 1

        def loop(i, carry):
            one(i, steps[0] + i, False)
            return carry

        lax.fori_loop(first, number, loop, 0)
    if last:
        for h in range(HEADS):
            cols = slice(h * HEAD_DIM, (h + 1) * HEAD_DIM)
            back_key[0, :, cols] = turn(dk[0, :, cols] * SCALE, cosine[...], -sine[...]).astype(BF16)
        back_value[0] = dv[0].astype(BF16)


def key_gradients(meta, keys, values, queries, slopes, steps, first=(), angle=()):
    micros = keys.shape[0]
    whole = seq_spec(ROWS, D)
    anywhere = pl.BlockSpec(memory_space=pl.ANY)
    sources = []
    for step in steps:
        sources += [*queries[step], *slopes[step]]
    last = bool(first)
    sum_scratch = [pltpu.VMEM((1, ROWS, D), F32)] * 2 if last else []
    return pl.pallas_call(
        functools.partial(key_kernel, steps=steps, micros=micros, last=last),
        grid_spec=pltpu.PrefetchScalarGridSpec(
            num_scalar_prefetch=1,
            grid=(micros,),
            in_specs=[whole, whole]
            + [anywhere] * len(sources)
            + [whole] * len(first)
            + [full_spec(ROWS, HEAD_DIM)] * len(angle),
            out_specs=[whole, whole],
            scratch_shapes=sum_scratch
            + [
                pltpu.VMEM((2, 2, len(steps), ROWS, SW), BF16),
                pltpu.VMEM((2, 2, len(steps), SENT, SW), BF16),
                pltpu.SemaphoreType.DMA((2,)),
            ],
        ),
        out_shape=[seq_shape(micros, ROWS, D, dtype=BF16 if last else F32)] * 2,
        compiler_params=params(40),
        name="key_gradients",
        cost_estimate=pl.CostEstimate(
            flops=3_000_000_000 * len(steps), bytes_accessed=20_000_000, transcendentals=0
        ),
    )(meta, keys, values, *sources, *first, *angle)


def bits(size):
    return [1 << i for i in range(size.bit_length() - 1)]


def by_rows(rows, chunks):
    return rows % (16 * chunks) == 0


PIECE = 512


def tail_kernel(
    acc_a,
    acc_b,
    part_a,
    part_b,
    cosine,
    sine,
    gain,
    second,
    *rest,
    count,
    shards,
    parts,
):
    early_far, rest = rest[:parts], rest[parts:]
    tail_work(
        acc_a, acc_b, part_a, part_b, cosine, sine, gain, second, early_far, *rest, count=count, shards=shards
    )


def tail_work(
    acc_a,
    acc_b,
    part_a,
    part_b,
    cosine,
    sine,
    gain,
    second,
    early_far,
    back_key_far,
    back_value_far,
    turned_far,
    query_far,
    pairs_far,
    x_far,
    middle_far,
    early_out,
    late_out,
    gains_out,
    input_out,
    *scratch,
    count,
    shards,
):
    scratch = list(scratch)
    halves = [scratch.pop(0) for _ in bits(shards)]
    (
        back_query,
        back_key,
        back_value,
        turned,
        weight,
        x,
        middle,
        early,
        given,
        early_slots,
        late_slots,
        gain_in,
        gain_sum,
        ring_send,
        ring_recv,
        half_send,
        half_recv,
        gain_send,
        gain_recv,
        near,
    ) = scratch
    micros = x.shape[0]
    chunks = 2 * count
    shard_rows = D // shards
    here, shard = lax.axis_index("ctx"), lax.axis_index("fsdp")
    place = ring_place(count)
    neighbour = (ring_index(place + 1, count), ring_index(place + count - 1, count))
    partners = [("fsdp", shard, bit) for bit in bits(shards)] + [("ctx", here, bit) for bit in bits(count)]

    copies = {}
    column = 0
    pieces = []
    for i, part in enumerate(early_far):
        pieces.append((f"early{i}", part, early.at[:, :, column : column + part.shape[2]]))
        column += part.shape[2]
    for number, (name, source, target) in enumerate(
        (
            *pieces,
            ("turned", turned_far, turned),
            ("back_key", back_key_far, back_key),
            ("back_value", back_value_far, back_value),
            ("query", query_far, weight.at[0]),
            ("pairs", pairs_far, weight.at[1:]),
            ("x", x_far, x),
            ("middle", middle_far, middle),
        )
    ):
        copies[name] = pltpu.make_async_copy(source, target, near.at[number])
        copies[name].start()

    def partner(axis, index, bit):
        return {axis: index + bit * (1 - 2 * ((index // bit) % 2))}

    barrier = pltpu.get_barrier_semaphore()
    known = [{"ctx": neighbour[0]}, {"ctx": neighbour[1]}] + [partner(*p) for p in partners]
    for device in known:
        pl.semaphore_signal(barrier, inc=1, device_id=device, device_id_type=pl.DeviceIdType.MESH)
    pl.semaphore_wait(barrier, len(known))

    sent = []

    def send(source, target, send_sem, recv_sem, device):
        copy = pltpu.make_async_remote_copy(
            source, target, send_sem, recv_sem, device_id=device, device_id_type=pl.DeviceIdType.MESH
        )
        copy.start()
        sent.append(copy)
        return copy

    def flow(number, first_source, source, slots, out):
        def home(side, hop):
            sign = 1 - 2 * side
            return side * count + (place - sign * hop + 2 * count) % count

        def start(hop):
            result = []
            for side in range(2):
                if hop == 1:
                    pair = first_source(home(side, 1)), slots(side, 0)
                elif hop < count:
                    pair = slots(side, hop - 2), slots(side, hop - 1)
                else:
                    chunk = home(side, hop - count)
                    pair = out(chunk), out(chunk)
                result.append(
                    send(
                        *pair,
                        ring_send.at[number, side, hop - 1],
                        ring_recv.at[number, side, hop - 1],
                        {"ctx": neighbour[side]},
                    )
                )
            return result

        def finish(hop, pending):
            for side in range(2):
                pending[side].wait_recv()
                if hop < count:
                    got = slots(side, hop - 1)
                    total = got[...].astype(F32) + source(home(side, 1 + hop))[...].astype(F32)
                    target = out(home(side, 0)) if hop == count - 1 else got
                    target[...] = total.astype(BF16)

        return start, finish

    class Run:
        def __init__(self, *arguments):
            self.start, self.finish = flow(*arguments)
            self.hop, self.pending = 0, None

        def advance(self):
            if self.hop:
                self.finish(self.hop, self.pending)
            self.hop += 1
            if self.hop <= 2 * count - 2:
                self.pending = self.start(self.hop)

        def done(self):
            return self.hop > 2 * count - 2

    width = early.shape[2]
    middle_column = width // HEAD_DIM // 2 * HEAD_DIM
    runs = []
    for number, cols in enumerate((slice(0, middle_column), slice(middle_column, width))):
        runs.append(
            Run(
                number,
                lambda c, cols=cols: early.at[c, :, cols],
                lambda c, cols=cols: early.at[c, :, cols],
                lambda side, slot, cols=cols: early_slots.at[side, slot, :, cols],
                lambda c, cols=cols: early_out.at[c, :, cols],
            )
        )

    sources = (back_query, back_key, back_value)

    def product(s, target, add):
        rows = turned[pl.ds(pl.multiple_of(s * shard_rows, shard_rows), shard_rows), :]
        for start in range(0, 3 * D, PIECE):
            column = start % D
            right = sources[start // D][:, :, column : column + PIECE].reshape(micros * ROWS, PIECE)
            value = nn(rows, right)
            if by_rows(shard_rows, chunks):
                value = value.reshape(chunks, shard_rows // chunks, PIECE)
                spots = [((slice(None), slice(None), slice(start, start + PIECE)), value)]
            else:
                step = target.shape[2]
                spots = [
                    (((start + c) // step,), value[:, c : c + step]) for c in range(0, PIECE, step)
                ]
            for spot, piece in spots:
                if add:
                    piece = target[spot].astype(F32) + piece.astype(BF16).astype(F32)
                target[spot] = piece.astype(BF16)

    if not by_rows(shard_rows, chunks):
        used = 3 * D // halves[0].shape[3]
        for c in range(used, chunks):
            given[:, c] = jnp.zeros_like(given[:, c])

    def bit_of(i):
        return (shard // (1 << i)) % 2

    def give(j):
        product(2 * j + 1 - bit_of(0), given.at[j], False)
        return send(
            given.at[j], halves[0].at[j], half_send.at[0, j], half_recv.at[0, j], partner("fsdp", shard, 1)
        )

    def halve_start(i):
        return [
            send(
                halves[i - 1].at[2 * j + 1 - bit_of(i)],
                halves[i].at[j],
                half_send.at[i, j],
                half_recv.at[i, j],
                partner("fsdp", shard, 1 << i),
            )
            for j in range(shards >> (i + 1))
        ]

    def halve_finish(i, j, copy):
        copy.wait_recv()
        if i == 0:
            product(2 * j + bit_of(0), halves[0].at[j], True)
            return

        def add(c, carry):
            halves[i][j, c] = (
                halves[i][j, c].astype(F32) + halves[i - 1][2 * j + bit_of(i), c].astype(F32)
            ).astype(BF16)
            return carry

        lax.fori_loop(0, chunks, add, 0)

    def unturn():
        for m in range(micros):
            for h in range(HEADS):
                acc, part = (acc_a, part_a) if h < SIDE else (acc_b, part_b)
                cols = slice(h % SIDE * HEAD_DIM, (h % SIDE + 1) * HEAD_DIM)
                value = (acc[m, :, cols].astype(F32) + part[m, :, cols].astype(F32)) * SCALE
                back_query[m, :, h * HEAD_DIM : (h + 1) * HEAD_DIM] = turn(
                    value, cosine[...], -sine[...]
                ).astype(BF16)

    def input_back(m):
        slope = nt(back_query[m], weight[0]) + nt(back_key[m], weight[1]) + nt(back_value[m], weight[2])
        value = x[m].astype(F32)
        scale = lax.rsqrt(jnp.mean(value * value, axis=-1, keepdims=True) + EPS)
        hat = value * scale
        first = jnp.sum((slope * hat).reshape(ROWS // 8, 8, D), axis=0)
        slope = slope * gain[...]
        input_out[m] = middle[m] + scale * (slope - hat * jnp.mean(slope * hat, axis=-1, keepdims=True))
        gain_sum[1] = first if m == 0 else gain_sum[1] + first

    def gains_ready():
        first = jnp.sum(gain_sum[1], axis=0, keepdims=True)
        other = jnp.sum(jnp.sum(second[...], axis=0), axis=0, keepdims=True)
        gain_sum[0] = jnp.concatenate([first, other, jnp.zeros((6, D), F32)], axis=0)

    def gain_start(i):
        return send(gain_sum.at[i], gain_in.at[i], gain_send.at[i], gain_recv.at[i], partner(*partners[i]))

    def gain_finish(i, copy):
        copy.wait_recv()
        gain_sum[i + 1] = gain_sum[i] + gain_in[i]

    stages = len(halves)
    late = []

    def advance():
        for run in runs:
            for each in (run, *late):
                if not each.done():
                    each.advance()

    for i in range(len(early_far)):
        copies[f"early{i}"].wait()
    advance()
    unturn()
    for name in ("turned", "back_key", "back_value"):
        copies[name].wait()
    half = []
    for j in range(shards // 2):
        half.append(give(j))
        advance()
    for j in range(shards // 2):
        halve_finish(0, j, half[j])
        advance()
    for i in range(1, stages):
        half = halve_start(i)
        if i < stages - 1:
            for j, copy in enumerate(half):
                halve_finish(i, j, copy)
            advance()
    for name in ("query", "pairs", "x", "middle"):
        copies[name].wait()
    for m in range(micros):
        input_back(m)
        advance()
    gains_ready()
    for i in range(len(partners)):
        copy = gain_start(i)
        advance()
        if i == 0:
            if stages > 1:
                halve_finish(stages - 1, 0, half[0])
            late.append(
                Run(
                    2,
                    lambda c: halves[-1].at[0, c],
                    lambda c: halves[-1].at[0, c],
                    lambda side, slot: late_slots.at[side, slot],
                    lambda c: late_out.at[c],
                )
            )
        gain_finish(i, copy)
    while not all(run.done() for run in runs + late):
        advance()
    gains_out[...] = gain_sum[len(partners)]
    for copy in sent:
        copy.wait_send()


def tail(received, own, angle, gain, second, early, back_key, back_value, turned, weights, x, middle, count, shards):
    micros = x.shape[0]
    chunks = 2 * count
    shard_rows = D // shards
    if by_rows(shard_rows, chunks):
        late = (chunks, shard_rows // chunks, 3 * D)
    else:
        late = (chunks, shard_rows, -(-3 * D // (chunks * HEAD_DIM)) * HEAD_DIM)
    exchanges = len(bits(shards)) + len(bits(count))
    early_shape = early[0].shape[:2] + (sum(part.shape[2] for part in early),)
    vmem = pl.BlockSpec(memory_space=pltpu.VMEM)
    anywhere = pl.BlockSpec(memory_space=pl.ANY)
    return pl.pallas_call(
        functools.partial(tail_kernel, count=count, shards=shards, parts=len(early)),
        in_specs=[vmem] * 8 + [anywhere] * (7 + len(early)),
        out_specs=[vmem] * 4,
        out_shape=[
            jax.ShapeDtypeStruct(early_shape, BF16),
            jax.ShapeDtypeStruct(late, BF16),
            jax.ShapeDtypeStruct((8, D), F32),
            seq_shape(micros, ROWS, D, dtype=F32),
        ],
        scratch_shapes=[pltpu.VMEM((shards // (2 * bit),) + late, BF16) for bit in bits(shards)]
        + [pltpu.VMEM((micros, ROWS, D), BF16)] * 3
        + [
            pltpu.VMEM(turned.shape, BF16),
            pltpu.VMEM((3, D, D), BF16),
            pltpu.VMEM((micros, ROWS, D), BF16),
            pltpu.VMEM((micros, ROWS, D), F32),
            pltpu.VMEM(early_shape, BF16),
            pltpu.VMEM((shards // 2,) + late, BF16),
            pltpu.VMEM((2, count - 1) + early_shape[1:], BF16),
            pltpu.VMEM((2, count - 1) + late[1:], BF16),
            pltpu.VMEM((exchanges, 8, D), F32),
            pltpu.VMEM((exchanges + 1, 8, D), F32),
            pltpu.SemaphoreType.DMA((3, 2, 2 * count - 2)),
            pltpu.SemaphoreType.DMA((3, 2, 2 * count - 2)),
            pltpu.SemaphoreType.DMA((len(bits(shards)), shards // 2)),
            pltpu.SemaphoreType.DMA((len(bits(shards)), shards // 2)),
            pltpu.SemaphoreType.DMA((exchanges,)),
            pltpu.SemaphoreType.DMA((exchanges,)),
            pltpu.SemaphoreType.DMA((7 + len(early),)),
        ],
        compiler_params=pltpu.CompilerParams(
            vmem_limit_bytes=60 * 2**20, collective_id=0, has_side_effects=True
        ),
        name="tail",
        cost_estimate=pl.CostEstimate(flops=12_000_000_000, bytes_accessed=300_000_000, transcendentals=0),
    )(
        *received,
        *own,
        *angle,
        gain,
        second,
        *early,
        back_key,
        back_value,
        turned,
        *weights,
        x,
        middle,
    )


def to_chunks(parts, count):
    rows = parts[0].shape[0]
    chunks = 2 * count
    if by_rows(rows, chunks):
        return [part.reshape(chunks, rows // chunks, -1) for part in parts]
    value = jnp.concatenate(parts, axis=1)
    width = value.shape[1]
    step = -(-width // (chunks * HEAD_DIM)) * HEAD_DIM
    value = jnp.pad(value, [(0, 0), (0, step * chunks - width)])
    return [jnp.moveaxis(value.reshape(rows, chunks, step), 1, 0)]


def from_chunks(value, rows, width):
    if by_rows(rows, value.shape[0]):
        return value.reshape(rows, width)
    return jnp.moveaxis(value, 0, 1).reshape(rows, -1)[:, :width]


def body(
    tokens,
    cotangent,
    query_weight,
    key_weight,
    value_weight,
    output_weight,
    gate_weight,
    up_weight,
    down_weight,
    first_gain,
    second_gain,
    cache_keys,
    cache_values,
    block_indices,
    partner,
):
    count = lax.axis_size("ctx")
    here = lax.axis_index("ctx")
    micros = tokens.shape[0]
    rows = micros * ROWS
    onward, backward = ring_pairs(count)

    def gather(value):
        return lax.all_gather(value, "fsdp", axis=0, tiled=True)

    shards = lax.axis_size("fsdp")
    requested = block_indices.reshape(micros, -1)
    own_rows = D // shards
    indices, gains = share(
        jnp.pad(requested, ((0, -micros % 8), (0, 0))),
        jnp.pad(
            jnp.stack([first_gain, second_gain]).astype(F32), ((0, 6), (0, -own_rows % HEAD_DIM))
        ),
        count,
        shards,
    )
    indices = jnp.moveaxis(indices[:, :micros], 0, 1)
    gains = jnp.moveaxis(gains[:, :2, :own_rows], 0, 1).reshape(2, D)
    full_query = gather(query_weight)
    pair_weights = lax.all_gather(jnp.stack([key_weight, value_weight]), "fsdp", axis=1, tiled=True)
    full_output = gather(output_weight)
    full_gate = gather(gate_weight)
    full_up = gather(up_weight)
    full_down = gather(down_weight)
    gain_one = gains[0:1]
    gain_two = gains[1:2]

    pieces_at = jnp.stack([here, 2 * count - 1 - here])
    positions = (pieces_at[:, None] * HALF + jnp.arange(HALF, dtype=jnp.int32)[None, :]).reshape(ROWS)
    inverse = 10000.0 ** (-jnp.arange(HEAD_DIM // 2, dtype=F32) * 2.0 / HEAD_DIM)
    phase = positions.astype(F32)[:, None] * inverse[None, :]
    cosine = jnp.tile(jnp.cos(phase), (1, 2))
    sine = jnp.sin(phase)
    sine = jnp.concatenate([-sine, sine], axis=1)

    meta, cap = make_meta(indices, partner, cache_keys.shape[1] // BLOCK, count)
    x = tokens.reshape(micros, ROWS, D)
    normed_low, qa, qb = project_query(x, gain_one, full_query, cosine, sine)
    meta, qa, qb = lax.optimization_barrier((meta, qa, qb))
    queries = [(qa, qb)]
    for _ in range(count - 1):
        qa, qb = lax.ppermute(qa, "ctx", onward), lax.ppermute(qb, "ctx", backward)
        queries.append((qa, qb))
    memory_keys, memory_values = collect(meta, cache_keys, cache_values, count, cap)
    queries[1], normed_low, memory_keys = lax.optimization_barrier((queries[1], normed_low, memory_keys))
    keys, values, normed_turned = project_pairs(normed_low, pair_weights, cosine, sine)
    for step in range(1, count - 1):
        queries[step], queries[step + 1] = lax.optimization_barrier((queries[step], queries[step + 1]))


    acc = ()
    for step in list(range(1, count)) + [0]:
        pa, pb, ta, tb = attend(
            meta, *queries[step], keys, values, memory_keys, memory_values, step, count, cap
        )
        if acc:
            acc = (lax.ppermute(acc[0], "ctx", onward), lax.ppermute(acc[1], "ctx", backward))
        if step == 0:
            mixed, mixed_low, total, middle, middle_low = finish(
                *acc, pa, pb, ta, tb, x, full_output, gain_two
            )
        else:
            acc = combine(acc, (pa, pb), (ta, tb))

    incoming = cotangent.reshape(micros, ROWS, D)
    layer_output, back_mid_normed, gradient_gate, gradient_up, gradient_down = feed(
        middle_low, incoming, middle, full_gate, full_up, full_down
    )
    da, db, back_middle, back_attn, gain_part = prepare(
        back_mid_normed, middle, incoming, gain_two, full_output, mixed, total
    )

    def scatter(part):
        return lax.psum_scatter(part, "fsdp", scatter_dimension=0, tiled=True)

    slopes = [(da, db)]
    for _ in range(count - 1):
        da, db = slopes[-1]
        slopes.append((lax.ppermute(da, "ctx", onward), lax.ppermute(db, "ctx", backward)))

    slopes[1], back_attn = lax.optimization_barrier((slopes[1], back_attn))
    gradient_output = jnp.einsum(
        "tc,td->cd", mixed_low.reshape(rows, D), back_attn.reshape(rows, D), preferred_element_type=F32
    ).astype(BF16)
    early = [
        scatter(part).reshape(own_rows, -1)
        for part in (gradient_down, gradient_gate, gradient_up, gradient_output)
    ]
    early_width = sum(part.shape[1] for part in early)
    for step in range(1, count - 1):
        slopes[step], slopes[step + 1] = lax.optimization_barrier((slopes[step], slopes[step + 1]))
    acc = ()
    for step in range(count):
        part = unattend(
            meta, *queries[step], *slopes[step], keys, values, memory_keys, memory_values, step, count, cap
        )
        if step == 0:
            own = part
            continue
        if acc:
            acc = (lax.ppermute(acc[0], "ctx", onward), lax.ppermute(acc[1], "ctx", backward))
        acc = combine(acc, part)
    middle_step = count // 2
    first_sums = key_gradients(meta, keys, values, queries, slopes, range(middle_step))
    back_key, back_value = key_gradients(
        meta, keys, values, queries, slopes, range(middle_step, count), first_sums, (cosine, sine)
    )
    ra, rb = lax.ppermute(acc[0], "ctx", onward), lax.ppermute(acc[1], "ctx", backward)
    early_sum, late_sum, gain_changes, input_gradient = tail(
        (ra, rb),
        own,
        (cosine, sine),
        gain_one,
        gain_part,
        to_chunks(early, count),
        back_key,
        back_value,
        normed_turned,
        (full_query, pair_weights),
        x,
        back_middle,
        count,
        shards,
    )
    early = from_chunks(early_sum, own_rows, early_width).astype(F32)
    three = from_chunks(late_sum, D // shards, 3 * D).astype(F32)
    units = gate_weight.shape[1]
    gain_changes = lax.dynamic_slice_in_dim(
        gain_changes, lax.axis_index("fsdp") * own_rows, own_rows, axis=1
    )
    return (
        layer_output.reshape(tokens.shape),
        input_gradient.reshape(tokens.shape),
        three[:, :D],
        three[:, D : 2 * D],
        three[:, 2 * D :],
        early[:, 3 * units :],
        early[:, units : 2 * units],
        early[:, 2 * units : 3 * units],
        early[:, :units].reshape(down_weight.shape),
        gain_changes[0],
        gain_changes[1],
    )


def solution(mesh):
    split = P("fsdp", "ctx", None, None, None)
    shard = P("fsdp", None)
    return jax.shard_map(
        body,
        mesh=mesh,
        in_specs=(
            split,
            split,
            *([shard] * 7),
            P("fsdp"),
            P("fsdp"),
            P("fsdp", "ctx", None),
            P("fsdp", "ctx", None),
            P("fsdp", "ctx", None, None, None, None),
            P("fsdp"),
        ),
        out_specs=(split, split, *([shard] * 7), P("fsdp"), P("fsdp")),
        check_vma=False,
    )
```

```python
import functools

import jax
import jax.numpy as jnp
from jax import lax
from jax.experimental import pallas as pl
from jax.experimental.pallas import tpu as pltpu
from jax.sharding import PartitionSpec as P

D = 1024
HEADS = 8
HEAD_DIM = 128
HALF = 128
ROWS = 2 * HALF
BLOCK = 64
TOPK = 4
SIDE = HEADS // 2
SW = SIDE * HEAD_DIM
GROUP = 8
EPS = 1e-05
SCALE = HEAD_DIM**-0.5
LOG2E = 1.4426950408889634
F32 = jnp.float32
BF16 = jnp.bfloat16
EXTRA = 16
SENT = ROWS + EXTRA


def nn(a, b):
    return lax.dot_general(a, b, (((1,), (0,)), ((), ())), preferred_element_type=F32)


def nt(a, b):
    return lax.dot_general(a, b, (((1,), (1,)), ((), ())), preferred_element_type=F32)


def tn(a, b):
    return lax.dot_general(a, b, (((0,), (0,)), ((), ())), preferred_element_type=F32)


def params(mib=56):
    return pltpu.CompilerParams(vmem_limit_bytes=mib * 2**20)


def ring_order(count):
    if count == 8:
        return [0, 2, 4, 6, 7, 5, 3, 1]
    half = count // 2
    return list(range(half)) + [count - 1 - i for i in range(count - half)]


def ring_place(count):
    here = lax.axis_index("ctx")
    half = count // 2
    if count == 8:
        turned = here % 2
        return (1 - turned) * (here // 2) + turned * (count - 1 - here // 2)
    turned = here // half
    return (1 - turned) * here + turned * (count - 1 + half - here)


def ring_index(place, count):
    half = count // 2
    place = place % count
    turned = place // half
    if count == 8:
        return (1 - turned) * 2 * place + turned * (2 * count - 1 - 2 * place)
    return (1 - turned) * place + turned * (count - 1 + half - place)


def ring_pairs(count):
    order = ring_order(count)
    onward = [(order[i], order[(i + 1) % count]) for i in range(count)]
    return onward, [(b, a) for a, b in onward]


def list_base(count):
    return 1 + 2 * count


def list_at(owner, micro, side, micros, cap):
    return ((owner * micros + micro) * 2 + side) * (cap + 1)


def make_meta(indices, partner, cb_dev, count):
    micros = indices.shape[0]
    here = lax.axis_index("ctx")
    order = ring_order(count)
    place = ring_place(count)
    steps = jnp.arange(count, dtype=jnp.int32)
    at = jnp.stack([(place - steps) % count, (place + steps) % count], axis=1)
    owners = sum(jnp.where(at == p, d, 0) for p, d in enumerate(order))
    blocks = cb_dev * count
    cap = 2 * 128 // count
    side_shape = (micros, count, 2 * ROWS // (2 * BLOCK), 2, SIDE, TOPK)
    index = indices.reshape(side_shape).transpose(1, 0, 3, 2, 4, 5)
    index = index.reshape(count, micros, 2, -1)
    number = index % blocks
    mine = (number // cb_dev) == here
    own = jnp.arange(micros, dtype=jnp.int32)[None, :, None, None]
    document = jnp.where(index < blocks, own, partner[None, :, None, None])
    entries = index.shape[-1]
    entry = jnp.arange(entries, dtype=jnp.int32)
    query_block = entry // (SIDE * TOPK)
    head = entry // TOPK % SIDE
    code = ((document * cb_dev + number % cb_dev) * 4 + query_block) * SIDE + head
    before = (entry[:, None] < entry[None, :]).astype(F32)
    flags = mine.astype(F32)
    rank = jnp.dot(flags.reshape(-1, entries), before, preferred_element_type=F32).reshape(flags.shape)
    rank = rank.astype(jnp.int32)
    slot = jnp.arange(cap, dtype=jnp.int32)
    hit = mine[..., None, :] & (rank[..., None, :] == slot[:, None])
    codes = jnp.sum(jnp.where(hit, code[..., None, :], 0), axis=-1)
    length = jnp.sum(mine.astype(jnp.int32), axis=-1, keepdims=True)
    lists = jnp.concatenate([length, codes], axis=-1).reshape(-1)
    return jnp.concatenate([here.reshape(1), owners.reshape(-1), lists]).astype(jnp.int32), cap


def share_kernel(indices, gains, all_indices, all_gains, send_sem, recv_sem, *, count, shards):
    here, shard = lax.axis_index("ctx"), lax.axis_index("fsdp")
    groups = (("ctx", here, count, indices, all_indices), ("fsdp", shard, shards, gains, all_gains))
    barrier = pltpu.get_barrier_semaphore()
    for axis, index, size, _, _ in groups:
        for k in range(1, size):
            pl.semaphore_signal(
                barrier, inc=1, device_id={axis: (index + k) % size}, device_id_type=pl.DeviceIdType.MESH
            )
    pl.semaphore_wait(barrier, count + shards - 2)
    copies = []
    for number, (axis, index, size, source, target) in enumerate(groups):
        for k in range(1, size):
            copy = pltpu.make_async_remote_copy(
                source,
                target.at[index],
                send_sem.at[number, k],
                recv_sem.at[number, k],
                device_id={axis: (index + k) % size},
                device_id_type=pl.DeviceIdType.MESH,
            )
            copy.start()
            copies.append(copy)
        target[index] = source[...]
    for copy in copies:
        copy.wait()


def share(indices, gains, count, shards):
    vmem = pl.BlockSpec(memory_space=pltpu.VMEM)
    most = max(count, shards)
    return pl.pallas_call(
        functools.partial(share_kernel, count=count, shards=shards),
        in_specs=[vmem, vmem],
        out_specs=[vmem, vmem],
        out_shape=[
            jax.ShapeDtypeStruct((count,) + indices.shape, indices.dtype),
            jax.ShapeDtypeStruct((shards,) + gains.shape, gains.dtype),
        ],
        scratch_shapes=[pltpu.SemaphoreType.DMA((2, most)), pltpu.SemaphoreType.DMA((2, most))],
        compiler_params=pltpu.CompilerParams(
            vmem_limit_bytes=8 * 2**20, collective_id=1, has_side_effects=True
        ),
        name="share",
        cost_estimate=pl.CostEstimate(flops=0, bytes_accessed=20_000_000, transcendentals=0),
    )(indices, gains)


def collect_kernel(meta, ck, cv, *refs, micros, count, cap, first):
    mk, mv, sem_k, sem_v = refs[-4:]
    owner = pl.program_id(0) + first

    def list_of(i):
        base = list_base(count) + (owner * 2 * micros + i) * (cap + 1)
        return base, meta[base]

    def start(i, carry):
        base, length = list_of(i)

        def one(j, c):
            code = meta[base + 1 + j]
            head = (i & 1) * SIDE + (code & (SIDE - 1))
            rows = pl.ds(pl.multiple_of((code >> 4) << 6, BLOCK), BLOCK)
            cols = pl.ds(pl.multiple_of(head << 7, HEAD_DIM), HEAD_DIM)
            pltpu.make_async_copy(ck.at[rows, cols], mk.at[i >> 1, 0, i & 1, j], sem_k).start()
            pltpu.make_async_copy(cv.at[rows, cols], mv.at[i >> 1, 0, i & 1, j], sem_v).start()
            return c

        def clear(j, c):
            mk[i >> 1, 0, i & 1, j] = jnp.zeros((BLOCK, HEAD_DIM), BF16)
            mv[i >> 1, 0, i & 1, j] = jnp.zeros((BLOCK, HEAD_DIM), BF16)
            return c

        lax.fori_loop(0, length, one, carry)
        return lax.fori_loop(length, (length + GROUP - 1) // GROUP * GROUP, clear, carry)

    def finish(i, carry):
        _, length = list_of(i)
        rounds = length // GROUP

        def many(g, c):
            some = pl.ds(g * GROUP, GROUP)
            for place, sem in ((mk, sem_k), (mv, sem_v)):
                whole = place.at[i >> 1, 0, i & 1, some]
                pltpu.make_async_copy(whole, whole, sem).wait()
            return c

        def one(j, c):
            for place, sem in ((mk, sem_k), (mv, sem_v)):
                whole = place.at[i >> 1, 0, i & 1, j]
                pltpu.make_async_copy(whole, whole, sem).wait()
            return c

        lax.fori_loop(0, rounds, many, carry)
        return lax.fori_loop(rounds * GROUP, length, one, carry)

    lax.fori_loop(0, 2 * micros, start, 0)
    lax.fori_loop(0, 2 * micros, finish, 0)


def collect(meta, cache_keys, cache_values, count, cap, owners, into=()):
    micros = cache_keys.shape[0]
    shape = jax.ShapeDtypeStruct((micros, count, 2, cap, BLOCK, HEAD_DIM), BF16)
    anywhere = pl.BlockSpec(memory_space=pl.ANY)
    block = pl.BlockSpec((micros, 1, 2, cap, BLOCK, HEAD_DIM), lambda o, meta: (0, o + owners.start, 0, 0, 0, 0))
    return pl.pallas_call(
        functools.partial(collect_kernel, micros=micros, count=count, cap=cap, first=owners.start),
        grid_spec=pltpu.PrefetchScalarGridSpec(
            num_scalar_prefetch=1,
            grid=(len(owners),),
            in_specs=[anywhere, anywhere] + [anywhere] * len(into),
            out_specs=[block, block],
            scratch_shapes=[pltpu.SemaphoreType.DMA, pltpu.SemaphoreType.DMA],
        ),
        out_shape=[shape, shape],
        input_output_aliases={3: 0, 4: 1} if into else {},
        compiler_params=params(),
        name="collect",
        cost_estimate=pl.CostEstimate(
            flops=0, bytes_accessed=11_000_000 * len(owners), transcendentals=0
        ),
    )(meta, cache_keys.reshape(-1, D), cache_values.reshape(-1, D), *into)


def turn(value, cosine, sine):
    return value * cosine + pltpu.roll(value, HEAD_DIM // 2, 1) * sine


def first_kernel(x, gain, weight, cosine, sine, normed, qa, qb):
    value = x[0].astype(F32)
    scale = lax.rsqrt(jnp.mean(value * value, axis=-1, keepdims=True) + EPS)
    low = (value * scale * gain[...]).astype(BF16)
    normed[0] = low
    product = nn(low, weight[...])
    for h in range(HEADS):
        cols = slice(h * HEAD_DIM, (h + 1) * HEAD_DIM)
        out = qa if h < SIDE else qb
        place = slice((h % SIDE) * HEAD_DIM, (h % SIDE + 1) * HEAD_DIM)
        out[0, :, place] = turn(product[:, cols], cosine[...], sine[...]).astype(BF16)


def second_kernel(normed, weights, cosine, sine, keys, values, turned):
    low = normed[0]
    turned[...] = low.T
    product = nn(low, weights[0])
    for h in range(HEADS):
        cols = slice(h * HEAD_DIM, (h + 1) * HEAD_DIM)
        keys[0, :, cols] = turn(product[:, cols], cosine[...], sine[...]).astype(BF16)
    values[0] = nn(low, weights[1]).astype(BF16)


def seq_spec(*shape):
    return pl.BlockSpec((1,) + shape, lambda m, *_: (m,) + (0,) * len(shape))


def full_spec(*shape):
    return pl.BlockSpec(shape, lambda m, *_: (0,) * len(shape))


def seq_shape(micros, *shape, dtype=BF16):
    return jax.ShapeDtypeStruct((micros,) + shape, dtype)


def project_query(x, gain, weight, cosine, sine):
    micros = x.shape[0]
    return pl.pallas_call(
        first_kernel,
        grid=(micros,),
        in_specs=[
            seq_spec(ROWS, D),
            full_spec(1, D),
            full_spec(D, D),
            full_spec(ROWS, HEAD_DIM),
            full_spec(ROWS, HEAD_DIM),
        ],
        out_specs=[seq_spec(ROWS, D), seq_spec(ROWS, SW), seq_spec(ROWS, SW)],
        out_shape=[seq_shape(micros, ROWS, D), seq_shape(micros, ROWS, SW), seq_shape(micros, ROWS, SW)],
        compiler_params=params(),
        name="project_query",
        cost_estimate=pl.CostEstimate(flops=2 * micros * ROWS * D * D, bytes_accessed=8_000_000, transcendentals=0),
    )(x, gain, weight, cosine, sine)


def project_pairs(normed, weights, cosine, sine):
    micros = normed.shape[0]
    return pl.pallas_call(
        second_kernel,
        grid=(micros,),
        in_specs=[
            seq_spec(ROWS, D),
            full_spec(2, D, D),
            full_spec(ROWS, HEAD_DIM),
            full_spec(ROWS, HEAD_DIM),
        ],
        out_specs=[seq_spec(ROWS, D), seq_spec(ROWS, D), pl.BlockSpec((D, ROWS), lambda m: (0, m))],
        out_shape=[
            seq_shape(micros, ROWS, D),
            seq_shape(micros, ROWS, D),
            jax.ShapeDtypeStruct((D, micros * ROWS), BF16),
        ],
        compiler_params=params(),
        name="project_pairs",
        cost_estimate=pl.CostEstimate(flops=4 * micros * ROWS * D * D, bytes_accessed=10_000_000, transcendentals=0),
    )(normed, weights, cosine, sine)


def causal_mask(turned=False):
    row = lax.broadcasted_iota(jnp.int32, (ROWS, ROWS), 0)
    col = lax.broadcasted_iota(jnp.int32, (ROWS, ROWS), 1)
    return row <= col if turned else row >= col


def to_lanes(wide):
    lane = lax.broadcasted_iota(jnp.int32, (ROWS, HEAD_DIM), 1)
    packed = jnp.zeros((ROWS, HEAD_DIM), F32)
    for h in range(SIDE):
        packed = jnp.where(lane == h, wide[:, h * HEAD_DIM : (h + 1) * HEAD_DIM], packed)
    return packed.T[:8]


def to_columns(lanes):
    return jnp.concatenate([lanes, jnp.zeros((HEAD_DIM - 8, ROWS), F32)], axis=0).T


def split3(value):
    high = value.astype(BF16).astype(F32)
    middle = (value - high).astype(BF16).astype(F32)
    return high, middle, value - high - middle


def pack_lanes(lanes):
    high, middle, low = split3(lanes)
    rows = jnp.concatenate(
        [jnp.concatenate([high, middle], axis=1), jnp.concatenate([low, jnp.zeros_like(low)], axis=1)],
        axis=0,
    )
    return rows.astype(BF16)


def unpack_lanes(rows):
    value = rows.astype(F32)
    return value[:8, :ROWS] + value[:8, ROWS:] + value[8:, :ROWS]


def requests(meta, mk, mv, kbuf, vbuf, sem, micro, act, *, step, count, cap, micros):
    slot = micro % 2
    for side in range(2):
        owner = meta[1 + 2 * step + side]
        length = meta[list_base(count) + list_at(owner, micro, side, micros, cap)]

        def one(g, carry):
            some = pl.ds(g * GROUP, GROUP)
            for source, place in ((mk, kbuf), (mv, vbuf)):
                copy = pltpu.make_async_copy(
                    source.at[micro, owner, side, some], place.at[slot, side, some], sem.at[slot]
                )
                if act == "start":
                    copy.start()
                else:
                    copy.wait()
            return carry

        lax.fori_loop(0, (length + GROUP - 1) // GROUP, one, 0)


def request_ahead(fetch, micro, micros):
    @pl.when(micro == 0)
    def _():
        fetch(micro, "start")

    @pl.when(micro + 1 < micros)
    def _():
        fetch(micro + 1, "start")


def request_scratch(cap):
    return [
        pltpu.VMEM((2, 2, cap, BLOCK, HEAD_DIM), BF16),
        pltpu.VMEM((2, 2, cap, BLOCK, HEAD_DIM), BF16),
        pltpu.SemaphoreType.DMA((2,)),
    ]


EVERYTHING, LOW, HIGH = slice(0, ROWS), slice(0, HALF), slice(HALF, ROWS)


def tiles(side):
    return [
        (
            slice(h * HEAD_DIM, (h + 1) * HEAD_DIM),
            slice((side * SIDE + h) * HEAD_DIM, (side * SIDE + h + 1) * HEAD_DIM),
        )
        for h in range(SIDE)
    ]


def forward_kernel(
    meta, qa, qb, k, v, mk, mv, pa, pb, ta, tb, part, wide, kbuf, vbuf, sem, *, step, count, cap, micros
):
    micro = pl.program_id(0)
    here = meta[0]
    fetch = functools.partial(
        requests, meta, mk, mv, kbuf, vbuf, sem, step=step, count=count, cap=cap, micros=micros
    )
    request_ahead(fetch, micro, micros)
    for side, q in enumerate((qa, qb)):
        owner = meta[1 + 2 * step + side]

        def local(qrows, krows, masked):
            spots = tiles(side)
            scores = [nt(q[0, qrows, cols], k[0, krows, kcols]) for cols, kcols in spots]
            weights = [jnp.exp2(score * (SCALE * LOG2E)) for score in scores]
            if masked:
                weights = [jnp.where(causal_mask(), weight, 0.0) for weight in weights]
            for weight, (cols, kcols) in zip(weights, spots):
                values = v[0, krows, kcols]
                more = jnp.concatenate([values, jnp.ones_like(values)], axis=1)
                out = nn(weight.astype(BF16), more)
                part[qrows, kcols] = out[:, :HEAD_DIM]
                wide[qrows, kcols] = out[:, HEAD_DIM:]

        if step == 0:
            local(EVERYTHING, EVERYTHING, True)
        else:

            @pl.when(owner < here)
            def _():
                zeros = jnp.zeros((HALF, SW), F32)
                part[LOW, side * SW : (side + 1) * SW] = zeros
                wide[LOW, side * SW : (side + 1) * SW] = zeros
                local(HIGH, EVERYTHING, False)

            @pl.when(owner > here)
            def _():
                local(EVERYTHING, LOW, False)

    fetch(micro, "wait")
    slot = micro % 2
    for side, (q, out, total) in enumerate(((qa, pa, ta), (qb, pb, tb))):
        owner = meta[1 + 2 * step + side]
        base = list_base(count) + list_at(owner, micro, side, micros, cap)
        length = meta[base]

        def group(i, carry):
            numbers = [i * GROUP + j for j in range(GROUP)]
            places = [request_place(meta[base + 1 + number]) for number in numbers]
            scores = [
                nt(q[0, rows, cols], kbuf[slot, side, number])
                for number, (rows, cols) in zip(numbers, places)
            ]
            weights = [
                jnp.where(number < length, jnp.exp2(score * (SCALE * LOG2E)), 0.0).astype(BF16)
                for number, score in zip(numbers, scores)
            ]
            outs = []
            for number, weight in zip(numbers, weights):
                values = vbuf[slot, side, number]
                outs.append(nn(weight, jnp.concatenate([values, jnp.ones_like(values)], axis=1)))
            for o, (rows, cols) in zip(outs, places):
                cols = pl.ds(pl.multiple_of(cols.start + side * SW, HEAD_DIM), HEAD_DIM)
                part[rows, cols] += o[:, :HEAD_DIM]
                wide[rows, cols] += o[:, HEAD_DIM:]
            return carry

        lax.fori_loop(0, (length + GROUP - 1) // GROUP, group, 0)
        out[0] = part[:, side * SW : (side + 1) * SW].astype(BF16)
        total[0] = to_lanes(wide[:, side * SW : (side + 1) * SW])


def request_place(code):
    return (
        pl.ds(pl.multiple_of(((code >> 2) & 3) << 6, BLOCK), BLOCK),
        pl.ds(pl.multiple_of((code & 3) << 7, HEAD_DIM), HEAD_DIM),
    )


def attend(meta, qa, qb, keys, values, memory_keys, memory_values, step, count, cap):
    micros = qa.shape[0]
    half, whole, lanes = seq_spec(ROWS, SW), seq_spec(ROWS, D), seq_spec(8, ROWS)
    anywhere = pl.BlockSpec(memory_space=pl.ANY)
    return pl.pallas_call(
        functools.partial(forward_kernel, step=step, count=count, cap=cap, micros=micros),
        grid_spec=pltpu.PrefetchScalarGridSpec(
            num_scalar_prefetch=1,
            grid=(micros,),
            in_specs=[half, half, whole, whole, anywhere, anywhere],
            out_specs=[half, half, lanes, lanes],
            scratch_shapes=[pltpu.VMEM((ROWS, D), F32), pltpu.VMEM((ROWS, D), F32)]
            + request_scratch(cap),
        ),
        out_shape=[
            seq_shape(micros, ROWS, SW),
            seq_shape(micros, ROWS, SW),
            seq_shape(micros, 8, ROWS, dtype=F32),
            seq_shape(micros, 8, ROWS, dtype=F32),
        ],
        compiler_params=params(24),
        name="attend",
        cost_estimate=pl.CostEstimate(flops=6_000_000_000, bytes_accessed=10_000_000, transcendentals=0),
    )(meta, qa, qb, keys, values, memory_keys, memory_values)


def combine_kernel(*refs, carried, sums):
    refs = list(refs)
    received = [refs.pop(0), refs.pop(0)] if carried else [None, None]
    parts = [refs.pop(0), refs.pop(0)]
    totals = [refs.pop(0), refs.pop(0)] if sums else [None, None]
    for got, part, total, out in zip(received, parts, totals, refs):
        value = part[0].astype(F32)
        if carried:
            value = value + got[0, :ROWS].astype(F32)
        out[0, :ROWS] = value.astype(BF16)
        if sums:
            lanes = total[0]
            if carried:
                lanes = lanes + unpack_lanes(got[0, ROWS:])
            out[0, ROWS:] = pack_lanes(lanes)


def combine(received, parts, totals=()):
    micros = parts[0].shape[0]
    sent = SENT if totals else ROWS
    half, lanes, packed = seq_spec(ROWS, SW), seq_spec(8, ROWS), seq_spec(sent, SW)
    return pl.pallas_call(
        functools.partial(combine_kernel, carried=bool(received), sums=bool(totals)),
        grid=(micros,),
        in_specs=[packed] * len(received) + [half] * 2 + [lanes] * len(totals),
        out_specs=[packed, packed],
        out_shape=[seq_shape(micros, sent, SW)] * 2,
        compiler_params=params(16),
        name="combine",
        cost_estimate=pl.CostEstimate(flops=2_000_000, bytes_accessed=7_000_000, transcendentals=0),
    )(*received, *parts, *totals)


def finish_kernel(acc_a, acc_b, pa, pb, ta, tb, x, weight, gain, mixed, low, total, middle, normed):
    for side, (acc, part, own) in enumerate(((acc_a, pa, ta), (acc_b, pb, tb))):
        lanes = unpack_lanes(acc[0, ROWS:]) + own[0]
        total[0, side] = lanes
        columns = to_columns(lanes)
        for h in range(SIDE):
            cols = slice(h * HEAD_DIM, (h + 1) * HEAD_DIM)
            place = slice((side * SIDE + h) * HEAD_DIM, (side * SIDE + h + 1) * HEAD_DIM)
            weighted = acc[0, :ROWS, cols].astype(F32) + part[0, :, cols].astype(F32)
            value = weighted / columns[:, h : h + 1]
            mixed[0, :, place] = value
            low[0, :, place] = value.astype(BF16)
    value = x[0].astype(F32) + nn(low[0], weight[...])
    middle[0] = value
    scale = lax.rsqrt(jnp.mean(value * value, axis=-1, keepdims=True) + EPS)
    normed[0] = (value * scale * gain[...]).astype(BF16)


def finish(acc_a, acc_b, pa, pb, ta, tb, x, weight, gain):
    micros = acc_a.shape[0]
    packed, half, lanes = seq_spec(SENT, SW), seq_spec(ROWS, SW), seq_spec(8, ROWS)
    whole = seq_spec(ROWS, D)
    return pl.pallas_call(
        finish_kernel,
        grid=(micros,),
        in_specs=[packed, packed, half, half, lanes, lanes, whole, full_spec(D, D), full_spec(1, D)],
        out_specs=[whole, whole, seq_spec(2, 8, ROWS), whole, whole],
        out_shape=[
            seq_shape(micros, ROWS, D, dtype=F32),
            seq_shape(micros, ROWS, D),
            seq_shape(micros, 2, 8, ROWS, dtype=F32),
            seq_shape(micros, ROWS, D, dtype=F32),
            seq_shape(micros, ROWS, D),
        ],
        compiler_params=params(),
        name="finish",
        cost_estimate=pl.CostEstimate(flops=2 * micros * ROWS * D * D, bytes_accessed=16_000_000, transcendentals=0),
    )(acc_a, acc_b, pa, pb, ta, tb, x, weight, gain)


TILE = 256


def feed_kernel(
    normed, incoming, middle, gate_weight, up_weight, down_weight, out, back, dg, du, dd, turned, acc, hid, bg, bu
):
    step = pl.program_id(0)
    micros = normed.shape[0]

    @pl.when(step == 0)
    def _():
        for m in range(micros):
            turned[:, m * ROWS : (m + 1) * ROWS] = normed[m].T
            acc[m] = middle[m]
            back[m] = jnp.zeros((ROWS, D), F32)

    wg, wu, wd = gate_weight[...], up_weight[...], down_weight[...]
    for m in range(micros):
        rows = slice(m * ROWS, (m + 1) * ROWS)
        gate = nn(normed[m], wg)
        upper = nn(normed[m], wu)
        slope = nt(incoming[m], wd)
        sigma = 1.0 / (1.0 + jnp.exp(-gate))
        silu = gate * sigma
        hid[rows] = (silu * upper).astype(BF16)
        bg[rows] = (slope * upper * (sigma * (1.0 + gate * (1.0 - sigma)))).astype(BF16)
        bu[rows] = (slope * silu).astype(BF16)
        acc[m] += nn(hid[rows], wd)
        back[m] += nt(bg[rows], wg) + nt(bu[rows], wu)
    dg[...] = nn(turned[...], bg[...]).astype(BF16)
    du[...] = nn(turned[...], bu[...]).astype(BF16)
    dd[...] = tn(hid[...], incoming[...].reshape(micros * ROWS, D)).astype(BF16)

    @pl.when(step == pl.num_programs(0) - 1)
    def _():
        out[...] = acc[...].astype(BF16)


def feed(normed, incoming, middle, gate_weight, up_weight, down_weight):
    micros = normed.shape[0]
    units = gate_weight.shape[1]
    whole = full_spec(micros, ROWS, D)
    wide = pl.BlockSpec((D, TILE), lambda f: (0, f))
    tall = pl.BlockSpec((TILE, D), lambda f: (f, 0))
    return pl.pallas_call(
        feed_kernel,
        grid=(units // TILE,),
        in_specs=[whole, whole, whole, wide, wide, tall],
        out_specs=[whole, whole, wide, wide, tall],
        out_shape=[
            seq_shape(micros, ROWS, D),
            seq_shape(micros, ROWS, D, dtype=F32),
            jax.ShapeDtypeStruct((D, units), BF16),
            jax.ShapeDtypeStruct((D, units), BF16),
            jax.ShapeDtypeStruct((units, D), BF16),
        ],
        scratch_shapes=[
            pltpu.VMEM((D, micros * ROWS), BF16),
            pltpu.VMEM((micros, ROWS, D), F32),
            pltpu.VMEM((micros * ROWS, TILE), BF16),
            pltpu.VMEM((micros * ROWS, TILE), BF16),
            pltpu.VMEM((micros * ROWS, TILE), BF16),
        ],
        compiler_params=params(),
        name="feed",
        cost_estimate=pl.CostEstimate(
            flops=18 * micros * ROWS * D * units, bytes_accessed=50_000_000, transcendentals=0
        ),
    )(normed, incoming, middle, gate_weight, up_weight, down_weight)


def prepare_kernel(back_normed, middle, incoming, gain, weight, mixed, total, da, db, back_middle, back_attn, dgain):
    value = middle[0]
    scale = lax.rsqrt(jnp.mean(value * value, axis=-1, keepdims=True) + EPS)
    hat = value * scale
    slope = back_normed[0] * gain[...]
    slope = incoming[0].astype(F32) + scale * (
        slope - hat * jnp.mean(slope * hat, axis=-1, keepdims=True)
    )
    back_middle[0] = slope
    back_attn[0] = slope.astype(BF16)
    dgain[0] = jnp.sum((back_normed[0] * hat).reshape(ROWS // 8, 8, D), axis=0)
    lane = lax.broadcasted_iota(jnp.int32, (ROWS, HEAD_DIM), 1)
    for side, out in enumerate((da, db)):
        columns = to_columns(total[0, side])
        packed = jnp.zeros((ROWS, HEAD_DIM), F32)
        back = nt(back_attn[0], weight[side * SW : (side + 1) * SW, :])
        for h in range(SIDE):
            cols = slice(h * HEAD_DIM, (h + 1) * HEAD_DIM)
            place = slice((side * SIDE + h) * HEAD_DIM, (side * SIDE + h + 1) * HEAD_DIM)
            part = back[:, cols]
            divisor = columns[:, h : h + 1]
            out[0, :ROWS, cols] = (part / divisor).astype(BF16)
            product = jnp.sum(part * mixed[0, :, place], axis=1, keepdims=True)
            packed = jnp.where(lane == h, -product / divisor, packed)
        out[0, ROWS:] = pack_lanes(packed.T[:8])


def prepare(back_normed, middle, incoming, gain, weight, mixed, total):
    micros = middle.shape[0]
    whole = seq_spec(ROWS, D)
    return pl.pallas_call(
        prepare_kernel,
        grid=(micros,),
        in_specs=[whole, whole, whole, full_spec(1, D), full_spec(D, D), whole, seq_spec(2, 8, ROWS)],
        out_specs=[seq_spec(SENT, SW), seq_spec(SENT, SW), whole, whole, seq_spec(8, D)],
        out_shape=[
            seq_shape(micros, SENT, SW),
            seq_shape(micros, SENT, SW),
            seq_shape(micros, ROWS, D, dtype=F32),
            seq_shape(micros, ROWS, D),
            seq_shape(micros, 8, D, dtype=F32),
        ],
        compiler_params=params(),
        name="prepare",
        cost_estimate=pl.CostEstimate(flops=2 * micros * ROWS * D * D, bytes_accessed=22_000_000, transcendentals=0),
    )(back_normed, middle, incoming, gain, weight, mixed, total)


def backward_kernel(
    meta, qa, qb, da, db, k, v, mk, mv, dqa, dqb, part, wide, kbuf, vbuf, sem, *, step, count, cap, micros
):
    micro = pl.program_id(0)
    here = meta[0]
    fetch = functools.partial(
        requests, meta, mk, mv, kbuf, vbuf, sem, step=step, count=count, cap=cap, micros=micros
    )
    request_ahead(fetch, micro, micros)
    for side, (q, d) in enumerate(((qa, da), (qb, db))):
        owner = meta[1 + 2 * step + side]
        columns = to_columns(unpack_lanes(d[0, ROWS:]))
        for h, (_, place) in enumerate(tiles(side)):
            wide[:, place] = jnp.broadcast_to(columns[:, h : h + 1], (ROWS, HEAD_DIM))

        def local(qrows, krows, masked):
            spots = tiles(side)
            scores = [nt(q[0, qrows, cols], k[0, krows, kcols]) for cols, kcols in spots]
            slopes = [nt(d[0, qrows, cols], v[0, krows, kcols]) for cols, kcols in spots]
            weights = [jnp.exp2(score * (SCALE * LOG2E)) for score in scores]
            if masked:
                weights = [jnp.where(causal_mask(), weight, 0.0) for weight in weights]
            slopes = [
                (weight * (slope + wide[qrows, kcols][:, :1])).astype(BF16)
                for weight, slope, (_, kcols) in zip(weights, slopes, spots)
            ]
            for slope, (_, kcols) in zip(slopes, spots):
                part[qrows, kcols] = nn(slope, k[0, krows, kcols])

        if step == 0:
            local(EVERYTHING, EVERYTHING, True)
        else:

            @pl.when(owner < here)
            def _():
                part[LOW, side * SW : (side + 1) * SW] = jnp.zeros((HALF, SW), F32)
                local(HIGH, EVERYTHING, False)

            @pl.when(owner > here)
            def _():
                local(EVERYTHING, LOW, False)

    fetch(micro, "wait")
    slot = micro % 2
    for side, (q, d, out) in enumerate(((qa, da, dqa), (qb, db, dqb))):
        owner = meta[1 + 2 * step + side]
        base = list_base(count) + list_at(owner, micro, side, micros, cap)
        length = meta[base]

        def group(i, carry):
            numbers = [i * GROUP + j for j in range(GROUP)]
            places = [request_place(meta[base + 1 + number]) for number in numbers]
            shifted = [
                (rows, pl.ds(pl.multiple_of(cols.start + side * SW, HEAD_DIM), HEAD_DIM))
                for rows, cols in places
            ]
            scores = [
                nt(q[0, rows, cols], kbuf[slot, side, number])
                for number, (rows, cols) in zip(numbers, places)
            ]
            slopes = [
                nt(d[0, rows, cols], vbuf[slot, side, number])
                for number, (rows, cols) in zip(numbers, places)
            ]
            weights = [jnp.exp2(score * (SCALE * LOG2E)) for score in scores]
            slopes = [
                jnp.where(
                    number < length, weight * (slope + wide[rows, cols][:, :BLOCK]), 0.0
                ).astype(BF16)
                for number, weight, slope, (rows, cols) in zip(numbers, weights, slopes, shifted)
            ]
            outs = [nn(slope, kbuf[slot, side, number]) for number, slope in zip(numbers, slopes)]
            for o, (rows, cols) in zip(outs, shifted):
                part[rows, cols] += o
            return carry

        lax.fori_loop(0, (length + GROUP - 1) // GROUP, group, 0)
        out[0] = part[:, side * SW : (side + 1) * SW].astype(BF16)


def unattend(meta, qa, qb, da, db, keys, values, memory_keys, memory_values, step, count, cap):
    micros = qa.shape[0]
    half, packed, whole = seq_spec(ROWS, SW), seq_spec(SENT, SW), seq_spec(ROWS, D)
    anywhere = pl.BlockSpec(memory_space=pl.ANY)
    return pl.pallas_call(
        functools.partial(backward_kernel, step=step, count=count, cap=cap, micros=micros),
        grid_spec=pltpu.PrefetchScalarGridSpec(
            num_scalar_prefetch=1,
            grid=(micros,),
            in_specs=[half, half, packed, packed, whole, whole, anywhere, anywhere],
            out_specs=[half, half],
            scratch_shapes=[pltpu.VMEM((ROWS, D), F32), pltpu.VMEM((ROWS, D), F32)]
            + request_scratch(cap),
        ),
        out_shape=[seq_shape(micros, ROWS, SW), seq_shape(micros, ROWS, SW)],
        compiler_params=params(24),
        name="unattend",
        cost_estimate=pl.CostEstimate(flops=8_000_000_000, bytes_accessed=12_000_000, transcendentals=0),
    )(meta, qa, qb, da, db, keys, values, memory_keys, memory_values)


def key_kernel(meta, k, v, *refs, steps, micros, last):
    number = len(steps)
    sources, refs = refs[: 4 * number], refs[4 * number :]
    if last:
        dk_first, dv_first, cosine, sine, back_key, back_value, dk, dv, qbuf, dbuf, sem = refs
    else:
        dk, dv, qbuf, dbuf, sem = refs
    micro = pl.program_id(0)
    here = meta[0]

    def fetch(m, act):
        slot = m % 2
        for i in range(number):
            for side in range(2):
                for source, place in (
                    (sources[4 * i + side], qbuf.at[slot, side, i]),
                    (sources[4 * i + 2 + side], dbuf.at[slot, side, i]),
                ):
                    copy = pltpu.make_async_copy(source.at[m], place, sem.at[slot])
                    if act == "start":
                        copy.start()
                    else:
                        copy.wait()

    request_ahead(fetch, micro, micros)
    fetch(micro, "wait")
    dk[0] = dk_first[0] if last else jnp.zeros((ROWS, D), F32)
    dv[0] = dv_first[0] if last else jnp.zeros((ROWS, D), F32)
    slot = micro % 2
    for side in range(2):
        spots = tiles(side)

        def one(i, step, own):
            q, d = qbuf.at[slot, side, i], dbuf.at[slot, side, i]
            shift = unpack_lanes(d[ROWS:, :])

            def local(qrows, krows, masked):
                scores = [nt(k[0, krows, kcols], q[qrows, cols]) for cols, kcols in spots]
                slopes = [nt(v[0, krows, kcols], d[qrows, cols]) for cols, kcols in spots]
                weights = [jnp.exp2(score * (SCALE * LOG2E)) for score in scores]
                if masked:
                    weights = [jnp.where(causal_mask(True), weight, 0.0) for weight in weights]
                slopes = [
                    (weight * (slope + shift[h : h + 1, qrows])).astype(BF16)
                    for h, (weight, slope) in enumerate(zip(weights, slopes))
                ]
                for weight, slope, (cols, kcols) in zip(weights, slopes, spots):
                    dk[0, krows, kcols] += nn(slope, q[qrows, cols])
                    dv[0, krows, kcols] += nn(weight.astype(BF16), d[qrows, cols])

            if own:
                local(EVERYTHING, EVERYTHING, True)
                return
            owner = meta[1 + 2 * step + side]

            @pl.when(owner < here)
            def _():
                local(HIGH, EVERYTHING, False)

            @pl.when(owner > here)
            def _():
                local(EVERYTHING, LOW, False)

        first = 0
        if steps[0] == 0:
            one(0, 0, True)
            first = 1

        def loop(i, carry):
            one(i, steps[0] + i, False)
            return carry

        lax.fori_loop(first, number, loop, 0)
    if last:
        for h in range(HEADS):
            cols = slice(h * HEAD_DIM, (h + 1) * HEAD_DIM)
            back_key[0, :, cols] = turn(dk[0, :, cols] * SCALE, cosine[...], -sine[...]).astype(BF16)
        back_value[0] = dv[0].astype(BF16)


def key_gradients(meta, keys, values, queries, slopes, steps, first=(), angle=()):
    micros = keys.shape[0]
    whole = seq_spec(ROWS, D)
    anywhere = pl.BlockSpec(memory_space=pl.ANY)
    sources = []
    for step in steps:
        sources += [*queries[step], *slopes[step]]
    last = bool(first)
    sum_scratch = [pltpu.VMEM((1, ROWS, D), F32)] * 2 if last else []
    return pl.pallas_call(
        functools.partial(key_kernel, steps=steps, micros=micros, last=last),
        grid_spec=pltpu.PrefetchScalarGridSpec(
            num_scalar_prefetch=1,
            grid=(micros,),
            in_specs=[whole, whole]
            + [anywhere] * len(sources)
            + [whole] * len(first)
            + [full_spec(ROWS, HEAD_DIM)] * len(angle),
            out_specs=[whole, whole],
            scratch_shapes=sum_scratch
            + [
                pltpu.VMEM((2, 2, len(steps), ROWS, SW), BF16),
                pltpu.VMEM((2, 2, len(steps), SENT, SW), BF16),
                pltpu.SemaphoreType.DMA((2,)),
            ],
        ),
        out_shape=[seq_shape(micros, ROWS, D, dtype=BF16 if last else F32)] * 2,
        compiler_params=params(40),
        name="key_gradients",
        cost_estimate=pl.CostEstimate(
            flops=3_000_000_000 * len(steps), bytes_accessed=20_000_000, transcendentals=0
        ),
    )(meta, keys, values, *sources, *first, *angle)


def bits(size):
    return [1 << i for i in range(size.bit_length() - 1)]


def by_rows(rows, chunks):
    return rows % (16 * chunks) == 0


PIECE = 512


def tail_kernel(
    acc_a,
    acc_b,
    part_a,
    part_b,
    cosine,
    sine,
    gain,
    second,
    *rest,
    count,
    shards,
    parts,
):
    early_far, rest = rest[:parts], rest[parts:]
    tail_work(
        acc_a, acc_b, part_a, part_b, cosine, sine, gain, second, early_far, *rest, count=count, shards=shards
    )


def tail_work(
    acc_a,
    acc_b,
    part_a,
    part_b,
    cosine,
    sine,
    gain,
    second,
    early_far,
    back_key_far,
    back_value_far,
    turned_far,
    query_far,
    pairs_far,
    x_far,
    middle_far,
    early_out,
    late_out,
    gains_out,
    input_out,
    *scratch,
    count,
    shards,
):
    scratch = list(scratch)
    halves = [scratch.pop(0) for _ in bits(shards)]
    (
        back_query,
        back_key,
        back_value,
        turned,
        weight,
        x,
        middle,
        early,
        given,
        early_slots,
        late_slots,
        gain_in,
        gain_sum,
        ring_send,
        ring_recv,
        half_send,
        half_recv,
        gain_send,
        gain_recv,
        near,
    ) = scratch
    micros = x.shape[0]
    chunks = 2 * count
    shard_rows = D // shards
    here, shard = lax.axis_index("ctx"), lax.axis_index("fsdp")
    place = ring_place(count)
    neighbour = (ring_index(place + 1, count), ring_index(place + count - 1, count))
    partners = [("fsdp", shard, bit) for bit in bits(shards)] + [("ctx", here, bit) for bit in bits(count)]

    copies = {}
    column = 0
    pieces = []
    for i, part in enumerate(early_far):
        pieces.append((f"early{i}", part, early.at[:, :, column : column + part.shape[2]]))
        column += part.shape[2]
    for number, (name, source, target) in enumerate(
        (
            *pieces,
            ("turned", turned_far, turned),
            ("back_key", back_key_far, back_key),
            ("back_value", back_value_far, back_value),
            ("query", query_far, weight.at[0]),
            ("pairs", pairs_far, weight.at[1:]),
            ("x", x_far, x),
            ("middle", middle_far, middle),
        )
    ):
        copies[name] = pltpu.make_async_copy(source, target, near.at[number])
        copies[name].start()

    def partner(axis, index, bit):
        return {axis: index + bit * (1 - 2 * ((index // bit) % 2))}

    barrier = pltpu.get_barrier_semaphore()
    known = [{"ctx": neighbour[0]}, {"ctx": neighbour[1]}] + [partner(*p) for p in partners]
    for device in known:
        pl.semaphore_signal(barrier, inc=1, device_id=device, device_id_type=pl.DeviceIdType.MESH)
    pl.semaphore_wait(barrier, len(known))

    sent = []

    def send(source, target, send_sem, recv_sem, device):
        copy = pltpu.make_async_remote_copy(
            source, target, send_sem, recv_sem, device_id=device, device_id_type=pl.DeviceIdType.MESH
        )
        copy.start()
        sent.append(copy)
        return copy

    def flow(number, first_source, source, slots, out):
        def home(side, hop):
            sign = 1 - 2 * side
            return side * count + (place - sign * hop + 2 * count) % count

        def start(hop):
            result = []
            for side in range(2):
                if hop == 1:
                    pair = first_source(home(side, 1)), slots(side, 0)
                elif hop < count:
                    pair = slots(side, hop - 2), slots(side, hop - 1)
                else:
                    chunk = home(side, hop - count)
                    pair = out(chunk), out(chunk)
                result.append(
                    send(
                        *pair,
                        ring_send.at[number, side, hop - 1],
                        ring_recv.at[number, side, hop - 1],
                        {"ctx": neighbour[side]},
                    )
                )
            return result

        def finish(hop, pending):
            for side in range(2):
                pending[side].wait_recv()
                if hop < count:
                    got = slots(side, hop - 1)
                    total = got[...].astype(F32) + source(home(side, 1 + hop))[...].astype(F32)
                    target = out(home(side, 0)) if hop == count - 1 else got
                    target[...] = total.astype(BF16)

        return start, finish

    class Run:
        def __init__(self, *arguments):
            self.start, self.finish = flow(*arguments)
            self.hop, self.pending = 0, None

        def advance(self):
            if self.hop:
                self.finish(self.hop, self.pending)
            self.hop += 1
            if self.hop <= 2 * count - 2:
                self.pending = self.start(self.hop)

        def done(self):
            return self.hop > 2 * count - 2

    width = early.shape[2]
    middle_column = width // HEAD_DIM // 2 * HEAD_DIM
    runs = []
    for number, cols in enumerate((slice(0, middle_column), slice(middle_column, width))):
        runs.append(
            Run(
                number,
                lambda c, cols=cols: early.at[c, :, cols],
                lambda c, cols=cols: early.at[c, :, cols],
                lambda side, slot, cols=cols: early_slots.at[side, slot, :, cols],
                lambda c, cols=cols: early_out.at[c, :, cols],
            )
        )

    sources = (back_query, back_key, back_value)

    def product(s, target, add):
        rows = turned[pl.ds(pl.multiple_of(s * shard_rows, shard_rows), shard_rows), :]
        for start in range(0, 3 * D, PIECE):
            column = start % D
            right = sources[start // D][:, :, column : column + PIECE].reshape(micros * ROWS, PIECE)
            value = nn(rows, right)
            if by_rows(shard_rows, chunks):
                value = value.reshape(chunks, shard_rows // chunks, PIECE)
                spots = [((slice(None), slice(None), slice(start, start + PIECE)), value)]
            else:
                step = target.shape[2]
                spots = [
                    (((start + c) // step,), value[:, c : c + step]) for c in range(0, PIECE, step)
                ]
            for spot, piece in spots:
                if add:
                    piece = target[spot].astype(F32) + piece.astype(BF16).astype(F32)
                target[spot] = piece.astype(BF16)

    if not by_rows(shard_rows, chunks):
        used = 3 * D // halves[0].shape[3]
        for c in range(used, chunks):
            given[:, c] = jnp.zeros_like(given[:, c])

    def bit_of(i):
        return (shard // (1 << i)) % 2

    def give(j):
        product(2 * j + 1 - bit_of(0), given.at[j], False)
        return send(
            given.at[j], halves[0].at[j], half_send.at[0, j], half_recv.at[0, j], partner("fsdp", shard, 1)
        )

    def halve_start(i):
        return [
            send(
                halves[i - 1].at[2 * j + 1 - bit_of(i)],
                halves[i].at[j],
                half_send.at[i, j],
                half_recv.at[i, j],
                partner("fsdp", shard, 1 << i),
            )
            for j in range(shards >> (i + 1))
        ]

    def halve_finish(i, j, copy):
        copy.wait_recv()
        if i == 0:
            product(2 * j + bit_of(0), halves[0].at[j], True)
            return

        def add(c, carry):
            halves[i][j, c] = (
                halves[i][j, c].astype(F32) + halves[i - 1][2 * j + bit_of(i), c].astype(F32)
            ).astype(BF16)
            return carry

        lax.fori_loop(0, chunks, add, 0)

    def unturn():
        for m in range(micros):
            for h in range(HEADS):
                acc, part = (acc_a, part_a) if h < SIDE else (acc_b, part_b)
                cols = slice(h % SIDE * HEAD_DIM, (h % SIDE + 1) * HEAD_DIM)
                value = (acc[m, :, cols].astype(F32) + part[m, :, cols].astype(F32)) * SCALE
                back_query[m, :, h * HEAD_DIM : (h + 1) * HEAD_DIM] = turn(
                    value, cosine[...], -sine[...]
                ).astype(BF16)

    def input_back(m):
        slope = nt(back_query[m], weight[0]) + nt(back_key[m], weight[1]) + nt(back_value[m], weight[2])
        value = x[m].astype(F32)
        scale = lax.rsqrt(jnp.mean(value * value, axis=-1, keepdims=True) + EPS)
        hat = value * scale
        first = jnp.sum((slope * hat).reshape(ROWS // 8, 8, D), axis=0)
        slope = slope * gain[...]
        input_out[m] = middle[m] + scale * (slope - hat * jnp.mean(slope * hat, axis=-1, keepdims=True))
        gain_sum[1] = first if m == 0 else gain_sum[1] + first

    def gains_ready():
        first = jnp.sum(gain_sum[1], axis=0, keepdims=True)
        other = jnp.sum(jnp.sum(second[...], axis=0), axis=0, keepdims=True)
        gain_sum[0] = jnp.concatenate([first, other, jnp.zeros((6, D), F32)], axis=0)

    def gain_start(i):
        return send(gain_sum.at[i], gain_in.at[i], gain_send.at[i], gain_recv.at[i], partner(*partners[i]))

    def gain_finish(i, copy):
        copy.wait_recv()
        gain_sum[i + 1] = gain_sum[i] + gain_in[i]

    stages = len(halves)
    late = []

    def advance():
        for run in runs:
            for each in (run, *late):
                if not each.done():
                    each.advance()

    for i in range(len(early_far)):
        copies[f"early{i}"].wait()
    advance()
    unturn()
    for name in ("turned", "back_key", "back_value"):
        copies[name].wait()
    order = [list(range(shards // 2))]
    if stages > 1:
        order = [
            [2 * j + 1 - bit_of(1) for j in range(shards // 4)],
            [2 * j + bit_of(1) for j in range(shards // 4)],
        ]
    half = None
    for numbers in order:
        given_now = []
        for j in numbers:
            given_now.append(give(j))
            advance()
        for j, copy in zip(numbers, given_now):
            halve_finish(0, j, copy)
            advance()
        if half is None and stages > 1:
            half = halve_start(1)
    for i in range(1, stages - 1):
        for j, copy in enumerate(half):
            halve_finish(i, j, copy)
        half = halve_start(i + 1)
        advance()
    for name in ("query", "pairs", "x", "middle"):
        copies[name].wait()
    for m in range(micros):
        if m == micros - 1:
            if stages > 1:
                halve_finish(stages - 1, 0, half[0])
            late.append(
                Run(
                    2,
                    lambda c: halves[-1].at[0, c],
                    lambda c: halves[-1].at[0, c],
                    lambda side, slot: late_slots.at[side, slot],
                    lambda c: late_out.at[c],
                )
            )
            advance()
        input_back(m)
        advance()
    gains_ready()
    for i in range(len(partners)):
        copy = gain_start(i)
        advance()
        gain_finish(i, copy)
    while not all(run.done() for run in runs + late):
        advance()
    gains_out[...] = gain_sum[len(partners)]
    for copy in sent:
        copy.wait_send()


def tail(received, own, angle, gain, second, early, back_key, back_value, turned, weights, x, middle, count, shards):
    micros = x.shape[0]
    chunks = 2 * count
    shard_rows = D // shards
    if by_rows(shard_rows, chunks):
        late = (chunks, shard_rows // chunks, 3 * D)
    else:
        late = (chunks, shard_rows, -(-3 * D // (chunks * HEAD_DIM)) * HEAD_DIM)
    exchanges = len(bits(shards)) + len(bits(count))
    early_shape = early[0].shape[:2] + (sum(part.shape[2] for part in early),)
    vmem = pl.BlockSpec(memory_space=pltpu.VMEM)
    anywhere = pl.BlockSpec(memory_space=pl.ANY)
    return pl.pallas_call(
        functools.partial(tail_kernel, count=count, shards=shards, parts=len(early)),
        in_specs=[vmem] * 8 + [anywhere] * (7 + len(early)),
        out_specs=[vmem] * 4,
        out_shape=[
            jax.ShapeDtypeStruct(early_shape, BF16),
            jax.ShapeDtypeStruct(late, BF16),
            jax.ShapeDtypeStruct((8, D), F32),
            seq_shape(micros, ROWS, D, dtype=F32),
        ],
        scratch_shapes=[pltpu.VMEM((shards // (2 * bit),) + late, BF16) for bit in bits(shards)]
        + [pltpu.VMEM((micros, ROWS, D), BF16)] * 3
        + [
            pltpu.VMEM(turned.shape, BF16),
            pltpu.VMEM((3, D, D), BF16),
            pltpu.VMEM((micros, ROWS, D), BF16),
            pltpu.VMEM((micros, ROWS, D), F32),
            pltpu.VMEM(early_shape, BF16),
            pltpu.VMEM((shards // 2,) + late, BF16),
            pltpu.VMEM((2, count - 1) + early_shape[1:], BF16),
            pltpu.VMEM((2, count - 1) + late[1:], BF16),
            pltpu.VMEM((exchanges, 8, D), F32),
            pltpu.VMEM((exchanges + 1, 8, D), F32),
            pltpu.SemaphoreType.DMA((3, 2, 2 * count - 2)),
            pltpu.SemaphoreType.DMA((3, 2, 2 * count - 2)),
            pltpu.SemaphoreType.DMA((len(bits(shards)), shards // 2)),
            pltpu.SemaphoreType.DMA((len(bits(shards)), shards // 2)),
            pltpu.SemaphoreType.DMA((exchanges,)),
            pltpu.SemaphoreType.DMA((exchanges,)),
            pltpu.SemaphoreType.DMA((7 + len(early),)),
        ],
        compiler_params=pltpu.CompilerParams(
            vmem_limit_bytes=60 * 2**20, collective_id=0, has_side_effects=True
        ),
        name="tail",
        cost_estimate=pl.CostEstimate(flops=12_000_000_000, bytes_accessed=300_000_000, transcendentals=0),
    )(
        *received,
        *own,
        *angle,
        gain,
        second,
        *early,
        back_key,
        back_value,
        turned,
        *weights,
        x,
        middle,
    )


def to_chunks(parts, count):
    rows = parts[0].shape[0]
    chunks = 2 * count
    if by_rows(rows, chunks):
        return [part.reshape(chunks, rows // chunks, -1) for part in parts]
    value = jnp.concatenate(parts, axis=1)
    width = value.shape[1]
    step = -(-width // (chunks * HEAD_DIM)) * HEAD_DIM
    value = jnp.pad(value, [(0, 0), (0, step * chunks - width)])
    return [jnp.moveaxis(value.reshape(rows, chunks, step), 1, 0)]


def from_chunks(value, rows, width):
    if by_rows(rows, value.shape[0]):
        return value.reshape(rows, width)
    return jnp.moveaxis(value, 0, 1).reshape(rows, -1)[:, :width]


def body(
    tokens,
    cotangent,
    query_weight,
    key_weight,
    value_weight,
    output_weight,
    gate_weight,
    up_weight,
    down_weight,
    first_gain,
    second_gain,
    cache_keys,
    cache_values,
    block_indices,
    partner,
):
    count = lax.axis_size("ctx")
    here = lax.axis_index("ctx")
    micros = tokens.shape[0]
    rows = micros * ROWS
    onward, backward = ring_pairs(count)

    def gather(value):
        return lax.all_gather(value, "fsdp", axis=0, tiled=True)

    shards = lax.axis_size("fsdp")
    requested = block_indices.reshape(micros, -1)
    own_rows = D // shards
    indices, gains = share(
        jnp.pad(requested, ((0, -micros % 8), (0, 0))),
        jnp.pad(
            jnp.stack([first_gain, second_gain]).astype(F32), ((0, 6), (0, -own_rows % HEAD_DIM))
        ),
        count,
        shards,
    )
    indices = jnp.moveaxis(indices[:, :micros], 0, 1)
    gains = jnp.moveaxis(gains[:, :2, :own_rows], 0, 1).reshape(2, D)
    full_query = gather(query_weight)
    pair_weights = lax.all_gather(jnp.stack([key_weight, value_weight]), "fsdp", axis=1, tiled=True)
    full_output = gather(output_weight)
    full_gate = gather(gate_weight)
    full_up = gather(up_weight)
    full_down = gather(down_weight)
    gain_one = gains[0:1]
    gain_two = gains[1:2]

    pieces_at = jnp.stack([here, 2 * count - 1 - here])
    positions = (pieces_at[:, None] * HALF + jnp.arange(HALF, dtype=jnp.int32)[None, :]).reshape(ROWS)
    inverse = 10000.0 ** (-jnp.arange(HEAD_DIM // 2, dtype=F32) * 2.0 / HEAD_DIM)
    phase = positions.astype(F32)[:, None] * inverse[None, :]
    cosine = jnp.tile(jnp.cos(phase), (1, 2))
    sine = jnp.sin(phase)
    sine = jnp.concatenate([-sine, sine], axis=1)

    meta, cap = make_meta(indices, partner, cache_keys.shape[1] // BLOCK, count)
    x = tokens.reshape(micros, ROWS, D)
    some = count * 3 // 8
    memory = collect(meta, cache_keys, cache_values, count, cap, range(some))
    x, memory = lax.optimization_barrier((x, memory))
    normed_low, qa, qb = project_query(x, gain_one, full_query, cosine, sine)
    meta, qa, qb = lax.optimization_barrier((meta, qa, qb))
    queries = [(qa, qb)]
    for _ in range(count - 1):
        qa, qb = lax.ppermute(qa, "ctx", onward), lax.ppermute(qb, "ctx", backward)
        queries.append((qa, qb))
    memory_keys, memory_values = collect(
        meta, cache_keys, cache_values, count, cap, range(some, count), memory
    )
    queries[1], normed_low = lax.optimization_barrier((queries[1], normed_low))
    keys, values, normed_turned = project_pairs(normed_low, pair_weights, cosine, sine)
    for step in range(1, count - 1):
        queries[step], queries[step + 1] = lax.optimization_barrier((queries[step], queries[step + 1]))


    acc = ()
    for step in list(range(1, count)) + [0]:
        pa, pb, ta, tb = attend(
            meta, *queries[step], keys, values, memory_keys, memory_values, step, count, cap
        )
        if acc:
            acc = (lax.ppermute(acc[0], "ctx", onward), lax.ppermute(acc[1], "ctx", backward))
        if step == 0:
            mixed, mixed_low, total, middle, middle_low = finish(
                *acc, pa, pb, ta, tb, x, full_output, gain_two
            )
        else:
            acc = combine(acc, (pa, pb), (ta, tb))

    incoming = cotangent.reshape(micros, ROWS, D)
    layer_output, back_mid_normed, gradient_gate, gradient_up, gradient_down = feed(
        middle_low, incoming, middle, full_gate, full_up, full_down
    )
    da, db, back_middle, back_attn, gain_part = prepare(
        back_mid_normed, middle, incoming, gain_two, full_output, mixed, total
    )

    def scatter(part):
        return lax.psum_scatter(part, "fsdp", scatter_dimension=0, tiled=True)

    slopes = [(da, db)]
    for _ in range(count - 1):
        da, db = slopes[-1]
        slopes.append((lax.ppermute(da, "ctx", onward), lax.ppermute(db, "ctx", backward)))

    slopes[1], back_attn = lax.optimization_barrier((slopes[1], back_attn))
    gradient_output = jnp.einsum(
        "tc,td->cd", mixed_low.reshape(rows, D), back_attn.reshape(rows, D), preferred_element_type=F32
    ).astype(BF16)
    early = [
        scatter(part).reshape(own_rows, -1)
        for part in (gradient_down, gradient_gate, gradient_up, gradient_output)
    ]
    early_width = sum(part.shape[1] for part in early)
    for step in range(1, count - 1):
        slopes[step], slopes[step + 1] = lax.optimization_barrier((slopes[step], slopes[step + 1]))
    middle_step = count // 2 + 1
    first_sums = key_gradients(meta, keys, values, queries, slopes, range(middle_step))
    slopes[middle_step - 2], first_sums = lax.optimization_barrier((slopes[middle_step - 2], first_sums))
    acc = ()
    for step in range(count):
        part = unattend(
            meta, *queries[step], *slopes[step], keys, values, memory_keys, memory_values, step, count, cap
        )
        if step == 0:
            own = part
            continue
        if acc:
            acc = (lax.ppermute(acc[0], "ctx", onward), lax.ppermute(acc[1], "ctx", backward))
        acc = combine(acc, part)
    back_key, back_value = key_gradients(
        meta, keys, values, queries, slopes, range(middle_step, count), first_sums, (cosine, sine)
    )
    ra, rb = lax.ppermute(acc[0], "ctx", onward), lax.ppermute(acc[1], "ctx", backward)
    early_sum, late_sum, gain_changes, input_gradient = tail(
        (ra, rb),
        own,
        (cosine, sine),
        gain_one,
        gain_part,
        to_chunks(early, count),
        back_key,
        back_value,
        normed_turned,
        (full_query, pair_weights),
        x,
        back_middle,
        count,
        shards,
    )
    early = from_chunks(early_sum, own_rows, early_width).astype(F32)
    three = from_chunks(late_sum, D // shards, 3 * D).astype(F32)
    units = gate_weight.shape[1]
    gain_changes = lax.dynamic_slice_in_dim(
        gain_changes, lax.axis_index("fsdp") * own_rows, own_rows, axis=1
    )
    return (
        layer_output.reshape(tokens.shape),
        input_gradient.reshape(tokens.shape),
        three[:, :D],
        three[:, D : 2 * D],
        three[:, 2 * D :],
        early[:, 3 * units :],
        early[:, units : 2 * units],
        early[:, 2 * units : 3 * units],
        early[:, :units].reshape(down_weight.shape),
        gain_changes[0],
        gain_changes[1],
    )


def solution(mesh):
    split = P("fsdp", "ctx", None, None, None)
    shard = P("fsdp", None)
    return jax.shard_map(
        body,
        mesh=mesh,
        in_specs=(
            split,
            split,
            *([shard] * 7),
            P("fsdp"),
            P("fsdp"),
            P("fsdp", "ctx", None),
            P("fsdp", "ctx", None),
            P("fsdp", "ctx", None, None, None, None),
            P("fsdp"),
        ),
        out_specs=(split, split, *([shard] * 7), P("fsdp"), P("fsdp")),
        check_vma=False,
    )
```

```python
import functools

import jax
import jax.numpy as jnp
from jax import lax
from jax.experimental import pallas as pl
from jax.experimental.pallas import tpu as pltpu
from jax.sharding import PartitionSpec as P

D = 1024
HEADS = 8
HEAD_DIM = 128
HALF = 128
ROWS = 2 * HALF
BLOCK = 64
TOPK = 4
SIDE = HEADS // 2
SW = SIDE * HEAD_DIM
GROUP = 8
EPS = 1e-05
SCALE = HEAD_DIM**-0.5
LOG2E = 1.4426950408889634
F32 = jnp.float32
BF16 = jnp.bfloat16
EXTRA = 16
SENT = ROWS + EXTRA


def nn(a, b):
    return lax.dot_general(a, b, (((1,), (0,)), ((), ())), preferred_element_type=F32)


def nt(a, b):
    return lax.dot_general(a, b, (((1,), (1,)), ((), ())), preferred_element_type=F32)


def tn(a, b):
    return lax.dot_general(a, b, (((0,), (0,)), ((), ())), preferred_element_type=F32)


def params(mib=56):
    return pltpu.CompilerParams(vmem_limit_bytes=mib * 2**20)


def ring_order(count):
    if count == 8:
        return [0, 2, 4, 6, 7, 5, 3, 1]
    half = count // 2
    return list(range(half)) + [count - 1 - i for i in range(count - half)]


def ring_place(count):
    here = lax.axis_index("ctx")
    half = count // 2
    if count == 8:
        turned = here % 2
        return (1 - turned) * (here // 2) + turned * (count - 1 - here // 2)
    turned = here // half
    return (1 - turned) * here + turned * (count - 1 + half - here)


def ring_index(place, count):
    half = count // 2
    place = place % count
    turned = place // half
    if count == 8:
        return (1 - turned) * 2 * place + turned * (2 * count - 1 - 2 * place)
    return (1 - turned) * place + turned * (count - 1 + half - place)


def ring_pairs(count):
    order = ring_order(count)
    onward = [(order[i], order[(i + 1) % count]) for i in range(count)]
    return onward, [(b, a) for a, b in onward]


def list_base(count):
    return 1 + 2 * count


def list_at(owner, micro, side, micros, cap):
    return ((owner * micros + micro) * 2 + side) * (cap + 1)


def make_meta(indices, partner, cb_dev, count):
    micros = indices.shape[0]
    here = lax.axis_index("ctx")
    order = ring_order(count)
    place = ring_place(count)
    steps = jnp.arange(count, dtype=jnp.int32)
    at = jnp.stack([(place - steps) % count, (place + steps) % count], axis=1)
    owners = sum(jnp.where(at == p, d, 0) for p, d in enumerate(order))
    blocks = cb_dev * count
    cap = 2 * 128 // count
    side_shape = (micros, count, 2 * ROWS // (2 * BLOCK), 2, SIDE, TOPK)
    index = indices.reshape(side_shape).transpose(1, 0, 3, 2, 4, 5)
    index = index.reshape(count, micros, 2, -1)
    number = index % blocks
    mine = (number // cb_dev) == here
    own = jnp.arange(micros, dtype=jnp.int32)[None, :, None, None]
    document = jnp.where(index < blocks, own, partner[None, :, None, None])
    entries = index.shape[-1]
    entry = jnp.arange(entries, dtype=jnp.int32)
    query_block = entry // (SIDE * TOPK)
    head = entry // TOPK % SIDE
    code = ((document * cb_dev + number % cb_dev) * 4 + query_block) * SIDE + head
    before = (entry[:, None] < entry[None, :]).astype(F32)
    flags = mine.astype(F32)
    rank = jnp.dot(flags.reshape(-1, entries), before, preferred_element_type=F32).reshape(flags.shape)
    rank = rank.astype(jnp.int32)
    slot = jnp.arange(cap, dtype=jnp.int32)
    hit = mine[..., None, :] & (rank[..., None, :] == slot[:, None])
    codes = jnp.sum(jnp.where(hit, code[..., None, :], 0), axis=-1)
    length = jnp.sum(mine.astype(jnp.int32), axis=-1, keepdims=True)
    lists = jnp.concatenate([length, codes], axis=-1).reshape(-1)
    return jnp.concatenate([here.reshape(1), owners.reshape(-1), lists]).astype(jnp.int32), cap


def share_kernel(indices, gains, all_indices, all_gains, send_sem, recv_sem, *, count, shards):
    here, shard = lax.axis_index("ctx"), lax.axis_index("fsdp")
    groups = (("ctx", here, count, indices, all_indices), ("fsdp", shard, shards, gains, all_gains))
    barrier = pltpu.get_barrier_semaphore()
    for axis, index, size, _, _ in groups:
        for k in range(1, size):
            pl.semaphore_signal(
                barrier, inc=1, device_id={axis: (index + k) % size}, device_id_type=pl.DeviceIdType.MESH
            )
    pl.semaphore_wait(barrier, count + shards - 2)
    copies = []
    for number, (axis, index, size, source, target) in enumerate(groups):
        for k in range(1, size):
            copy = pltpu.make_async_remote_copy(
                source,
                target.at[index],
                send_sem.at[number, k],
                recv_sem.at[number, k],
                device_id={axis: (index + k) % size},
                device_id_type=pl.DeviceIdType.MESH,
            )
            copy.start()
            copies.append(copy)
        target[index] = source[...]
    for copy in copies:
        copy.wait()


def share(indices, gains, count, shards):
    vmem = pl.BlockSpec(memory_space=pltpu.VMEM)
    most = max(count, shards)
    return pl.pallas_call(
        functools.partial(share_kernel, count=count, shards=shards),
        in_specs=[vmem, vmem],
        out_specs=[vmem, vmem],
        out_shape=[
            jax.ShapeDtypeStruct((count,) + indices.shape, indices.dtype),
            jax.ShapeDtypeStruct((shards,) + gains.shape, gains.dtype),
        ],
        scratch_shapes=[pltpu.SemaphoreType.DMA((2, most)), pltpu.SemaphoreType.DMA((2, most))],
        compiler_params=pltpu.CompilerParams(
            vmem_limit_bytes=8 * 2**20, collective_id=1, has_side_effects=True
        ),
        name="share",
        cost_estimate=pl.CostEstimate(flops=0, bytes_accessed=20_000_000, transcendentals=0),
    )(indices, gains)


def collect_kernel(meta, ck, cv, *refs, micros, count, cap, first):
    mk, mv, sem_k, sem_v = refs[-4:]
    owner = pl.program_id(0) + first

    def list_of(i):
        base = list_base(count) + (owner * 2 * micros + i) * (cap + 1)
        return base, meta[base]

    def start(i, carry):
        base, length = list_of(i)

        def one(j, c):
            code = meta[base + 1 + j]
            head = (i & 1) * SIDE + (code & (SIDE - 1))
            rows = pl.ds(pl.multiple_of((code >> 4) << 6, BLOCK), BLOCK)
            cols = pl.ds(pl.multiple_of(head << 7, HEAD_DIM), HEAD_DIM)
            pltpu.make_async_copy(ck.at[rows, cols], mk.at[i >> 1, 0, i & 1, j], sem_k).start()
            pltpu.make_async_copy(cv.at[rows, cols], mv.at[i >> 1, 0, i & 1, j], sem_v).start()
            return c

        def clear(j, c):
            mk[i >> 1, 0, i & 1, j] = jnp.zeros((BLOCK, HEAD_DIM), BF16)
            mv[i >> 1, 0, i & 1, j] = jnp.zeros((BLOCK, HEAD_DIM), BF16)
            return c

        lax.fori_loop(0, length, one, carry)
        return lax.fori_loop(length, (length + GROUP - 1) // GROUP * GROUP, clear, carry)

    def finish(i, carry):
        _, length = list_of(i)
        rounds = length // GROUP

        def many(g, c):
            some = pl.ds(g * GROUP, GROUP)
            for place, sem in ((mk, sem_k), (mv, sem_v)):
                whole = place.at[i >> 1, 0, i & 1, some]
                pltpu.make_async_copy(whole, whole, sem).wait()
            return c

        def one(j, c):
            for place, sem in ((mk, sem_k), (mv, sem_v)):
                whole = place.at[i >> 1, 0, i & 1, j]
                pltpu.make_async_copy(whole, whole, sem).wait()
            return c

        lax.fori_loop(0, rounds, many, carry)
        return lax.fori_loop(rounds * GROUP, length, one, carry)

    lax.fori_loop(0, 2 * micros, start, 0)
    lax.fori_loop(0, 2 * micros, finish, 0)


def collect(meta, cache_keys, cache_values, count, cap, owners, into=()):
    micros = cache_keys.shape[0]
    shape = jax.ShapeDtypeStruct((micros, count, 2, cap, BLOCK, HEAD_DIM), BF16)
    anywhere = pl.BlockSpec(memory_space=pl.ANY)
    block = pl.BlockSpec((micros, 1, 2, cap, BLOCK, HEAD_DIM), lambda o, meta: (0, o + owners.start, 0, 0, 0, 0))
    return pl.pallas_call(
        functools.partial(collect_kernel, micros=micros, count=count, cap=cap, first=owners.start),
        grid_spec=pltpu.PrefetchScalarGridSpec(
            num_scalar_prefetch=1,
            grid=(len(owners),),
            in_specs=[anywhere, anywhere] + [anywhere] * len(into),
            out_specs=[block, block],
            scratch_shapes=[pltpu.SemaphoreType.DMA, pltpu.SemaphoreType.DMA],
        ),
        out_shape=[shape, shape],
        input_output_aliases={3: 0, 4: 1} if into else {},
        compiler_params=params(),
        name="collect",
        cost_estimate=pl.CostEstimate(
            flops=0, bytes_accessed=11_000_000 * len(owners), transcendentals=0
        ),
    )(meta, cache_keys.reshape(-1, D), cache_values.reshape(-1, D), *into)


def turn(value, cosine, sine):
    return value * cosine + pltpu.roll(value, HEAD_DIM // 2, 1) * sine


def first_kernel(x, gain, weight, cosine, sine, normed, qa, qb):
    value = x[0].astype(F32)
    scale = lax.rsqrt(jnp.mean(value * value, axis=-1, keepdims=True) + EPS)
    low = (value * scale * gain[...]).astype(BF16)
    normed[0] = low
    product = nn(low, weight[...])
    for h in range(HEADS):
        cols = slice(h * HEAD_DIM, (h + 1) * HEAD_DIM)
        out = qa if h < SIDE else qb
        place = slice((h % SIDE) * HEAD_DIM, (h % SIDE + 1) * HEAD_DIM)
        out[0, :, place] = turn(product[:, cols], cosine[...], sine[...]).astype(BF16)


def second_kernel(normed, weights, cosine, sine, keys, values, turned):
    low = normed[0]
    turned[...] = low.T
    product = nn(low, weights[0])
    for h in range(HEADS):
        cols = slice(h * HEAD_DIM, (h + 1) * HEAD_DIM)
        keys[0, :, cols] = turn(product[:, cols], cosine[...], sine[...]).astype(BF16)
    values[0] = nn(low, weights[1]).astype(BF16)


def seq_spec(*shape):
    return pl.BlockSpec((1,) + shape, lambda m, *_: (m,) + (0,) * len(shape))


def full_spec(*shape):
    return pl.BlockSpec(shape, lambda m, *_: (0,) * len(shape))


def seq_shape(micros, *shape, dtype=BF16):
    return jax.ShapeDtypeStruct((micros,) + shape, dtype)


def project_query(x, gain, weight, cosine, sine):
    micros = x.shape[0]
    return pl.pallas_call(
        first_kernel,
        grid=(micros,),
        in_specs=[
            seq_spec(ROWS, D),
            full_spec(1, D),
            full_spec(D, D),
            full_spec(ROWS, HEAD_DIM),
            full_spec(ROWS, HEAD_DIM),
        ],
        out_specs=[seq_spec(ROWS, D), seq_spec(ROWS, SW), seq_spec(ROWS, SW)],
        out_shape=[seq_shape(micros, ROWS, D), seq_shape(micros, ROWS, SW), seq_shape(micros, ROWS, SW)],
        compiler_params=params(),
        name="project_query",
        cost_estimate=pl.CostEstimate(flops=2 * micros * ROWS * D * D, bytes_accessed=8_000_000, transcendentals=0),
    )(x, gain, weight, cosine, sine)


def project_pairs(normed, weights, cosine, sine):
    micros = normed.shape[0]
    return pl.pallas_call(
        second_kernel,
        grid=(micros,),
        in_specs=[
            seq_spec(ROWS, D),
            full_spec(2, D, D),
            full_spec(ROWS, HEAD_DIM),
            full_spec(ROWS, HEAD_DIM),
        ],
        out_specs=[seq_spec(ROWS, D), seq_spec(ROWS, D), pl.BlockSpec((D, ROWS), lambda m: (0, m))],
        out_shape=[
            seq_shape(micros, ROWS, D),
            seq_shape(micros, ROWS, D),
            jax.ShapeDtypeStruct((D, micros * ROWS), BF16),
        ],
        compiler_params=params(),
        name="project_pairs",
        cost_estimate=pl.CostEstimate(flops=4 * micros * ROWS * D * D, bytes_accessed=10_000_000, transcendentals=0),
    )(normed, weights, cosine, sine)


def causal_mask(turned=False):
    row = lax.broadcasted_iota(jnp.int32, (ROWS, ROWS), 0)
    col = lax.broadcasted_iota(jnp.int32, (ROWS, ROWS), 1)
    return row <= col if turned else row >= col


def to_lanes(wide):
    lane = lax.broadcasted_iota(jnp.int32, (ROWS, HEAD_DIM), 1)
    packed = jnp.zeros((ROWS, HEAD_DIM), F32)
    for h in range(SIDE):
        packed = jnp.where(lane == h, wide[:, h * HEAD_DIM : (h + 1) * HEAD_DIM], packed)
    return packed.T[:8]


def to_columns(lanes):
    return jnp.concatenate([lanes, jnp.zeros((HEAD_DIM - 8, ROWS), F32)], axis=0).T


def split3(value):
    high = value.astype(BF16).astype(F32)
    middle = (value - high).astype(BF16).astype(F32)
    return high, middle, value - high - middle


def pack_lanes(lanes):
    high, middle, low = split3(lanes)
    rows = jnp.concatenate(
        [jnp.concatenate([high, middle], axis=1), jnp.concatenate([low, jnp.zeros_like(low)], axis=1)],
        axis=0,
    )
    return rows.astype(BF16)


def unpack_lanes(rows):
    value = rows.astype(F32)
    return value[:8, :ROWS] + value[:8, ROWS:] + value[8:, :ROWS]


def requests(meta, mk, mv, kbuf, vbuf, sem, micro, act, *, step, count, cap, micros):
    slot = micro % 2
    for side in range(2):
        owner = meta[1 + 2 * step + side]
        length = meta[list_base(count) + list_at(owner, micro, side, micros, cap)]

        def one(g, carry):
            some = pl.ds(g * GROUP, GROUP)
            for source, place in ((mk, kbuf), (mv, vbuf)):
                copy = pltpu.make_async_copy(
                    source.at[micro, owner, side, some], place.at[slot, side, some], sem.at[slot]
                )
                if act == "start":
                    copy.start()
                else:
                    copy.wait()
            return carry

        lax.fori_loop(0, (length + GROUP - 1) // GROUP, one, 0)


def request_ahead(fetch, micro, micros):
    @pl.when(micro == 0)
    def _():
        fetch(micro, "start")

    @pl.when(micro + 1 < micros)
    def _():
        fetch(micro + 1, "start")


def request_scratch(cap):
    return [
        pltpu.VMEM((2, 2, cap, BLOCK, HEAD_DIM), BF16),
        pltpu.VMEM((2, 2, cap, BLOCK, HEAD_DIM), BF16),
        pltpu.SemaphoreType.DMA((2,)),
    ]


EVERYTHING, LOW, HIGH = slice(0, ROWS), slice(0, HALF), slice(HALF, ROWS)


def tiles(side):
    return [
        (
            slice(h * HEAD_DIM, (h + 1) * HEAD_DIM),
            slice((side * SIDE + h) * HEAD_DIM, (side * SIDE + h + 1) * HEAD_DIM),
        )
        for h in range(SIDE)
    ]


def forward_kernel(
    meta, qa, qb, k, v, mk, mv, pa, pb, ta, tb, part, wide, kbuf, vbuf, sem, *, step, count, cap, micros
):
    micro = pl.program_id(0)
    here = meta[0]
    fetch = functools.partial(
        requests, meta, mk, mv, kbuf, vbuf, sem, step=step, count=count, cap=cap, micros=micros
    )
    request_ahead(fetch, micro, micros)
    for side, q in enumerate((qa, qb)):
        owner = meta[1 + 2 * step + side]

        def local(qrows, krows, masked):
            spots = tiles(side)
            scores = [nt(q[0, qrows, cols], k[0, krows, kcols]) for cols, kcols in spots]
            weights = [jnp.exp2(score * (SCALE * LOG2E)) for score in scores]
            if masked:
                weights = [jnp.where(causal_mask(), weight, 0.0) for weight in weights]
            for weight, (cols, kcols) in zip(weights, spots):
                values = v[0, krows, kcols]
                more = jnp.concatenate([values, jnp.ones_like(values)], axis=1)
                out = nn(weight.astype(BF16), more)
                part[qrows, kcols] = out[:, :HEAD_DIM]
                wide[qrows, kcols] = out[:, HEAD_DIM:]

        if step == 0:
            local(EVERYTHING, EVERYTHING, True)
        else:

            @pl.when(owner < here)
            def _():
                zeros = jnp.zeros((HALF, SW), F32)
                part[LOW, side * SW : (side + 1) * SW] = zeros
                wide[LOW, side * SW : (side + 1) * SW] = zeros
                local(HIGH, EVERYTHING, False)

            @pl.when(owner > here)
            def _():
                local(EVERYTHING, LOW, False)

    fetch(micro, "wait")
    slot = micro % 2
    for side, (q, out, total) in enumerate(((qa, pa, ta), (qb, pb, tb))):
        owner = meta[1 + 2 * step + side]
        base = list_base(count) + list_at(owner, micro, side, micros, cap)
        length = meta[base]

        def group(i, carry):
            numbers = [i * GROUP + j for j in range(GROUP)]
            places = [request_place(meta[base + 1 + number]) for number in numbers]
            scores = [
                nt(q[0, rows, cols], kbuf[slot, side, number])
                for number, (rows, cols) in zip(numbers, places)
            ]
            weights = [
                jnp.where(number < length, jnp.exp2(score * (SCALE * LOG2E)), 0.0).astype(BF16)
                for number, score in zip(numbers, scores)
            ]
            outs = []
            for number, weight in zip(numbers, weights):
                values = vbuf[slot, side, number]
                outs.append(nn(weight, jnp.concatenate([values, jnp.ones_like(values)], axis=1)))
            for o, (rows, cols) in zip(outs, places):
                cols = pl.ds(pl.multiple_of(cols.start + side * SW, HEAD_DIM), HEAD_DIM)
                part[rows, cols] += o[:, :HEAD_DIM]
                wide[rows, cols] += o[:, HEAD_DIM:]
            return carry

        lax.fori_loop(0, (length + GROUP - 1) // GROUP, group, 0)
        out[0] = part[:, side * SW : (side + 1) * SW].astype(BF16)
        total[0] = to_lanes(wide[:, side * SW : (side + 1) * SW])


def request_place(code):
    return (
        pl.ds(pl.multiple_of(((code >> 2) & 3) << 6, BLOCK), BLOCK),
        pl.ds(pl.multiple_of((code & 3) << 7, HEAD_DIM), HEAD_DIM),
    )


def attend(meta, qa, qb, keys, values, memory_keys, memory_values, step, count, cap):
    micros = qa.shape[0]
    half, whole, lanes = seq_spec(ROWS, SW), seq_spec(ROWS, D), seq_spec(8, ROWS)
    anywhere = pl.BlockSpec(memory_space=pl.ANY)
    return pl.pallas_call(
        functools.partial(forward_kernel, step=step, count=count, cap=cap, micros=micros),
        grid_spec=pltpu.PrefetchScalarGridSpec(
            num_scalar_prefetch=1,
            grid=(micros,),
            in_specs=[half, half, whole, whole, anywhere, anywhere],
            out_specs=[half, half, lanes, lanes],
            scratch_shapes=[pltpu.VMEM((ROWS, D), F32), pltpu.VMEM((ROWS, D), F32)]
            + request_scratch(cap),
        ),
        out_shape=[
            seq_shape(micros, ROWS, SW),
            seq_shape(micros, ROWS, SW),
            seq_shape(micros, 8, ROWS, dtype=F32),
            seq_shape(micros, 8, ROWS, dtype=F32),
        ],
        compiler_params=params(24),
        name="attend",
        cost_estimate=pl.CostEstimate(flops=6_000_000_000, bytes_accessed=10_000_000, transcendentals=0),
    )(meta, qa, qb, keys, values, memory_keys, memory_values)


def combine_kernel(*refs, carried, sums):
    refs = list(refs)
    received = [refs.pop(0), refs.pop(0)] if carried else [None, None]
    parts = [refs.pop(0), refs.pop(0)]
    totals = [refs.pop(0), refs.pop(0)] if sums else [None, None]
    for got, part, total, out in zip(received, parts, totals, refs):
        value = part[0].astype(F32)
        if carried:
            value = value + got[0, :ROWS].astype(F32)
        out[0, :ROWS] = value.astype(BF16)
        if sums:
            lanes = total[0]
            if carried:
                lanes = lanes + unpack_lanes(got[0, ROWS:])
            out[0, ROWS:] = pack_lanes(lanes)


def combine(received, parts, totals=()):
    micros = parts[0].shape[0]
    sent = SENT if totals else ROWS
    half, lanes, packed = seq_spec(ROWS, SW), seq_spec(8, ROWS), seq_spec(sent, SW)
    return pl.pallas_call(
        functools.partial(combine_kernel, carried=bool(received), sums=bool(totals)),
        grid=(micros,),
        in_specs=[packed] * len(received) + [half] * 2 + [lanes] * len(totals),
        out_specs=[packed, packed],
        out_shape=[seq_shape(micros, sent, SW)] * 2,
        compiler_params=params(16),
        name="combine",
        cost_estimate=pl.CostEstimate(flops=2_000_000, bytes_accessed=7_000_000, transcendentals=0),
    )(*received, *parts, *totals)


def finish_kernel(acc_a, acc_b, pa, pb, ta, tb, x, weight, gain, mixed, low, total, middle, normed):
    for side, (acc, part, own) in enumerate(((acc_a, pa, ta), (acc_b, pb, tb))):
        lanes = unpack_lanes(acc[0, ROWS:]) + own[0]
        total[0, side] = lanes
        columns = to_columns(lanes)
        for h in range(SIDE):
            cols = slice(h * HEAD_DIM, (h + 1) * HEAD_DIM)
            place = slice((side * SIDE + h) * HEAD_DIM, (side * SIDE + h + 1) * HEAD_DIM)
            weighted = acc[0, :ROWS, cols].astype(F32) + part[0, :, cols].astype(F32)
            value = weighted / columns[:, h : h + 1]
            mixed[0, :, place] = value
            low[0, :, place] = value.astype(BF16)
    value = x[0].astype(F32) + nn(low[0], weight[...])
    middle[0] = value
    scale = lax.rsqrt(jnp.mean(value * value, axis=-1, keepdims=True) + EPS)
    normed[0] = (value * scale * gain[...]).astype(BF16)


def finish(acc_a, acc_b, pa, pb, ta, tb, x, weight, gain):
    micros = acc_a.shape[0]
    packed, half, lanes = seq_spec(SENT, SW), seq_spec(ROWS, SW), seq_spec(8, ROWS)
    whole = seq_spec(ROWS, D)
    return pl.pallas_call(
        finish_kernel,
        grid=(micros,),
        in_specs=[packed, packed, half, half, lanes, lanes, whole, full_spec(D, D), full_spec(1, D)],
        out_specs=[whole, whole, seq_spec(2, 8, ROWS), whole, whole],
        out_shape=[
            seq_shape(micros, ROWS, D, dtype=F32),
            seq_shape(micros, ROWS, D),
            seq_shape(micros, 2, 8, ROWS, dtype=F32),
            seq_shape(micros, ROWS, D, dtype=F32),
            seq_shape(micros, ROWS, D),
        ],
        compiler_params=params(),
        name="finish",
        cost_estimate=pl.CostEstimate(flops=2 * micros * ROWS * D * D, bytes_accessed=16_000_000, transcendentals=0),
    )(acc_a, acc_b, pa, pb, ta, tb, x, weight, gain)


TILE = 256


def feed_kernel(
    normed, incoming, middle, gate_weight, up_weight, down_weight, out, back, dg, du, dd, turned, acc, hid, bg, bu
):
    step = pl.program_id(0)
    micros = normed.shape[0]

    @pl.when(step == 0)
    def _():
        for m in range(micros):
            turned[:, m * ROWS : (m + 1) * ROWS] = normed[m].T
            acc[m] = middle[m]
            back[m] = jnp.zeros((ROWS, D), F32)

    wg, wu, wd = gate_weight[...], up_weight[...], down_weight[...]
    for m in range(micros):
        rows = slice(m * ROWS, (m + 1) * ROWS)
        gate = nn(normed[m], wg)
        upper = nn(normed[m], wu)
        slope = nt(incoming[m], wd)
        sigma = 1.0 / (1.0 + jnp.exp(-gate))
        silu = gate * sigma
        hid[rows] = (silu * upper).astype(BF16)
        bg[rows] = (slope * upper * (sigma * (1.0 + gate * (1.0 - sigma)))).astype(BF16)
        bu[rows] = (slope * silu).astype(BF16)
        acc[m] += nn(hid[rows], wd)
        back[m] += nt(bg[rows], wg) + nt(bu[rows], wu)
    dg[...] = nn(turned[...], bg[...]).astype(BF16)
    du[...] = nn(turned[...], bu[...]).astype(BF16)
    dd[...] = tn(hid[...], incoming[...].reshape(micros * ROWS, D)).astype(BF16)

    @pl.when(step == pl.num_programs(0) - 1)
    def _():
        out[...] = acc[...].astype(BF16)


def feed(normed, incoming, middle, gate_weight, up_weight, down_weight):
    micros = normed.shape[0]
    units = gate_weight.shape[1]
    whole = full_spec(micros, ROWS, D)
    wide = pl.BlockSpec((D, TILE), lambda f: (0, f))
    tall = pl.BlockSpec((TILE, D), lambda f: (f, 0))
    return pl.pallas_call(
        feed_kernel,
        grid=(units // TILE,),
        in_specs=[whole, whole, whole, wide, wide, tall],
        out_specs=[whole, whole, wide, wide, tall],
        out_shape=[
            seq_shape(micros, ROWS, D),
            seq_shape(micros, ROWS, D, dtype=F32),
            jax.ShapeDtypeStruct((D, units), BF16),
            jax.ShapeDtypeStruct((D, units), BF16),
            jax.ShapeDtypeStruct((units, D), BF16),
        ],
        scratch_shapes=[
            pltpu.VMEM((D, micros * ROWS), BF16),
            pltpu.VMEM((micros, ROWS, D), F32),
            pltpu.VMEM((micros * ROWS, TILE), BF16),
            pltpu.VMEM((micros * ROWS, TILE), BF16),
            pltpu.VMEM((micros * ROWS, TILE), BF16),
        ],
        compiler_params=params(),
        name="feed",
        cost_estimate=pl.CostEstimate(
            flops=18 * micros * ROWS * D * units, bytes_accessed=50_000_000, transcendentals=0
        ),
    )(normed, incoming, middle, gate_weight, up_weight, down_weight)


def prepare_kernel(back_normed, middle, incoming, gain, weight, mixed, total, da, db, back_middle, back_attn, dgain):
    value = middle[0]
    scale = lax.rsqrt(jnp.mean(value * value, axis=-1, keepdims=True) + EPS)
    hat = value * scale
    slope = back_normed[0] * gain[...]
    slope = incoming[0].astype(F32) + scale * (
        slope - hat * jnp.mean(slope * hat, axis=-1, keepdims=True)
    )
    back_middle[0] = slope
    back_attn[0] = slope.astype(BF16)
    dgain[0] = jnp.sum((back_normed[0] * hat).reshape(ROWS // 8, 8, D), axis=0)
    lane = lax.broadcasted_iota(jnp.int32, (ROWS, HEAD_DIM), 1)
    for side, out in enumerate((da, db)):
        columns = to_columns(total[0, side])
        packed = jnp.zeros((ROWS, HEAD_DIM), F32)
        back = nt(back_attn[0], weight[side * SW : (side + 1) * SW, :])
        for h in range(SIDE):
            cols = slice(h * HEAD_DIM, (h + 1) * HEAD_DIM)
            place = slice((side * SIDE + h) * HEAD_DIM, (side * SIDE + h + 1) * HEAD_DIM)
            part = back[:, cols]
            divisor = columns[:, h : h + 1]
            out[0, :ROWS, cols] = (part / divisor).astype(BF16)
            product = jnp.sum(part * mixed[0, :, place], axis=1, keepdims=True)
            packed = jnp.where(lane == h, -product / divisor, packed)
        out[0, ROWS:] = pack_lanes(packed.T[:8])


def prepare(back_normed, middle, incoming, gain, weight, mixed, total):
    micros = middle.shape[0]
    whole = seq_spec(ROWS, D)
    return pl.pallas_call(
        prepare_kernel,
        grid=(micros,),
        in_specs=[whole, whole, whole, full_spec(1, D), full_spec(D, D), whole, seq_spec(2, 8, ROWS)],
        out_specs=[seq_spec(SENT, SW), seq_spec(SENT, SW), whole, whole, seq_spec(8, D)],
        out_shape=[
            seq_shape(micros, SENT, SW),
            seq_shape(micros, SENT, SW),
            seq_shape(micros, ROWS, D, dtype=F32),
            seq_shape(micros, ROWS, D),
            seq_shape(micros, 8, D, dtype=F32),
        ],
        compiler_params=params(),
        name="prepare",
        cost_estimate=pl.CostEstimate(flops=2 * micros * ROWS * D * D, bytes_accessed=22_000_000, transcendentals=0),
    )(back_normed, middle, incoming, gain, weight, mixed, total)


def backward_kernel(
    meta, qa, qb, da, db, k, v, mk, mv, dqa, dqb, part, wide, kbuf, vbuf, sem, *, step, count, cap, micros
):
    micro = pl.program_id(0)
    here = meta[0]
    fetch = functools.partial(
        requests, meta, mk, mv, kbuf, vbuf, sem, step=step, count=count, cap=cap, micros=micros
    )
    request_ahead(fetch, micro, micros)
    for side, (q, d) in enumerate(((qa, da), (qb, db))):
        owner = meta[1 + 2 * step + side]
        columns = to_columns(unpack_lanes(d[0, ROWS:]))
        for h, (_, place) in enumerate(tiles(side)):
            wide[:, place] = jnp.broadcast_to(columns[:, h : h + 1], (ROWS, HEAD_DIM))

        def local(qrows, krows, masked):
            spots = tiles(side)
            scores = [nt(q[0, qrows, cols], k[0, krows, kcols]) for cols, kcols in spots]
            slopes = [nt(d[0, qrows, cols], v[0, krows, kcols]) for cols, kcols in spots]
            weights = [jnp.exp2(score * (SCALE * LOG2E)) for score in scores]
            if masked:
                weights = [jnp.where(causal_mask(), weight, 0.0) for weight in weights]
            slopes = [
                (weight * (slope + wide[qrows, kcols][:, :1])).astype(BF16)
                for weight, slope, (_, kcols) in zip(weights, slopes, spots)
            ]
            for slope, (_, kcols) in zip(slopes, spots):
                part[qrows, kcols] = nn(slope, k[0, krows, kcols])

        if step == 0:
            local(EVERYTHING, EVERYTHING, True)
        else:

            @pl.when(owner < here)
            def _():
                part[LOW, side * SW : (side + 1) * SW] = jnp.zeros((HALF, SW), F32)
                local(HIGH, EVERYTHING, False)

            @pl.when(owner > here)
            def _():
                local(EVERYTHING, LOW, False)

    fetch(micro, "wait")
    slot = micro % 2
    for side, (q, d, out) in enumerate(((qa, da, dqa), (qb, db, dqb))):
        owner = meta[1 + 2 * step + side]
        base = list_base(count) + list_at(owner, micro, side, micros, cap)
        length = meta[base]

        def group(i, carry):
            numbers = [i * GROUP + j for j in range(GROUP)]
            places = [request_place(meta[base + 1 + number]) for number in numbers]
            shifted = [
                (rows, pl.ds(pl.multiple_of(cols.start + side * SW, HEAD_DIM), HEAD_DIM))
                for rows, cols in places
            ]
            scores = [
                nt(q[0, rows, cols], kbuf[slot, side, number])
                for number, (rows, cols) in zip(numbers, places)
            ]
            slopes = [
                nt(d[0, rows, cols], vbuf[slot, side, number])
                for number, (rows, cols) in zip(numbers, places)
            ]
            weights = [jnp.exp2(score * (SCALE * LOG2E)) for score in scores]
            slopes = [
                jnp.where(
                    number < length, weight * (slope + wide[rows, cols][:, :BLOCK]), 0.0
                ).astype(BF16)
                for number, weight, slope, (rows, cols) in zip(numbers, weights, slopes, shifted)
            ]
            outs = [nn(slope, kbuf[slot, side, number]) for number, slope in zip(numbers, slopes)]
            for o, (rows, cols) in zip(outs, shifted):
                part[rows, cols] += o
            return carry

        lax.fori_loop(0, (length + GROUP - 1) // GROUP, group, 0)
        out[0] = part[:, side * SW : (side + 1) * SW].astype(BF16)


def unattend(meta, qa, qb, da, db, keys, values, memory_keys, memory_values, step, count, cap):
    micros = qa.shape[0]
    half, packed, whole = seq_spec(ROWS, SW), seq_spec(SENT, SW), seq_spec(ROWS, D)
    anywhere = pl.BlockSpec(memory_space=pl.ANY)
    return pl.pallas_call(
        functools.partial(backward_kernel, step=step, count=count, cap=cap, micros=micros),
        grid_spec=pltpu.PrefetchScalarGridSpec(
            num_scalar_prefetch=1,
            grid=(micros,),
            in_specs=[half, half, packed, packed, whole, whole, anywhere, anywhere],
            out_specs=[half, half],
            scratch_shapes=[pltpu.VMEM((ROWS, D), F32), pltpu.VMEM((ROWS, D), F32)]
            + request_scratch(cap),
        ),
        out_shape=[seq_shape(micros, ROWS, SW), seq_shape(micros, ROWS, SW)],
        compiler_params=params(24),
        name="unattend",
        cost_estimate=pl.CostEstimate(flops=8_000_000_000, bytes_accessed=12_000_000, transcendentals=0),
    )(meta, qa, qb, da, db, keys, values, memory_keys, memory_values)


def key_kernel(meta, k, v, *refs, steps, micros, last):
    number = len(steps)
    sources, refs = refs[: 4 * number], refs[4 * number :]
    if last:
        dk_first, dv_first, cosine, sine, back_key, back_value, dk, dv, qbuf, dbuf, sem = refs
    else:
        dk, dv, qbuf, dbuf, sem = refs
    micro = pl.program_id(0)
    here = meta[0]

    def fetch(m, act):
        slot = m % 2
        for i in range(number):
            for side in range(2):
                for source, place in (
                    (sources[4 * i + side], qbuf.at[slot, side, i]),
                    (sources[4 * i + 2 + side], dbuf.at[slot, side, i]),
                ):
                    copy = pltpu.make_async_copy(source.at[m], place, sem.at[slot])
                    if act == "start":
                        copy.start()
                    else:
                        copy.wait()

    request_ahead(fetch, micro, micros)
    fetch(micro, "wait")
    dk[0] = dk_first[0] if last else jnp.zeros((ROWS, D), F32)
    dv[0] = dv_first[0] if last else jnp.zeros((ROWS, D), F32)
    slot = micro % 2
    for side in range(2):
        spots = tiles(side)

        def one(i, step, own):
            q, d = qbuf.at[slot, side, i], dbuf.at[slot, side, i]
            shift = unpack_lanes(d[ROWS:, :])

            def local(qrows, krows, masked):
                scores = [nt(k[0, krows, kcols], q[qrows, cols]) for cols, kcols in spots]
                slopes = [nt(v[0, krows, kcols], d[qrows, cols]) for cols, kcols in spots]
                weights = [jnp.exp2(score * (SCALE * LOG2E)) for score in scores]
                if masked:
                    weights = [jnp.where(causal_mask(True), weight, 0.0) for weight in weights]
                slopes = [
                    (weight * (slope + shift[h : h + 1, qrows])).astype(BF16)
                    for h, (weight, slope) in enumerate(zip(weights, slopes))
                ]
                for weight, slope, (cols, kcols) in zip(weights, slopes, spots):
                    dk[0, krows, kcols] += nn(slope, q[qrows, cols])
                    dv[0, krows, kcols] += nn(weight.astype(BF16), d[qrows, cols])

            if own:
                local(EVERYTHING, EVERYTHING, True)
                return
            owner = meta[1 + 2 * step + side]

            @pl.when(owner < here)
            def _():
                local(HIGH, EVERYTHING, False)

            @pl.when(owner > here)
            def _():
                local(EVERYTHING, LOW, False)

        first = 0
        if steps[0] == 0:
            one(0, 0, True)
            first = 1

        def loop(i, carry):
            one(i, steps[0] + i, False)
            return carry

        lax.fori_loop(first, number, loop, 0)
    if last:
        for h in range(HEADS):
            cols = slice(h * HEAD_DIM, (h + 1) * HEAD_DIM)
            back_key[0, :, cols] = turn(dk[0, :, cols] * SCALE, cosine[...], -sine[...]).astype(BF16)
        back_value[0] = dv[0].astype(BF16)


def key_gradients(meta, keys, values, queries, slopes, steps, first=(), angle=()):
    micros = keys.shape[0]
    whole = seq_spec(ROWS, D)
    anywhere = pl.BlockSpec(memory_space=pl.ANY)
    sources = []
    for step in steps:
        sources += [*queries[step], *slopes[step]]
    last = bool(first)
    sum_scratch = [pltpu.VMEM((1, ROWS, D), F32)] * 2 if last else []
    return pl.pallas_call(
        functools.partial(key_kernel, steps=steps, micros=micros, last=last),
        grid_spec=pltpu.PrefetchScalarGridSpec(
            num_scalar_prefetch=1,
            grid=(micros,),
            in_specs=[whole, whole]
            + [anywhere] * len(sources)
            + [whole] * len(first)
            + [full_spec(ROWS, HEAD_DIM)] * len(angle),
            out_specs=[whole, whole],
            scratch_shapes=sum_scratch
            + [
                pltpu.VMEM((2, 2, len(steps), ROWS, SW), BF16),
                pltpu.VMEM((2, 2, len(steps), SENT, SW), BF16),
                pltpu.SemaphoreType.DMA((2,)),
            ],
        ),
        out_shape=[seq_shape(micros, ROWS, D, dtype=BF16 if last else F32)] * 2,
        compiler_params=params(40),
        name="key_gradients",
        cost_estimate=pl.CostEstimate(
            flops=3_000_000_000 * len(steps), bytes_accessed=20_000_000, transcendentals=0
        ),
    )(meta, keys, values, *sources, *first, *angle)


def bits(size):
    return [1 << i for i in range(size.bit_length() - 1)]


def by_rows(rows, chunks):
    return rows % (16 * chunks) == 0


PIECE = 512


def tail_kernel(
    acc_a,
    acc_b,
    part_a,
    part_b,
    cosine,
    sine,
    gain,
    second,
    *rest,
    count,
    shards,
    parts,
):
    early_far, rest = rest[:parts], rest[parts:]
    tail_work(
        acc_a, acc_b, part_a, part_b, cosine, sine, gain, second, early_far, *rest, count=count, shards=shards
    )


def tail_work(
    acc_a,
    acc_b,
    part_a,
    part_b,
    cosine,
    sine,
    gain,
    second,
    early_far,
    back_key_far,
    back_value_far,
    turned_far,
    query_far,
    pairs_far,
    x_far,
    middle_far,
    early_out,
    late_out,
    gains_out,
    input_out,
    *scratch,
    count,
    shards,
):
    scratch = list(scratch)
    halves = [scratch.pop(0) for _ in bits(shards)]
    (
        back_query,
        back_key,
        back_value,
        turned,
        weight,
        x,
        middle,
        early,
        given,
        early_slots,
        late_slots,
        gain_in,
        gain_sum,
        ring_send,
        ring_recv,
        half_send,
        half_recv,
        gain_send,
        gain_recv,
        near,
    ) = scratch
    micros = x.shape[0]
    chunks = 2 * count
    shard_rows = D // shards
    here, shard = lax.axis_index("ctx"), lax.axis_index("fsdp")
    place = ring_place(count)
    neighbour = (ring_index(place + 1, count), ring_index(place + count - 1, count))
    partners = [("fsdp", shard, bit) for bit in bits(shards)] + [("ctx", here, bit) for bit in bits(count)]

    copies = {}
    column = 0
    pieces = []
    for i, part in enumerate(early_far):
        pieces.append((f"early{i}", part, early.at[:, :, column : column + part.shape[2]]))
        column += part.shape[2]
    for number, (name, source, target) in enumerate(
        (
            *pieces,
            ("turned", turned_far, turned),
            ("back_key", back_key_far, back_key),
            ("back_value", back_value_far, back_value),
            ("query", query_far, weight.at[0]),
            ("pairs", pairs_far, weight.at[1:]),
            ("x", x_far, x),
            ("middle", middle_far, middle),
        )
    ):
        copies[name] = pltpu.make_async_copy(source, target, near.at[number])
        copies[name].start()

    def partner(axis, index, bit):
        return {axis: index + bit * (1 - 2 * ((index // bit) % 2))}

    barrier = pltpu.get_barrier_semaphore()
    known = [{"ctx": neighbour[0]}, {"ctx": neighbour[1]}] + [partner(*p) for p in partners]
    for device in known:
        pl.semaphore_signal(barrier, inc=1, device_id=device, device_id_type=pl.DeviceIdType.MESH)
    pl.semaphore_wait(barrier, len(known))

    sent = []

    def send(source, target, send_sem, recv_sem, device):
        copy = pltpu.make_async_remote_copy(
            source, target, send_sem, recv_sem, device_id=device, device_id_type=pl.DeviceIdType.MESH
        )
        copy.start()
        sent.append(copy)
        return copy

    def flow(number, first_source, source, slots, out):
        def home(side, hop):
            sign = 1 - 2 * side
            return side * count + (place - sign * hop + 2 * count) % count

        def start(hop):
            result = []
            for side in range(2):
                if hop == 1:
                    pair = first_source(home(side, 1)), slots(side, 0)
                elif hop < count:
                    pair = slots(side, hop - 2), slots(side, hop - 1)
                else:
                    chunk = home(side, hop - count)
                    pair = out(chunk), out(chunk)
                result.append(
                    send(
                        *pair,
                        ring_send.at[number, side, hop - 1],
                        ring_recv.at[number, side, hop - 1],
                        {"ctx": neighbour[side]},
                    )
                )
            return result

        def finish(hop, pending):
            for side in range(2):
                pending[side].wait_recv()
                if hop < count:
                    got = slots(side, hop - 1)
                    total = got[...].astype(F32) + source(home(side, 1 + hop))[...].astype(F32)
                    target = out(home(side, 0)) if hop == count - 1 else got
                    target[...] = total.astype(BF16)

        return start, finish

    class Run:
        def __init__(self, *arguments):
            self.start, self.finish = flow(*arguments)
            self.hop, self.pending = 0, None

        def advance(self):
            if self.hop:
                self.finish(self.hop, self.pending)
            self.hop += 1
            if self.hop <= 2 * count - 2:
                self.pending = self.start(self.hop)

        def done(self):
            return self.hop > 2 * count - 2

    width = early.shape[2]
    middle_column = width // HEAD_DIM // 2 * HEAD_DIM
    runs = []
    for number, cols in enumerate((slice(0, middle_column), slice(middle_column, width))):
        runs.append(
            Run(
                number,
                lambda c, cols=cols: early.at[c, :, cols],
                lambda c, cols=cols: early.at[c, :, cols],
                lambda side, slot, cols=cols: early_slots.at[side, slot, :, cols],
                lambda c, cols=cols: early_out.at[c, :, cols],
            )
        )

    sources = (back_query, back_key, back_value)

    def product(s, target, add):
        rows = turned[pl.ds(pl.multiple_of(s * shard_rows, shard_rows), shard_rows), :]
        for start in range(0, 3 * D, PIECE):
            column = start % D
            right = sources[start // D][:, :, column : column + PIECE].reshape(micros * ROWS, PIECE)
            value = nn(rows, right)
            if by_rows(shard_rows, chunks):
                value = value.reshape(chunks, shard_rows // chunks, PIECE)
                spots = [((slice(None), slice(None), slice(start, start + PIECE)), value)]
            else:
                step = target.shape[2]
                spots = [
                    (((start + c) // step,), value[:, c : c + step]) for c in range(0, PIECE, step)
                ]
            for spot, piece in spots:
                if add:
                    piece = target[spot].astype(F32) + piece.astype(BF16).astype(F32)
                target[spot] = piece.astype(BF16)

    if not by_rows(shard_rows, chunks):
        used = 3 * D // halves[0].shape[3]
        for c in range(used, chunks):
            given[:, c] = jnp.zeros_like(given[:, c])

    def bit_of(i):
        return (shard // (1 << i)) % 2

    def give(j):
        product(2 * j + 1 - bit_of(0), given.at[j], False)
        return send(
            given.at[j], halves[0].at[j], half_send.at[0, j], half_recv.at[0, j], partner("fsdp", shard, 1)
        )

    def halve_start(i):
        return [
            send(
                halves[i - 1].at[2 * j + 1 - bit_of(i)],
                halves[i].at[j],
                half_send.at[i, j],
                half_recv.at[i, j],
                partner("fsdp", shard, 1 << i),
            )
            for j in range(shards >> (i + 1))
        ]

    def halve_finish(i, j, copy):
        copy.wait_recv()
        if i == 0:
            product(2 * j + bit_of(0), halves[0].at[j], True)
            return

        def add(c, carry):
            halves[i][j, c] = (
                halves[i][j, c].astype(F32) + halves[i - 1][2 * j + bit_of(i), c].astype(F32)
            ).astype(BF16)
            return carry

        lax.fori_loop(0, chunks, add, 0)

    def unturn():
        for m in range(micros):
            for h in range(HEADS):
                acc, part = (acc_a, part_a) if h < SIDE else (acc_b, part_b)
                cols = slice(h % SIDE * HEAD_DIM, (h % SIDE + 1) * HEAD_DIM)
                value = (acc[m, :, cols].astype(F32) + part[m, :, cols].astype(F32)) * SCALE
                back_query[m, :, h * HEAD_DIM : (h + 1) * HEAD_DIM] = turn(
                    value, cosine[...], -sine[...]
                ).astype(BF16)

    def input_back(m):
        slope = nt(back_query[m], weight[0]) + nt(back_key[m], weight[1]) + nt(back_value[m], weight[2])
        value = x[m].astype(F32)
        scale = lax.rsqrt(jnp.mean(value * value, axis=-1, keepdims=True) + EPS)
        hat = value * scale
        first = jnp.sum((slope * hat).reshape(ROWS // 8, 8, D), axis=0)
        slope = slope * gain[...]
        input_out[m] = middle[m] + scale * (slope - hat * jnp.mean(slope * hat, axis=-1, keepdims=True))
        gain_sum[1] = first if m == 0 else gain_sum[1] + first

    def gains_ready():
        first = jnp.sum(gain_sum[1], axis=0, keepdims=True)
        other = jnp.sum(jnp.sum(second[...], axis=0), axis=0, keepdims=True)
        gain_sum[0] = jnp.concatenate([first, other, jnp.zeros((6, D), F32)], axis=0)

    def gain_start(i):
        return send(gain_sum.at[i], gain_in.at[i], gain_send.at[i], gain_recv.at[i], partner(*partners[i]))

    def gain_finish(i, copy):
        copy.wait_recv()
        gain_sum[i + 1] = gain_sum[i] + gain_in[i]

    stages = len(halves)
    late = []

    def advance():
        for run in runs:
            for each in (run, *late):
                if not each.done():
                    each.advance()

    for i in range(len(early_far)):
        copies[f"early{i}"].wait()
    advance()
    unturn()
    for name in ("turned", "back_key", "back_value"):
        copies[name].wait()
    order = [list(range(shards // 2))]
    if stages > 1:
        order = [
            [2 * j + 1 - bit_of(1) for j in range(shards // 4)],
            [2 * j + bit_of(1) for j in range(shards // 4)],
        ]
    half = None
    for numbers in order:
        given_now = []
        for j in numbers:
            given_now.append(give(j))
            advance()
        for j, copy in zip(numbers, given_now):
            halve_finish(0, j, copy)
            advance()
        if half is None and stages > 1:
            half = halve_start(1)
    for i in range(1, stages - 1):
        for j, copy in enumerate(half):
            halve_finish(i, j, copy)
        half = halve_start(i + 1)
        advance()
    for name in ("query", "pairs", "x", "middle"):
        copies[name].wait()
    for m in range(micros):
        if m == micros - 1:
            if stages > 1:
                halve_finish(stages - 1, 0, half[0])
            late.append(
                Run(
                    2,
                    lambda c: halves[-1].at[0, c],
                    lambda c: halves[-1].at[0, c],
                    lambda side, slot: late_slots.at[side, slot],
                    lambda c: late_out.at[c],
                )
            )
            advance()
        input_back(m)
        advance()
    gains_ready()
    for i in range(len(partners)):
        copy = gain_start(i)
        advance()
        gain_finish(i, copy)
    while not all(run.done() for run in runs + late):
        advance()
    gains_out[...] = gain_sum[len(partners)]
    for copy in sent:
        copy.wait_send()


def tail(received, own, angle, gain, second, early, back_key, back_value, turned, weights, x, middle, count, shards):
    micros = x.shape[0]
    chunks = 2 * count
    shard_rows = D // shards
    if by_rows(shard_rows, chunks):
        late = (chunks, shard_rows // chunks, 3 * D)
    else:
        late = (chunks, shard_rows, -(-3 * D // (chunks * HEAD_DIM)) * HEAD_DIM)
    exchanges = len(bits(shards)) + len(bits(count))
    early_shape = early[0].shape[:2] + (sum(part.shape[2] for part in early),)
    vmem = pl.BlockSpec(memory_space=pltpu.VMEM)
    anywhere = pl.BlockSpec(memory_space=pl.ANY)
    return pl.pallas_call(
        functools.partial(tail_kernel, count=count, shards=shards, parts=len(early)),
        in_specs=[vmem] * 8 + [anywhere] * (7 + len(early)),
        out_specs=[vmem] * 4,
        out_shape=[
            jax.ShapeDtypeStruct(early_shape, BF16),
            jax.ShapeDtypeStruct(late, BF16),
            jax.ShapeDtypeStruct((8, D), F32),
            seq_shape(micros, ROWS, D, dtype=F32),
        ],
        scratch_shapes=[pltpu.VMEM((shards // (2 * bit),) + late, BF16) for bit in bits(shards)]
        + [pltpu.VMEM((micros, ROWS, D), BF16)] * 3
        + [
            pltpu.VMEM(turned.shape, BF16),
            pltpu.VMEM((3, D, D), BF16),
            pltpu.VMEM((micros, ROWS, D), BF16),
            pltpu.VMEM((micros, ROWS, D), F32),
            pltpu.VMEM(early_shape, BF16),
            pltpu.VMEM((shards // 2,) + late, BF16),
            pltpu.VMEM((2, count - 1) + early_shape[1:], BF16),
            pltpu.VMEM((2, count - 1) + late[1:], BF16),
            pltpu.VMEM((exchanges, 8, D), F32),
            pltpu.VMEM((exchanges + 1, 8, D), F32),
            pltpu.SemaphoreType.DMA((3, 2, 2 * count - 2)),
            pltpu.SemaphoreType.DMA((3, 2, 2 * count - 2)),
            pltpu.SemaphoreType.DMA((len(bits(shards)), shards // 2)),
            pltpu.SemaphoreType.DMA((len(bits(shards)), shards // 2)),
            pltpu.SemaphoreType.DMA((exchanges,)),
            pltpu.SemaphoreType.DMA((exchanges,)),
            pltpu.SemaphoreType.DMA((7 + len(early),)),
        ],
        compiler_params=pltpu.CompilerParams(
            vmem_limit_bytes=60 * 2**20, collective_id=0, has_side_effects=True
        ),
        name="tail",
        cost_estimate=pl.CostEstimate(flops=12_000_000_000, bytes_accessed=300_000_000, transcendentals=0),
    )(
        *received,
        *own,
        *angle,
        gain,
        second,
        *early,
        back_key,
        back_value,
        turned,
        *weights,
        x,
        middle,
    )


def to_chunks(parts, count):
    rows = parts[0].shape[0]
    chunks = 2 * count
    if by_rows(rows, chunks):
        return [part.reshape(chunks, rows // chunks, -1) for part in parts]
    value = jnp.concatenate(parts, axis=1)
    width = value.shape[1]
    step = -(-width // (chunks * HEAD_DIM)) * HEAD_DIM
    value = jnp.pad(value, [(0, 0), (0, step * chunks - width)])
    return [jnp.moveaxis(value.reshape(rows, chunks, step), 1, 0)]


def from_chunks(value, rows, width):
    if by_rows(rows, value.shape[0]):
        return value.reshape(rows, width)
    return jnp.moveaxis(value, 0, 1).reshape(rows, -1)[:, :width]


def body(
    tokens,
    cotangent,
    query_weight,
    key_weight,
    value_weight,
    output_weight,
    gate_weight,
    up_weight,
    down_weight,
    first_gain,
    second_gain,
    cache_keys,
    cache_values,
    block_indices,
    partner,
):
    count = lax.axis_size("ctx")
    here = lax.axis_index("ctx")
    micros = tokens.shape[0]
    rows = micros * ROWS
    onward, backward = ring_pairs(count)

    def gather(value):
        return lax.all_gather(value, "fsdp", axis=0, tiled=True)

    shards = lax.axis_size("fsdp")
    requested = block_indices.reshape(micros, -1)
    own_rows = D // shards
    indices, gains = share(
        jnp.pad(requested, ((0, -micros % 8), (0, 0))),
        jnp.pad(
            jnp.stack([first_gain, second_gain]).astype(F32), ((0, 6), (0, -own_rows % HEAD_DIM))
        ),
        count,
        shards,
    )
    indices = jnp.moveaxis(indices[:, :micros], 0, 1)
    gains = jnp.moveaxis(gains[:, :2, :own_rows], 0, 1).reshape(2, D)
    full_query = gather(query_weight)
    pair_weights = lax.all_gather(jnp.stack([key_weight, value_weight]), "fsdp", axis=1, tiled=True)
    full_output = gather(output_weight)
    full_gate = gather(gate_weight)
    full_up = gather(up_weight)
    full_down = gather(down_weight)
    gain_one = gains[0:1]
    gain_two = gains[1:2]

    pieces_at = jnp.stack([here, 2 * count - 1 - here])
    positions = (pieces_at[:, None] * HALF + jnp.arange(HALF, dtype=jnp.int32)[None, :]).reshape(ROWS)
    inverse = 10000.0 ** (-jnp.arange(HEAD_DIM // 2, dtype=F32) * 2.0 / HEAD_DIM)
    phase = positions.astype(F32)[:, None] * inverse[None, :]
    cosine = jnp.tile(jnp.cos(phase), (1, 2))
    sine = jnp.sin(phase)
    sine = jnp.concatenate([-sine, sine], axis=1)

    meta, cap = make_meta(indices, partner, cache_keys.shape[1] // BLOCK, count)
    x = tokens.reshape(micros, ROWS, D)
    some = count * 3 // 8
    memory = collect(meta, cache_keys, cache_values, count, cap, range(some))
    x, memory = lax.optimization_barrier((x, memory))
    normed_low, qa, qb = project_query(x, gain_one, full_query, cosine, sine)
    meta, qa, qb = lax.optimization_barrier((meta, qa, qb))
    memory = collect(meta, cache_keys, cache_values, count, cap, range(some, count), memory)
    queries = [(qa, qb)]
    for step in range(1, count):
        qa, qb = lax.ppermute(qa, "ctx", onward), lax.ppermute(qb, "ctx", backward)
        if step == 1:
            qa, qb, memory = lax.optimization_barrier((qa, qb, memory))
        queries.append((qa, qb))
    memory_keys, memory_values = memory
    queries[1], normed_low = lax.optimization_barrier((queries[1], normed_low))
    keys, values, normed_turned = project_pairs(normed_low, pair_weights, cosine, sine)
    for step in range(1, count - 1):
        queries[step], queries[step + 1] = lax.optimization_barrier((queries[step], queries[step + 1]))


    acc = ()
    for step in list(range(1, count)) + [0]:
        pa, pb, ta, tb = attend(
            meta, *queries[step], keys, values, memory_keys, memory_values, step, count, cap
        )
        if acc:
            acc = (lax.ppermute(acc[0], "ctx", onward), lax.ppermute(acc[1], "ctx", backward))
        if step == 0:
            mixed, mixed_low, total, middle, middle_low = finish(
                *acc, pa, pb, ta, tb, x, full_output, gain_two
            )
        else:
            acc = combine(acc, (pa, pb), (ta, tb))

    incoming = cotangent.reshape(micros, ROWS, D)
    layer_output, back_mid_normed, gradient_gate, gradient_up, gradient_down = feed(
        middle_low, incoming, middle, full_gate, full_up, full_down
    )
    da, db, back_middle, back_attn, gain_part = prepare(
        back_mid_normed, middle, incoming, gain_two, full_output, mixed, total
    )

    def scatter(part):
        return lax.psum_scatter(part, "fsdp", scatter_dimension=0, tiled=True)

    slopes = [(da, db)]
    for _ in range(count - 1):
        da, db = slopes[-1]
        slopes.append((lax.ppermute(da, "ctx", onward), lax.ppermute(db, "ctx", backward)))

    slopes[1], back_attn = lax.optimization_barrier((slopes[1], back_attn))
    gradient_output = jnp.einsum(
        "tc,td->cd", mixed_low.reshape(rows, D), back_attn.reshape(rows, D), preferred_element_type=F32
    ).astype(BF16)
    early = [
        scatter(part).reshape(own_rows, -1)
        for part in (gradient_down, gradient_gate, gradient_up, gradient_output)
    ]
    early_width = sum(part.shape[1] for part in early)
    slopes[-1], early[0] = lax.optimization_barrier((slopes[-1], early[0]))
    for step in range(1, count - 1):
        slopes[step], slopes[step + 1] = lax.optimization_barrier((slopes[step], slopes[step + 1]))
    middle_step = count // 2 + 1
    first_sums = key_gradients(meta, keys, values, queries, slopes, range(middle_step))
    slopes[middle_step - 2], first_sums = lax.optimization_barrier((slopes[middle_step - 2], first_sums))
    acc = ()
    for step in range(count):
        part = unattend(
            meta, *queries[step], *slopes[step], keys, values, memory_keys, memory_values, step, count, cap
        )
        if step == 0:
            own = part
            continue
        if acc:
            acc = (lax.ppermute(acc[0], "ctx", onward), lax.ppermute(acc[1], "ctx", backward))
        acc = combine(acc, part)
    back_key, back_value = key_gradients(
        meta, keys, values, queries, slopes, range(middle_step, count), first_sums, (cosine, sine)
    )
    ra, rb = lax.ppermute(acc[0], "ctx", onward), lax.ppermute(acc[1], "ctx", backward)
    early_sum, late_sum, gain_changes, input_gradient = tail(
        (ra, rb),
        own,
        (cosine, sine),
        gain_one,
        gain_part,
        to_chunks(early, count),
        back_key,
        back_value,
        normed_turned,
        (full_query, pair_weights),
        x,
        back_middle,
        count,
        shards,
    )
    early = from_chunks(early_sum, own_rows, early_width).astype(F32)
    three = from_chunks(late_sum, D // shards, 3 * D).astype(F32)
    units = gate_weight.shape[1]
    gain_changes = lax.dynamic_slice_in_dim(
        gain_changes, lax.axis_index("fsdp") * own_rows, own_rows, axis=1
    )
    return (
        layer_output.reshape(tokens.shape),
        input_gradient.reshape(tokens.shape),
        three[:, :D],
        three[:, D : 2 * D],
        three[:, 2 * D :],
        early[:, 3 * units :],
        early[:, units : 2 * units],
        early[:, 2 * units : 3 * units],
        early[:, :units].reshape(down_weight.shape),
        gain_changes[0],
        gain_changes[1],
    )


def solution(mesh):
    split = P("fsdp", "ctx", None, None, None)
    shard = P("fsdp", None)
    return jax.shard_map(
        body,
        mesh=mesh,
        in_specs=(
            split,
            split,
            *([shard] * 7),
            P("fsdp"),
            P("fsdp"),
            P("fsdp", "ctx", None),
            P("fsdp", "ctx", None),
            P("fsdp", "ctx", None, None, None, None),
            P("fsdp"),
        ),
        out_specs=(split, split, *([shard] * 7), P("fsdp"), P("fsdp")),
        check_vma=False,
    )
```

```python
import functools

import jax
import jax.numpy as jnp
from jax import lax
from jax.experimental import pallas as pl
from jax.experimental.pallas import tpu as pltpu
from jax.sharding import PartitionSpec as P

D = 1024
HEADS = 8
HEAD_DIM = 128
HALF = 128
ROWS = 2 * HALF
BLOCK = 64
TOPK = 4
SIDE = HEADS // 2
SW = SIDE * HEAD_DIM
GROUP = 8
EPS = 1e-05
SCALE = HEAD_DIM**-0.5
LOG2E = 1.4426950408889634
F32 = jnp.float32
BF16 = jnp.bfloat16
EXTRA = 16
SENT = ROWS + EXTRA


def nn(a, b):
    return lax.dot_general(a, b, (((1,), (0,)), ((), ())), preferred_element_type=F32)


def nt(a, b):
    return lax.dot_general(a, b, (((1,), (1,)), ((), ())), preferred_element_type=F32)


def tn(a, b):
    return lax.dot_general(a, b, (((0,), (0,)), ((), ())), preferred_element_type=F32)


def params(mib=56):
    return pltpu.CompilerParams(vmem_limit_bytes=mib * 2**20)


def ring_order(count):
    if count == 8:
        return [0, 2, 4, 6, 7, 5, 3, 1]
    half = count // 2
    return list(range(half)) + [count - 1 - i for i in range(count - half)]


def ring_place(count):
    here = lax.axis_index("ctx")
    half = count // 2
    if count == 8:
        turned = here % 2
        return (1 - turned) * (here // 2) + turned * (count - 1 - here // 2)
    turned = here // half
    return (1 - turned) * here + turned * (count - 1 + half - here)


def ring_index(place, count):
    half = count // 2
    place = place % count
    turned = place // half
    if count == 8:
        return (1 - turned) * 2 * place + turned * (2 * count - 1 - 2 * place)
    return (1 - turned) * place + turned * (count - 1 + half - place)


def ring_pairs(count):
    order = ring_order(count)
    onward = [(order[i], order[(i + 1) % count]) for i in range(count)]
    return onward, [(b, a) for a, b in onward]


def list_base(count):
    return 1 + 2 * count


def list_at(owner, micro, side, micros, cap):
    return ((owner * micros + micro) * 2 + side) * (cap + 1)


def make_meta(indices, partner, cb_dev, count):
    micros = indices.shape[0]
    here = lax.axis_index("ctx")
    order = ring_order(count)
    place = ring_place(count)
    steps = jnp.arange(count, dtype=jnp.int32)
    at = jnp.stack([(place - steps) % count, (place + steps) % count], axis=1)
    owners = sum(jnp.where(at == p, d, 0) for p, d in enumerate(order))
    blocks = cb_dev * count
    cap = 2 * 128 // count
    side_shape = (micros, count, 2 * ROWS // (2 * BLOCK), 2, SIDE, TOPK)
    index = indices.reshape(side_shape).transpose(1, 0, 3, 2, 4, 5)
    index = index.reshape(count, micros, 2, -1)
    number = index % blocks
    mine = (number // cb_dev) == here
    own = jnp.arange(micros, dtype=jnp.int32)[None, :, None, None]
    document = jnp.where(index < blocks, own, partner[None, :, None, None])
    entries = index.shape[-1]
    entry = jnp.arange(entries, dtype=jnp.int32)
    query_block = entry // (SIDE * TOPK)
    head = entry // TOPK % SIDE
    code = ((document * cb_dev + number % cb_dev) * 4 + query_block) * SIDE + head
    before = (entry[:, None] < entry[None, :]).astype(F32)
    flags = mine.astype(F32)
    rank = jnp.dot(flags.reshape(-1, entries), before, preferred_element_type=F32).reshape(flags.shape)
    rank = rank.astype(jnp.int32)
    slot = jnp.arange(cap, dtype=jnp.int32)
    hit = mine[..., None, :] & (rank[..., None, :] == slot[:, None])
    codes = jnp.sum(jnp.where(hit, code[..., None, :], 0), axis=-1)
    length = jnp.sum(mine.astype(jnp.int32), axis=-1, keepdims=True)
    lists = jnp.concatenate([length, codes], axis=-1).reshape(-1)
    return jnp.concatenate([here.reshape(1), owners.reshape(-1), lists]).astype(jnp.int32), cap


def share_kernel(indices, gains, all_indices, all_gains, send_sem, recv_sem, *, count, shards):
    here, shard = lax.axis_index("ctx"), lax.axis_index("fsdp")
    groups = (("ctx", here, count, indices, all_indices), ("fsdp", shard, shards, gains, all_gains))
    barrier = pltpu.get_barrier_semaphore()
    for axis, index, size, _, _ in groups:
        for k in range(1, size):
            pl.semaphore_signal(
                barrier, inc=1, device_id={axis: (index + k) % size}, device_id_type=pl.DeviceIdType.MESH
            )
    pl.semaphore_wait(barrier, count + shards - 2)
    copies = []
    for number, (axis, index, size, source, target) in enumerate(groups):
        for k in range(1, size):
            copy = pltpu.make_async_remote_copy(
                source,
                target.at[index],
                send_sem.at[number, k],
                recv_sem.at[number, k],
                device_id={axis: (index + k) % size},
                device_id_type=pl.DeviceIdType.MESH,
            )
            copy.start()
            copies.append(copy)
        target[index] = source[...]
    for copy in copies:
        copy.wait()


def share(indices, gains, count, shards):
    vmem = pl.BlockSpec(memory_space=pltpu.VMEM)
    most = max(count, shards)
    return pl.pallas_call(
        functools.partial(share_kernel, count=count, shards=shards),
        in_specs=[vmem, vmem],
        out_specs=[vmem, vmem],
        out_shape=[
            jax.ShapeDtypeStruct((count,) + indices.shape, indices.dtype),
            jax.ShapeDtypeStruct((shards,) + gains.shape, gains.dtype),
        ],
        scratch_shapes=[pltpu.SemaphoreType.DMA((2, most)), pltpu.SemaphoreType.DMA((2, most))],
        compiler_params=pltpu.CompilerParams(
            vmem_limit_bytes=8 * 2**20, collective_id=1, has_side_effects=True
        ),
        name="share",
        cost_estimate=pl.CostEstimate(flops=0, bytes_accessed=20_000_000, transcendentals=0),
    )(indices, gains)


def collect_kernel(meta, ck, cv, *refs, micros, count, cap, first):
    mk, mv, sem_k, sem_v = refs[-4:]
    owner = pl.program_id(0) + first

    def list_of(i):
        base = list_base(count) + (owner * 2 * micros + i) * (cap + 1)
        return base, meta[base]

    def start(i, carry):
        base, length = list_of(i)

        def one(j, c):
            code = meta[base + 1 + j]
            head = (i & 1) * SIDE + (code & (SIDE - 1))
            rows = pl.ds(pl.multiple_of((code >> 4) << 6, BLOCK), BLOCK)
            cols = pl.ds(pl.multiple_of(head << 7, HEAD_DIM), HEAD_DIM)
            pltpu.make_async_copy(ck.at[rows, cols], mk.at[i >> 1, 0, i & 1, j], sem_k).start()
            pltpu.make_async_copy(cv.at[rows, cols], mv.at[i >> 1, 0, i & 1, j], sem_v).start()
            return c

        def clear(j, c):
            mk[i >> 1, 0, i & 1, j] = jnp.zeros((BLOCK, HEAD_DIM), BF16)
            mv[i >> 1, 0, i & 1, j] = jnp.zeros((BLOCK, HEAD_DIM), BF16)
            return c

        lax.fori_loop(0, length, one, carry)
        return lax.fori_loop(length, (length + GROUP - 1) // GROUP * GROUP, clear, carry)

    def finish(i, carry):
        _, length = list_of(i)
        rounds = length // GROUP

        def many(g, c):
            some = pl.ds(g * GROUP, GROUP)
            for place, sem in ((mk, sem_k), (mv, sem_v)):
                whole = place.at[i >> 1, 0, i & 1, some]
                pltpu.make_async_copy(whole, whole, sem).wait()
            return c

        def one(j, c):
            for place, sem in ((mk, sem_k), (mv, sem_v)):
                whole = place.at[i >> 1, 0, i & 1, j]
                pltpu.make_async_copy(whole, whole, sem).wait()
            return c

        lax.fori_loop(0, rounds, many, carry)
        return lax.fori_loop(rounds * GROUP, length, one, carry)

    lax.fori_loop(0, 2 * micros, start, 0)
    lax.fori_loop(0, 2 * micros, finish, 0)


def collect(meta, cache_keys, cache_values, count, cap, owners, into=()):
    micros = cache_keys.shape[0]
    shape = jax.ShapeDtypeStruct((micros, count, 2, cap, BLOCK, HEAD_DIM), BF16)
    anywhere = pl.BlockSpec(memory_space=pl.ANY)
    block = pl.BlockSpec((micros, 1, 2, cap, BLOCK, HEAD_DIM), lambda o, meta: (0, o + owners.start, 0, 0, 0, 0))
    return pl.pallas_call(
        functools.partial(collect_kernel, micros=micros, count=count, cap=cap, first=owners.start),
        grid_spec=pltpu.PrefetchScalarGridSpec(
            num_scalar_prefetch=1,
            grid=(len(owners),),
            in_specs=[anywhere, anywhere] + [anywhere] * len(into),
            out_specs=[block, block],
            scratch_shapes=[pltpu.SemaphoreType.DMA, pltpu.SemaphoreType.DMA],
        ),
        out_shape=[shape, shape],
        input_output_aliases={3: 0, 4: 1} if into else {},
        compiler_params=params(),
        name="collect",
        cost_estimate=pl.CostEstimate(
            flops=0, bytes_accessed=11_000_000 * len(owners), transcendentals=0
        ),
    )(meta, cache_keys.reshape(-1, D), cache_values.reshape(-1, D), *into)


def turn(value, cosine, sine):
    return value * cosine + pltpu.roll(value, HEAD_DIM // 2, 1) * sine


def first_kernel(x, gain, weight, cosine, sine, normed, qa, qb):
    value = x[0].astype(F32)
    scale = lax.rsqrt(jnp.mean(value * value, axis=-1, keepdims=True) + EPS)
    low = (value * scale * gain[...]).astype(BF16)
    normed[0] = low
    product = nn(low, weight[...])
    for h in range(HEADS):
        cols = slice(h * HEAD_DIM, (h + 1) * HEAD_DIM)
        out = qa if h < SIDE else qb
        place = slice((h % SIDE) * HEAD_DIM, (h % SIDE + 1) * HEAD_DIM)
        out[0, :, place] = turn(product[:, cols], cosine[...], sine[...]).astype(BF16)


def second_kernel(normed, weights, cosine, sine, keys, values, turned):
    low = normed[0]
    turned[...] = low.T
    product = nn(low, weights[0])
    for h in range(HEADS):
        cols = slice(h * HEAD_DIM, (h + 1) * HEAD_DIM)
        keys[0, :, cols] = turn(product[:, cols], cosine[...], sine[...]).astype(BF16)
    values[0] = nn(low, weights[1]).astype(BF16)


def seq_spec(*shape):
    return pl.BlockSpec((1,) + shape, lambda m, *_: (m,) + (0,) * len(shape))


def full_spec(*shape):
    return pl.BlockSpec(shape, lambda m, *_: (0,) * len(shape))


def seq_shape(micros, *shape, dtype=BF16):
    return jax.ShapeDtypeStruct((micros,) + shape, dtype)


def project_query(x, gain, weight, cosine, sine):
    micros = x.shape[0]
    return pl.pallas_call(
        first_kernel,
        grid=(micros,),
        in_specs=[
            seq_spec(ROWS, D),
            full_spec(1, D),
            full_spec(D, D),
            full_spec(ROWS, HEAD_DIM),
            full_spec(ROWS, HEAD_DIM),
        ],
        out_specs=[seq_spec(ROWS, D), seq_spec(ROWS, SW), seq_spec(ROWS, SW)],
        out_shape=[seq_shape(micros, ROWS, D), seq_shape(micros, ROWS, SW), seq_shape(micros, ROWS, SW)],
        compiler_params=params(),
        name="project_query",
        cost_estimate=pl.CostEstimate(flops=2 * micros * ROWS * D * D, bytes_accessed=8_000_000, transcendentals=0),
    )(x, gain, weight, cosine, sine)


def project_pairs(normed, weights, cosine, sine):
    micros = normed.shape[0]
    return pl.pallas_call(
        second_kernel,
        grid=(micros,),
        in_specs=[
            seq_spec(ROWS, D),
            full_spec(2, D, D),
            full_spec(ROWS, HEAD_DIM),
            full_spec(ROWS, HEAD_DIM),
        ],
        out_specs=[seq_spec(ROWS, D), seq_spec(ROWS, D), pl.BlockSpec((D, ROWS), lambda m: (0, m))],
        out_shape=[
            seq_shape(micros, ROWS, D),
            seq_shape(micros, ROWS, D),
            jax.ShapeDtypeStruct((D, micros * ROWS), BF16),
        ],
        compiler_params=params(),
        name="project_pairs",
        cost_estimate=pl.CostEstimate(flops=4 * micros * ROWS * D * D, bytes_accessed=10_000_000, transcendentals=0),
    )(normed, weights, cosine, sine)


def causal_mask(turned=False):
    row = lax.broadcasted_iota(jnp.int32, (ROWS, ROWS), 0)
    col = lax.broadcasted_iota(jnp.int32, (ROWS, ROWS), 1)
    return row <= col if turned else row >= col


def to_lanes(wide):
    lane = lax.broadcasted_iota(jnp.int32, (ROWS, HEAD_DIM), 1)
    packed = jnp.zeros((ROWS, HEAD_DIM), F32)
    for h in range(SIDE):
        packed = jnp.where(lane == h, wide[:, h * HEAD_DIM : (h + 1) * HEAD_DIM], packed)
    return packed.T[:8]


def to_columns(lanes):
    return jnp.concatenate([lanes, jnp.zeros((HEAD_DIM - 8, ROWS), F32)], axis=0).T


def split3(value):
    high = value.astype(BF16).astype(F32)
    middle = (value - high).astype(BF16).astype(F32)
    return high, middle, value - high - middle


def pack_lanes(lanes):
    high, middle, low = split3(lanes)
    rows = jnp.concatenate(
        [jnp.concatenate([high, middle], axis=1), jnp.concatenate([low, jnp.zeros_like(low)], axis=1)],
        axis=0,
    )
    return rows.astype(BF16)


def unpack_lanes(rows):
    value = rows.astype(F32)
    return value[:8, :ROWS] + value[:8, ROWS:] + value[8:, :ROWS]


def requests(meta, mk, mv, kbuf, vbuf, sem, micro, act, *, step, count, cap, micros):
    slot = micro % 2
    for side in range(2):
        owner = meta[1 + 2 * step + side]
        length = meta[list_base(count) + list_at(owner, micro, side, micros, cap)]

        def one(g, carry):
            some = pl.ds(g * GROUP, GROUP)
            for source, place in ((mk, kbuf), (mv, vbuf)):
                copy = pltpu.make_async_copy(
                    source.at[micro, owner, side, some], place.at[slot, side, some], sem.at[slot]
                )
                if act == "start":
                    copy.start()
                else:
                    copy.wait()
            return carry

        lax.fori_loop(0, (length + GROUP - 1) // GROUP, one, 0)


def request_ahead(fetch, micro, micros):
    @pl.when(micro == 0)
    def _():
        fetch(micro, "start")

    @pl.when(micro + 1 < micros)
    def _():
        fetch(micro + 1, "start")


def request_scratch(cap):
    return [
        pltpu.VMEM((2, 2, cap, BLOCK, HEAD_DIM), BF16),
        pltpu.VMEM((2, 2, cap, BLOCK, HEAD_DIM), BF16),
        pltpu.SemaphoreType.DMA((2,)),
    ]


EVERYTHING, LOW, HIGH = slice(0, ROWS), slice(0, HALF), slice(HALF, ROWS)


def tiles(side):
    return [
        (
            slice(h * HEAD_DIM, (h + 1) * HEAD_DIM),
            slice((side * SIDE + h) * HEAD_DIM, (side * SIDE + h + 1) * HEAD_DIM),
        )
        for h in range(SIDE)
    ]


def forward_kernel(
    meta, qa, qb, k, v, mk, mv, pa, pb, ta, tb, part, wide, kbuf, vbuf, sem, *, step, count, cap, micros
):
    micro = pl.program_id(0)
    here = meta[0]
    fetch = functools.partial(
        requests, meta, mk, mv, kbuf, vbuf, sem, step=step, count=count, cap=cap, micros=micros
    )
    request_ahead(fetch, micro, micros)
    for side, q in enumerate((qa, qb)):
        owner = meta[1 + 2 * step + side]

        def local(qrows, krows, masked):
            spots = tiles(side)
            scores = [nt(q[0, qrows, cols], k[0, krows, kcols]) for cols, kcols in spots]
            weights = [jnp.exp2(score * (SCALE * LOG2E)) for score in scores]
            if masked:
                weights = [jnp.where(causal_mask(), weight, 0.0) for weight in weights]
            for weight, (cols, kcols) in zip(weights, spots):
                values = v[0, krows, kcols]
                more = jnp.concatenate([values, jnp.ones_like(values)], axis=1)
                out = nn(weight.astype(BF16), more)
                part[qrows, kcols] = out[:, :HEAD_DIM]
                wide[qrows, kcols] = out[:, HEAD_DIM:]

        if step == 0:
            local(EVERYTHING, EVERYTHING, True)
        else:

            @pl.when(owner < here)
            def _():
                zeros = jnp.zeros((HALF, SW), F32)
                part[LOW, side * SW : (side + 1) * SW] = zeros
                wide[LOW, side * SW : (side + 1) * SW] = zeros
                local(HIGH, EVERYTHING, False)

            @pl.when(owner > here)
            def _():
                local(EVERYTHING, LOW, False)

    fetch(micro, "wait")
    slot = micro % 2
    for side, (q, out, total) in enumerate(((qa, pa, ta), (qb, pb, tb))):
        owner = meta[1 + 2 * step + side]
        base = list_base(count) + list_at(owner, micro, side, micros, cap)
        length = meta[base]

        def group(i, carry):
            numbers = [i * GROUP + j for j in range(GROUP)]
            places = [request_place(meta[base + 1 + number]) for number in numbers]
            scores = [
                nt(q[0, rows, cols], kbuf[slot, side, number])
                for number, (rows, cols) in zip(numbers, places)
            ]
            weights = [
                jnp.where(number < length, jnp.exp2(score * (SCALE * LOG2E)), 0.0).astype(BF16)
                for number, score in zip(numbers, scores)
            ]
            outs = []
            for number, weight in zip(numbers, weights):
                values = vbuf[slot, side, number]
                outs.append(nn(weight, jnp.concatenate([values, jnp.ones_like(values)], axis=1)))
            for o, (rows, cols) in zip(outs, places):
                cols = pl.ds(pl.multiple_of(cols.start + side * SW, HEAD_DIM), HEAD_DIM)
                part[rows, cols] += o[:, :HEAD_DIM]
                wide[rows, cols] += o[:, HEAD_DIM:]
            return carry

        lax.fori_loop(0, (length + GROUP - 1) // GROUP, group, 0)
        out[0] = part[:, side * SW : (side + 1) * SW].astype(BF16)
        total[0] = to_lanes(wide[:, side * SW : (side + 1) * SW])


def request_place(code):
    return (
        pl.ds(pl.multiple_of(((code >> 2) & 3) << 6, BLOCK), BLOCK),
        pl.ds(pl.multiple_of((code & 3) << 7, HEAD_DIM), HEAD_DIM),
    )


def attend(meta, qa, qb, keys, values, memory_keys, memory_values, step, count, cap):
    micros = qa.shape[0]
    half, whole, lanes = seq_spec(ROWS, SW), seq_spec(ROWS, D), seq_spec(8, ROWS)
    anywhere = pl.BlockSpec(memory_space=pl.ANY)
    return pl.pallas_call(
        functools.partial(forward_kernel, step=step, count=count, cap=cap, micros=micros),
        grid_spec=pltpu.PrefetchScalarGridSpec(
            num_scalar_prefetch=1,
            grid=(micros,),
            in_specs=[half, half, whole, whole, anywhere, anywhere],
            out_specs=[half, half, lanes, lanes],
            scratch_shapes=[pltpu.VMEM((ROWS, D), F32), pltpu.VMEM((ROWS, D), F32)]
            + request_scratch(cap),
        ),
        out_shape=[
            seq_shape(micros, ROWS, SW),
            seq_shape(micros, ROWS, SW),
            seq_shape(micros, 8, ROWS, dtype=F32),
            seq_shape(micros, 8, ROWS, dtype=F32),
        ],
        compiler_params=params(24),
        name="attend",
        cost_estimate=pl.CostEstimate(flops=6_000_000_000, bytes_accessed=10_000_000, transcendentals=0),
    )(meta, qa, qb, keys, values, memory_keys, memory_values)


def combine_kernel(*refs, carried, sums):
    refs = list(refs)
    received = [refs.pop(0), refs.pop(0)] if carried else [None, None]
    parts = [refs.pop(0), refs.pop(0)]
    totals = [refs.pop(0), refs.pop(0)] if sums else [None, None]
    for got, part, total, out in zip(received, parts, totals, refs):
        value = part[0].astype(F32)
        if carried:
            value = value + got[0, :ROWS].astype(F32)
        out[0, :ROWS] = value.astype(BF16)
        if sums:
            lanes = total[0]
            if carried:
                lanes = lanes + unpack_lanes(got[0, ROWS:])
            out[0, ROWS:] = pack_lanes(lanes)


def combine(received, parts, totals=()):
    micros = parts[0].shape[0]
    sent = SENT if totals else ROWS
    half, lanes, packed = seq_spec(ROWS, SW), seq_spec(8, ROWS), seq_spec(sent, SW)
    return pl.pallas_call(
        functools.partial(combine_kernel, carried=bool(received), sums=bool(totals)),
        grid=(micros,),
        in_specs=[packed] * len(received) + [half] * 2 + [lanes] * len(totals),
        out_specs=[packed, packed],
        out_shape=[seq_shape(micros, sent, SW)] * 2,
        compiler_params=params(16),
        name="combine",
        cost_estimate=pl.CostEstimate(flops=2_000_000, bytes_accessed=7_000_000, transcendentals=0),
    )(*received, *parts, *totals)


def finish_kernel(acc_a, acc_b, pa, pb, ta, tb, x, weight, gain, mixed, low, total, middle, normed):
    for side, (acc, part, own) in enumerate(((acc_a, pa, ta), (acc_b, pb, tb))):
        lanes = unpack_lanes(acc[0, ROWS:]) + own[0]
        total[0, side] = lanes
        columns = to_columns(lanes)
        for h in range(SIDE):
            cols = slice(h * HEAD_DIM, (h + 1) * HEAD_DIM)
            place = slice((side * SIDE + h) * HEAD_DIM, (side * SIDE + h + 1) * HEAD_DIM)
            weighted = acc[0, :ROWS, cols].astype(F32) + part[0, :, cols].astype(F32)
            value = weighted / columns[:, h : h + 1]
            mixed[0, :, place] = value
            low[0, :, place] = value.astype(BF16)
    value = x[0].astype(F32) + nn(low[0], weight[...])
    middle[0] = value
    scale = lax.rsqrt(jnp.mean(value * value, axis=-1, keepdims=True) + EPS)
    normed[0] = (value * scale * gain[...]).astype(BF16)


def finish(acc_a, acc_b, pa, pb, ta, tb, x, weight, gain):
    micros = acc_a.shape[0]
    packed, half, lanes = seq_spec(SENT, SW), seq_spec(ROWS, SW), seq_spec(8, ROWS)
    whole = seq_spec(ROWS, D)
    return pl.pallas_call(
        finish_kernel,
        grid=(micros,),
        in_specs=[packed, packed, half, half, lanes, lanes, whole, full_spec(D, D), full_spec(1, D)],
        out_specs=[whole, whole, seq_spec(2, 8, ROWS), whole, whole],
        out_shape=[
            seq_shape(micros, ROWS, D, dtype=F32),
            seq_shape(micros, ROWS, D),
            seq_shape(micros, 2, 8, ROWS, dtype=F32),
            seq_shape(micros, ROWS, D, dtype=F32),
            seq_shape(micros, ROWS, D),
        ],
        compiler_params=params(),
        name="finish",
        cost_estimate=pl.CostEstimate(flops=2 * micros * ROWS * D * D, bytes_accessed=16_000_000, transcendentals=0),
    )(acc_a, acc_b, pa, pb, ta, tb, x, weight, gain)


TILE = 256


def feed_kernel(
    normed, incoming, middle, gate_weight, up_weight, down_weight, out, back, dg, du, dd, turned, acc, hid, bg, bu
):
    step = pl.program_id(0)
    micros = normed.shape[0]

    @pl.when(step == 0)
    def _():
        for m in range(micros):
            turned[:, m * ROWS : (m + 1) * ROWS] = normed[m].T
            acc[m] = middle[m]
            back[m] = jnp.zeros((ROWS, D), F32)

    wg, wu, wd = gate_weight[...], up_weight[...], down_weight[...]
    for m in range(micros):
        rows = slice(m * ROWS, (m + 1) * ROWS)
        gate = nn(normed[m], wg)
        upper = nn(normed[m], wu)
        slope = nt(incoming[m], wd)
        sigma = 1.0 / (1.0 + jnp.exp(-gate))
        silu = gate * sigma
        hid[rows] = (silu * upper).astype(BF16)
        bg[rows] = (slope * upper * (sigma * (1.0 + gate * (1.0 - sigma)))).astype(BF16)
        bu[rows] = (slope * silu).astype(BF16)
        acc[m] += nn(hid[rows], wd)
        back[m] += nt(bg[rows], wg) + nt(bu[rows], wu)
    dg[...] = nn(turned[...], bg[...]).astype(BF16)
    du[...] = nn(turned[...], bu[...]).astype(BF16)
    dd[...] = tn(hid[...], incoming[...].reshape(micros * ROWS, D)).astype(BF16)

    @pl.when(step == pl.num_programs(0) - 1)
    def _():
        out[...] = acc[...].astype(BF16)


def feed(normed, incoming, middle, gate_weight, up_weight, down_weight):
    micros = normed.shape[0]
    units = gate_weight.shape[1]
    whole = full_spec(micros, ROWS, D)
    wide = pl.BlockSpec((D, TILE), lambda f: (0, f))
    tall = pl.BlockSpec((TILE, D), lambda f: (f, 0))
    return pl.pallas_call(
        feed_kernel,
        grid=(units // TILE,),
        in_specs=[whole, whole, whole, wide, wide, tall],
        out_specs=[whole, whole, wide, wide, tall],
        out_shape=[
            seq_shape(micros, ROWS, D),
            seq_shape(micros, ROWS, D, dtype=F32),
            jax.ShapeDtypeStruct((D, units), BF16),
            jax.ShapeDtypeStruct((D, units), BF16),
            jax.ShapeDtypeStruct((units, D), BF16),
        ],
        scratch_shapes=[
            pltpu.VMEM((D, micros * ROWS), BF16),
            pltpu.VMEM((micros, ROWS, D), F32),
            pltpu.VMEM((micros * ROWS, TILE), BF16),
            pltpu.VMEM((micros * ROWS, TILE), BF16),
            pltpu.VMEM((micros * ROWS, TILE), BF16),
        ],
        compiler_params=params(),
        name="feed",
        cost_estimate=pl.CostEstimate(
            flops=18 * micros * ROWS * D * units, bytes_accessed=50_000_000, transcendentals=0
        ),
    )(normed, incoming, middle, gate_weight, up_weight, down_weight)


def prepare_kernel(back_normed, middle, incoming, gain, weight, mixed, total, da, db, back_middle, back_attn, dgain):
    value = middle[0]
    scale = lax.rsqrt(jnp.mean(value * value, axis=-1, keepdims=True) + EPS)
    hat = value * scale
    slope = back_normed[0] * gain[...]
    slope = incoming[0].astype(F32) + scale * (
        slope - hat * jnp.mean(slope * hat, axis=-1, keepdims=True)
    )
    back_middle[0] = slope
    back_attn[0] = slope.astype(BF16)
    dgain[0] = jnp.sum((back_normed[0] * hat).reshape(ROWS // 8, 8, D), axis=0)
    lane = lax.broadcasted_iota(jnp.int32, (ROWS, HEAD_DIM), 1)
    for side, out in enumerate((da, db)):
        columns = to_columns(total[0, side])
        packed = jnp.zeros((ROWS, HEAD_DIM), F32)
        back = nt(back_attn[0], weight[side * SW : (side + 1) * SW, :])
        for h in range(SIDE):
            cols = slice(h * HEAD_DIM, (h + 1) * HEAD_DIM)
            place = slice((side * SIDE + h) * HEAD_DIM, (side * SIDE + h + 1) * HEAD_DIM)
            part = back[:, cols]
            divisor = columns[:, h : h + 1]
            out[0, :ROWS, cols] = (part / divisor).astype(BF16)
            product = jnp.sum(part * mixed[0, :, place], axis=1, keepdims=True)
            packed = jnp.where(lane == h, -product / divisor, packed)
        out[0, ROWS:] = pack_lanes(packed.T[:8])


def prepare(back_normed, middle, incoming, gain, weight, mixed, total):
    micros = middle.shape[0]
    whole = seq_spec(ROWS, D)
    return pl.pallas_call(
        prepare_kernel,
        grid=(micros,),
        in_specs=[whole, whole, whole, full_spec(1, D), full_spec(D, D), whole, seq_spec(2, 8, ROWS)],
        out_specs=[seq_spec(SENT, SW), seq_spec(SENT, SW), whole, whole, seq_spec(8, D)],
        out_shape=[
            seq_shape(micros, SENT, SW),
            seq_shape(micros, SENT, SW),
            seq_shape(micros, ROWS, D, dtype=F32),
            seq_shape(micros, ROWS, D),
            seq_shape(micros, 8, D, dtype=F32),
        ],
        compiler_params=params(),
        name="prepare",
        cost_estimate=pl.CostEstimate(flops=2 * micros * ROWS * D * D, bytes_accessed=22_000_000, transcendentals=0),
    )(back_normed, middle, incoming, gain, weight, mixed, total)


def backward_kernel(
    meta, qa, qb, da, db, k, v, mk, mv, dqa, dqb, part, wide, kbuf, vbuf, sem, *, step, count, cap, micros
):
    micro = pl.program_id(0)
    here = meta[0]
    fetch = functools.partial(
        requests, meta, mk, mv, kbuf, vbuf, sem, step=step, count=count, cap=cap, micros=micros
    )
    request_ahead(fetch, micro, micros)
    for side, (q, d) in enumerate(((qa, da), (qb, db))):
        owner = meta[1 + 2 * step + side]
        columns = to_columns(unpack_lanes(d[0, ROWS:]))
        for h, (_, place) in enumerate(tiles(side)):
            wide[:, place] = jnp.broadcast_to(columns[:, h : h + 1], (ROWS, HEAD_DIM))

        def local(qrows, krows, masked):
            spots = tiles(side)
            scores = [nt(q[0, qrows, cols], k[0, krows, kcols]) for cols, kcols in spots]
            slopes = [nt(d[0, qrows, cols], v[0, krows, kcols]) for cols, kcols in spots]
            weights = [jnp.exp2(score * (SCALE * LOG2E)) for score in scores]
            if masked:
                weights = [jnp.where(causal_mask(), weight, 0.0) for weight in weights]
            slopes = [
                (weight * (slope + wide[qrows, kcols][:, :1])).astype(BF16)
                for weight, slope, (_, kcols) in zip(weights, slopes, spots)
            ]
            for slope, (_, kcols) in zip(slopes, spots):
                part[qrows, kcols] = nn(slope, k[0, krows, kcols])

        if step == 0:
            local(EVERYTHING, EVERYTHING, True)
        else:

            @pl.when(owner < here)
            def _():
                part[LOW, side * SW : (side + 1) * SW] = jnp.zeros((HALF, SW), F32)
                local(HIGH, EVERYTHING, False)

            @pl.when(owner > here)
            def _():
                local(EVERYTHING, LOW, False)

    fetch(micro, "wait")
    slot = micro % 2
    for side, (q, d, out) in enumerate(((qa, da, dqa), (qb, db, dqb))):
        owner = meta[1 + 2 * step + side]
        base = list_base(count) + list_at(owner, micro, side, micros, cap)
        length = meta[base]

        def group(i, carry):
            numbers = [i * GROUP + j for j in range(GROUP)]
            places = [request_place(meta[base + 1 + number]) for number in numbers]
            shifted = [
                (rows, pl.ds(pl.multiple_of(cols.start + side * SW, HEAD_DIM), HEAD_DIM))
                for rows, cols in places
            ]
            scores = [
                nt(q[0, rows, cols], kbuf[slot, side, number])
                for number, (rows, cols) in zip(numbers, places)
            ]
            slopes = [
                nt(d[0, rows, cols], vbuf[slot, side, number])
                for number, (rows, cols) in zip(numbers, places)
            ]
            weights = [jnp.exp2(score * (SCALE * LOG2E)) for score in scores]
            slopes = [
                jnp.where(
                    number < length, weight * (slope + wide[rows, cols][:, :BLOCK]), 0.0
                ).astype(BF16)
                for number, weight, slope, (rows, cols) in zip(numbers, weights, slopes, shifted)
            ]
            outs = [nn(slope, kbuf[slot, side, number]) for number, slope in zip(numbers, slopes)]
            for o, (rows, cols) in zip(outs, shifted):
                part[rows, cols] += o
            return carry

        lax.fori_loop(0, (length + GROUP - 1) // GROUP, group, 0)
        out[0] = part[:, side * SW : (side + 1) * SW].astype(BF16)


def unattend(meta, qa, qb, da, db, keys, values, memory_keys, memory_values, step, count, cap):
    micros = qa.shape[0]
    half, packed, whole = seq_spec(ROWS, SW), seq_spec(SENT, SW), seq_spec(ROWS, D)
    anywhere = pl.BlockSpec(memory_space=pl.ANY)
    return pl.pallas_call(
        functools.partial(backward_kernel, step=step, count=count, cap=cap, micros=micros),
        grid_spec=pltpu.PrefetchScalarGridSpec(
            num_scalar_prefetch=1,
            grid=(micros,),
            in_specs=[half, half, packed, packed, whole, whole, anywhere, anywhere],
            out_specs=[half, half],
            scratch_shapes=[pltpu.VMEM((ROWS, D), F32), pltpu.VMEM((ROWS, D), F32)]
            + request_scratch(cap),
        ),
        out_shape=[seq_shape(micros, ROWS, SW), seq_shape(micros, ROWS, SW)],
        compiler_params=params(24),
        name="unattend",
        cost_estimate=pl.CostEstimate(flops=8_000_000_000, bytes_accessed=12_000_000, transcendentals=0),
    )(meta, qa, qb, da, db, keys, values, memory_keys, memory_values)


def key_kernel(meta, k, v, *refs, steps, micros, last):
    number = len(steps)
    sources, refs = refs[: 4 * number], refs[4 * number :]
    if last:
        dk_first, dv_first, cosine, sine, back_key, back_value, dk, dv, qbuf, dbuf, sem = refs
    else:
        dk, dv, qbuf, dbuf, sem = refs
    micro = pl.program_id(0)
    here = meta[0]

    def fetch(m, act):
        slot = m % 2
        for i in range(number):
            for side in range(2):
                for source, place in (
                    (sources[4 * i + side], qbuf.at[slot, side, i]),
                    (sources[4 * i + 2 + side], dbuf.at[slot, side, i]),
                ):
                    copy = pltpu.make_async_copy(source.at[m], place, sem.at[slot])
                    if act == "start":
                        copy.start()
                    else:
                        copy.wait()

    request_ahead(fetch, micro, micros)
    fetch(micro, "wait")
    dk[0] = dk_first[0] if last else jnp.zeros((ROWS, D), F32)
    dv[0] = dv_first[0] if last else jnp.zeros((ROWS, D), F32)
    slot = micro % 2
    for side in range(2):
        spots = tiles(side)

        def one(i, step, own):
            q, d = qbuf.at[slot, side, i], dbuf.at[slot, side, i]
            shift = unpack_lanes(d[ROWS:, :])

            def local(qrows, krows, masked):
                scores = [nt(k[0, krows, kcols], q[qrows, cols]) for cols, kcols in spots]
                slopes = [nt(v[0, krows, kcols], d[qrows, cols]) for cols, kcols in spots]
                weights = [jnp.exp2(score * (SCALE * LOG2E)) for score in scores]
                if masked:
                    weights = [jnp.where(causal_mask(True), weight, 0.0) for weight in weights]
                slopes = [
                    (weight * (slope + shift[h : h + 1, qrows])).astype(BF16)
                    for h, (weight, slope) in enumerate(zip(weights, slopes))
                ]
                for weight, slope, (cols, kcols) in zip(weights, slopes, spots):
                    dk[0, krows, kcols] += nn(slope, q[qrows, cols])
                    dv[0, krows, kcols] += nn(weight.astype(BF16), d[qrows, cols])

            if own:
                local(EVERYTHING, EVERYTHING, True)
                return
            owner = meta[1 + 2 * step + side]

            @pl.when(owner < here)
            def _():
                local(HIGH, EVERYTHING, False)

            @pl.when(owner > here)
            def _():
                local(EVERYTHING, LOW, False)

        first = 0
        if steps[0] == 0:
            one(0, 0, True)
            first = 1

        def loop(i, carry):
            one(i, steps[0] + i, False)
            return carry

        lax.fori_loop(first, number, loop, 0)
    if last:
        for h in range(HEADS):
            cols = slice(h * HEAD_DIM, (h + 1) * HEAD_DIM)
            back_key[0, :, cols] = turn(dk[0, :, cols] * SCALE, cosine[...], -sine[...]).astype(BF16)
        back_value[0] = dv[0].astype(BF16)


def key_gradients(meta, keys, values, queries, slopes, steps, first=(), angle=()):
    micros = keys.shape[0]
    whole = seq_spec(ROWS, D)
    anywhere = pl.BlockSpec(memory_space=pl.ANY)
    sources = []
    for step in steps:
        sources += [*queries[step], *slopes[step]]
    last = bool(first)
    sum_scratch = [pltpu.VMEM((1, ROWS, D), F32)] * 2 if last else []
    return pl.pallas_call(
        functools.partial(key_kernel, steps=steps, micros=micros, last=last),
        grid_spec=pltpu.PrefetchScalarGridSpec(
            num_scalar_prefetch=1,
            grid=(micros,),
            in_specs=[whole, whole]
            + [anywhere] * len(sources)
            + [whole] * len(first)
            + [full_spec(ROWS, HEAD_DIM)] * len(angle),
            out_specs=[whole, whole],
            scratch_shapes=sum_scratch
            + [
                pltpu.VMEM((2, 2, len(steps), ROWS, SW), BF16),
                pltpu.VMEM((2, 2, len(steps), SENT, SW), BF16),
                pltpu.SemaphoreType.DMA((2,)),
            ],
        ),
        out_shape=[seq_shape(micros, ROWS, D, dtype=BF16 if last else F32)] * 2,
        compiler_params=params(40),
        name="key_gradients",
        cost_estimate=pl.CostEstimate(
            flops=3_000_000_000 * len(steps), bytes_accessed=20_000_000, transcendentals=0
        ),
    )(meta, keys, values, *sources, *first, *angle)


def bits(size):
    return [1 << i for i in range(size.bit_length() - 1)]


def by_rows(rows, chunks):
    return rows % (16 * chunks) == 0


PIECE = 512


def tail_kernel(
    acc_a,
    acc_b,
    part_a,
    part_b,
    cosine,
    sine,
    gain,
    second,
    *rest,
    count,
    shards,
    parts,
):
    early_far, rest = rest[:parts], rest[parts:]
    tail_work(
        acc_a, acc_b, part_a, part_b, cosine, sine, gain, second, early_far, *rest, count=count, shards=shards
    )


def tail_work(
    acc_a,
    acc_b,
    part_a,
    part_b,
    cosine,
    sine,
    gain,
    second,
    early_far,
    back_key_far,
    back_value_far,
    turned_far,
    query_far,
    pairs_far,
    x_far,
    middle_far,
    early_out,
    late_out,
    gains_out,
    input_out,
    *scratch,
    count,
    shards,
):
    scratch = list(scratch)
    halves = [scratch.pop(0) for _ in bits(shards)]
    (
        back_query,
        back_key,
        back_value,
        turned,
        weight,
        x,
        middle,
        early,
        given,
        early_slots,
        late_slots,
        gain_in,
        gain_sum,
        ring_send,
        ring_recv,
        half_send,
        half_recv,
        gain_send,
        gain_recv,
        near,
    ) = scratch
    micros = x.shape[0]
    chunks = 2 * count
    shard_rows = D // shards
    here, shard = lax.axis_index("ctx"), lax.axis_index("fsdp")
    place = ring_place(count)
    neighbour = (ring_index(place + 1, count), ring_index(place + count - 1, count))
    partners = [("fsdp", shard, bit) for bit in bits(shards)] + [("ctx", here, bit) for bit in bits(count)]

    copies = {}
    column = 0
    pieces = []
    for i, part in enumerate(early_far):
        pieces.append((f"early{i}", part, early.at[:, :, column : column + part.shape[2]]))
        column += part.shape[2]
    for number, (name, source, target) in enumerate(
        (
            *pieces,
            ("turned", turned_far, turned),
            ("back_key", back_key_far, back_key),
            ("back_value", back_value_far, back_value),
            ("query", query_far, weight.at[0]),
            ("pairs", pairs_far, weight.at[1:]),
            ("x", x_far, x),
            ("middle", middle_far, middle),
        )
    ):
        copies[name] = pltpu.make_async_copy(source, target, near.at[number])
        copies[name].start()

    def partner(axis, index, bit):
        return {axis: index + bit * (1 - 2 * ((index // bit) % 2))}

    barrier = pltpu.get_barrier_semaphore()
    known = [{"ctx": neighbour[0]}, {"ctx": neighbour[1]}] + [partner(*p) for p in partners]
    for device in known:
        pl.semaphore_signal(barrier, inc=1, device_id=device, device_id_type=pl.DeviceIdType.MESH)
    pl.semaphore_wait(barrier, len(known))

    sent = []

    def send(source, target, send_sem, recv_sem, device):
        copy = pltpu.make_async_remote_copy(
            source, target, send_sem, recv_sem, device_id=device, device_id_type=pl.DeviceIdType.MESH
        )
        copy.start()
        sent.append(copy)
        return copy

    def flow(number, first_source, source, slots, out):
        def home(side, hop):
            sign = 1 - 2 * side
            return side * count + (place - sign * hop + 2 * count) % count

        def start(hop):
            result = []
            for side in range(2):
                if hop == 1:
                    pair = first_source(home(side, 1)), slots(side, 0)
                elif hop < count:
                    pair = slots(side, hop - 2), slots(side, hop - 1)
                else:
                    chunk = home(side, hop - count)
                    pair = out(chunk), out(chunk)
                result.append(
                    send(
                        *pair,
                        ring_send.at[number, side, hop - 1],
                        ring_recv.at[number, side, hop - 1],
                        {"ctx": neighbour[side]},
                    )
                )
            return result

        def finish(hop, pending):
            for side in range(2):
                pending[side].wait_recv()
                if hop < count:
                    got = slots(side, hop - 1)
                    total = got[...].astype(F32) + source(home(side, 1 + hop))[...].astype(F32)
                    target = out(home(side, 0)) if hop == count - 1 else got
                    target[...] = total.astype(BF16)

        return start, finish

    class Run:
        def __init__(self, *arguments):
            self.start, self.finish = flow(*arguments)
            self.hop, self.pending = 0, None

        def advance(self):
            if self.hop:
                self.finish(self.hop, self.pending)
            self.hop += 1
            if self.hop <= 2 * count - 2:
                self.pending = self.start(self.hop)

        def done(self):
            return self.hop > 2 * count - 2

    width = early.shape[2]
    middle_column = width // HEAD_DIM // 2 * HEAD_DIM
    runs = []
    for number, cols in enumerate((slice(0, middle_column), slice(middle_column, width))):
        runs.append(
            Run(
                number,
                lambda c, cols=cols: early.at[c, :, cols],
                lambda c, cols=cols: early.at[c, :, cols],
                lambda side, slot, cols=cols: early_slots.at[side, slot, :, cols],
                lambda c, cols=cols: early_out.at[c, :, cols],
            )
        )

    sources = (back_query, back_key, back_value)

    def product(s, target, add):
        rows = turned[pl.ds(pl.multiple_of(s * shard_rows, shard_rows), shard_rows), :]
        for start in range(0, 3 * D, PIECE):
            column = start % D
            right = sources[start // D][:, :, column : column + PIECE].reshape(micros * ROWS, PIECE)
            value = nn(rows, right)
            if by_rows(shard_rows, chunks):
                value = value.reshape(chunks, shard_rows // chunks, PIECE)
                spots = [((slice(None), slice(None), slice(start, start + PIECE)), value)]
            else:
                step = target.shape[2]
                spots = [
                    (((start + c) // step,), value[:, c : c + step]) for c in range(0, PIECE, step)
                ]
            for spot, piece in spots:
                if add:
                    piece = target[spot].astype(F32) + piece.astype(BF16).astype(F32)
                target[spot] = piece.astype(BF16)

    if not by_rows(shard_rows, chunks):
        used = 3 * D // halves[0].shape[3]
        for c in range(used, chunks):
            given[:, c] = jnp.zeros_like(given[:, c])

    def bit_of(i):
        return (shard // (1 << i)) % 2

    def give(j):
        product(2 * j + 1 - bit_of(0), given.at[j], False)
        return send(
            given.at[j], halves[0].at[j], half_send.at[0, j], half_recv.at[0, j], partner("fsdp", shard, 1)
        )

    def halve_start(i):
        return [
            send(
                halves[i - 1].at[2 * j + 1 - bit_of(i)],
                halves[i].at[j],
                half_send.at[i, j],
                half_recv.at[i, j],
                partner("fsdp", shard, 1 << i),
            )
            for j in range(shards >> (i + 1))
        ]

    def halve_finish(i, j, copy):
        copy.wait_recv()
        if i == 0:
            product(2 * j + bit_of(0), halves[0].at[j], True)
            return

        def add(c, carry):
            halves[i][j, c] = (
                halves[i][j, c].astype(F32) + halves[i - 1][2 * j + bit_of(i), c].astype(F32)
            ).astype(BF16)
            return carry

        lax.fori_loop(0, chunks, add, 0)

    def unturn():
        for m in range(micros):
            for h in range(HEADS):
                acc, part = (acc_a, part_a) if h < SIDE else (acc_b, part_b)
                cols = slice(h % SIDE * HEAD_DIM, (h % SIDE + 1) * HEAD_DIM)
                value = (acc[m, :, cols].astype(F32) + part[m, :, cols].astype(F32)) * SCALE
                back_query[m, :, h * HEAD_DIM : (h + 1) * HEAD_DIM] = turn(
                    value, cosine[...], -sine[...]
                ).astype(BF16)

    def input_back(m):
        slope = nt(back_query[m], weight[0]) + nt(back_key[m], weight[1]) + nt(back_value[m], weight[2])
        value = x[m].astype(F32)
        scale = lax.rsqrt(jnp.mean(value * value, axis=-1, keepdims=True) + EPS)
        hat = value * scale
        first = jnp.sum((slope * hat).reshape(ROWS // 8, 8, D), axis=0)
        slope = slope * gain[...]
        input_out[m] = middle[m] + scale * (slope - hat * jnp.mean(slope * hat, axis=-1, keepdims=True))
        gain_sum[1] = first if m == 0 else gain_sum[1] + first

    def gains_ready():
        first = jnp.sum(gain_sum[1], axis=0, keepdims=True)
        other = jnp.sum(jnp.sum(second[...], axis=0), axis=0, keepdims=True)
        gain_sum[0] = jnp.concatenate([first, other, jnp.zeros((6, D), F32)], axis=0)

    def gain_start(i):
        return send(gain_sum.at[i], gain_in.at[i], gain_send.at[i], gain_recv.at[i], partner(*partners[i]))

    def gain_finish(i, copy):
        copy.wait_recv()
        gain_sum[i + 1] = gain_sum[i] + gain_in[i]

    stages = len(halves)
    late = []

    def advance():
        for run in runs:
            for each in (run, *late):
                if not each.done():
                    each.advance()

    for i in range(len(early_far)):
        copies[f"early{i}"].wait()
    advance()
    unturn()
    for name in ("turned", "back_key", "back_value"):
        copies[name].wait()
    order = [list(range(shards // 2))]
    if stages > 1:
        order = [
            [2 * j + 1 - bit_of(1) for j in range(shards // 4)],
            [2 * j + bit_of(1) for j in range(shards // 4)],
        ]
    half = None
    for numbers in order:
        given_now = []
        for j in numbers:
            given_now.append(give(j))
            advance()
        for j, copy in zip(numbers, given_now):
            halve_finish(0, j, copy)
            advance()
        if half is None and stages > 1:
            half = halve_start(1)
    for i in range(1, stages - 1):
        for j, copy in enumerate(half):
            halve_finish(i, j, copy)
        half = halve_start(i + 1)
        advance()
    for name in ("query", "pairs", "x", "middle"):
        copies[name].wait()
    for m in range(micros):
        if m == micros - 1:
            if stages > 1:
                halve_finish(stages - 1, 0, half[0])
            late.append(
                Run(
                    2,
                    lambda c: halves[-1].at[0, c],
                    lambda c: halves[-1].at[0, c],
                    lambda side, slot: late_slots.at[side, slot],
                    lambda c: late_out.at[c],
                )
            )
            advance()
        input_back(m)
        advance()
    gains_ready()
    for i in range(len(partners)):
        copy = gain_start(i)
        advance()
        gain_finish(i, copy)
    while not all(run.done() for run in runs + late):
        advance()
    gains_out[...] = gain_sum[len(partners)]
    for copy in sent:
        copy.wait_send()


def tail(received, own, angle, gain, second, early, back_key, back_value, turned, weights, x, middle, count, shards):
    micros = x.shape[0]
    chunks = 2 * count
    shard_rows = D // shards
    if by_rows(shard_rows, chunks):
        late = (chunks, shard_rows // chunks, 3 * D)
    else:
        late = (chunks, shard_rows, -(-3 * D // (chunks * HEAD_DIM)) * HEAD_DIM)
    exchanges = len(bits(shards)) + len(bits(count))
    early_shape = early[0].shape[:2] + (sum(part.shape[2] for part in early),)
    vmem = pl.BlockSpec(memory_space=pltpu.VMEM)
    anywhere = pl.BlockSpec(memory_space=pl.ANY)
    return pl.pallas_call(
        functools.partial(tail_kernel, count=count, shards=shards, parts=len(early)),
        in_specs=[vmem] * 8 + [anywhere] * (7 + len(early)),
        out_specs=[vmem] * 4,
        out_shape=[
            jax.ShapeDtypeStruct(early_shape, BF16),
            jax.ShapeDtypeStruct(late, BF16),
            jax.ShapeDtypeStruct((8, D), F32),
            seq_shape(micros, ROWS, D, dtype=F32),
        ],
        scratch_shapes=[pltpu.VMEM((shards // (2 * bit),) + late, BF16) for bit in bits(shards)]
        + [pltpu.VMEM((micros, ROWS, D), BF16)] * 3
        + [
            pltpu.VMEM(turned.shape, BF16),
            pltpu.VMEM((3, D, D), BF16),
            pltpu.VMEM((micros, ROWS, D), BF16),
            pltpu.VMEM((micros, ROWS, D), F32),
            pltpu.VMEM(early_shape, BF16),
            pltpu.VMEM((shards // 2,) + late, BF16),
            pltpu.VMEM((2, count - 1) + early_shape[1:], BF16),
            pltpu.VMEM((2, count - 1) + late[1:], BF16),
            pltpu.VMEM((exchanges, 8, D), F32),
            pltpu.VMEM((exchanges + 1, 8, D), F32),
            pltpu.SemaphoreType.DMA((3, 2, 2 * count - 2)),
            pltpu.SemaphoreType.DMA((3, 2, 2 * count - 2)),
            pltpu.SemaphoreType.DMA((len(bits(shards)), shards // 2)),
            pltpu.SemaphoreType.DMA((len(bits(shards)), shards // 2)),
            pltpu.SemaphoreType.DMA((exchanges,)),
            pltpu.SemaphoreType.DMA((exchanges,)),
            pltpu.SemaphoreType.DMA((7 + len(early),)),
        ],
        compiler_params=pltpu.CompilerParams(
            vmem_limit_bytes=60 * 2**20, collective_id=0, has_side_effects=True
        ),
        name="tail",
        cost_estimate=pl.CostEstimate(flops=12_000_000_000, bytes_accessed=300_000_000, transcendentals=0),
    )(
        *received,
        *own,
        *angle,
        gain,
        second,
        *early,
        back_key,
        back_value,
        turned,
        *weights,
        x,
        middle,
    )


def to_chunks(parts, count):
    rows = parts[0].shape[0]
    chunks = 2 * count
    if by_rows(rows, chunks):
        return [part.reshape(chunks, rows // chunks, -1) for part in parts]
    value = jnp.concatenate(parts, axis=1)
    width = value.shape[1]
    step = -(-width // (chunks * HEAD_DIM)) * HEAD_DIM
    value = jnp.pad(value, [(0, 0), (0, step * chunks - width)])
    return [jnp.moveaxis(value.reshape(rows, chunks, step), 1, 0)]


def from_chunks(value, rows, width):
    if by_rows(rows, value.shape[0]):
        return value.reshape(rows, width)
    return jnp.moveaxis(value, 0, 1).reshape(rows, -1)[:, :width]


def body(
    tokens,
    cotangent,
    query_weight,
    key_weight,
    value_weight,
    output_weight,
    gate_weight,
    up_weight,
    down_weight,
    first_gain,
    second_gain,
    cache_keys,
    cache_values,
    block_indices,
    partner,
):
    count = lax.axis_size("ctx")
    here = lax.axis_index("ctx")
    micros = tokens.shape[0]
    rows = micros * ROWS
    onward, backward = ring_pairs(count)

    def gather(value):
        return lax.all_gather(value, "fsdp", axis=0, tiled=True)

    shards = lax.axis_size("fsdp")
    requested = block_indices.reshape(micros, -1)
    own_rows = D // shards
    indices, gains = share(
        jnp.pad(requested, ((0, -micros % 8), (0, 0))),
        jnp.pad(
            jnp.stack([first_gain, second_gain]).astype(F32), ((0, 6), (0, -own_rows % HEAD_DIM))
        ),
        count,
        shards,
    )
    indices = jnp.moveaxis(indices[:, :micros], 0, 1)
    gains = jnp.moveaxis(gains[:, :2, :own_rows], 0, 1).reshape(2, D)
    full_query = gather(query_weight)
    pair_weights = lax.all_gather(jnp.stack([key_weight, value_weight]), "fsdp", axis=1, tiled=True)
    full_output = gather(output_weight)
    full_gate = gather(gate_weight)
    full_up = gather(up_weight)
    full_down = gather(down_weight)
    gain_one = gains[0:1]
    gain_two = gains[1:2]

    pieces_at = jnp.stack([here, 2 * count - 1 - here])
    positions = (pieces_at[:, None] * HALF + jnp.arange(HALF, dtype=jnp.int32)[None, :]).reshape(ROWS)
    inverse = 10000.0 ** (-jnp.arange(HEAD_DIM // 2, dtype=F32) * 2.0 / HEAD_DIM)
    phase = positions.astype(F32)[:, None] * inverse[None, :]
    cosine = jnp.tile(jnp.cos(phase), (1, 2))
    sine = jnp.sin(phase)
    sine = jnp.concatenate([-sine, sine], axis=1)

    meta, cap = make_meta(indices, partner, cache_keys.shape[1] // BLOCK, count)
    x = tokens.reshape(micros, ROWS, D)
    some = count * 3 // 8
    memory = collect(meta, cache_keys, cache_values, count, cap, range(some))
    x, memory = lax.optimization_barrier((x, memory))
    normed_low, qa, qb = project_query(x, gain_one, full_query, cosine, sine)
    meta, qa, qb = lax.optimization_barrier((meta, qa, qb))
    memory = collect(meta, cache_keys, cache_values, count, cap, range(some, count), memory)
    queries = [(qa, qb)]
    for step in range(1, count):
        qa, qb = lax.ppermute(qa, "ctx", onward), lax.ppermute(qb, "ctx", backward)
        if step == 1:
            qa, qb, memory = lax.optimization_barrier((qa, qb, memory))
            keys, values, normed_turned = project_pairs(normed_low, pair_weights, cosine, sine)
        if step == 2:
            qa, qb, keys, values = lax.optimization_barrier((qa, qb, keys, values))
        queries.append((qa, qb))
    memory_keys, memory_values = memory
    for step in range(2, count - 1):
        queries[step], queries[step + 1] = lax.optimization_barrier((queries[step], queries[step + 1]))


    acc = ()
    for step in list(range(1, count)) + [0]:
        pa, pb, ta, tb = attend(
            meta, *queries[step], keys, values, memory_keys, memory_values, step, count, cap
        )
        if acc:
            acc = (lax.ppermute(acc[0], "ctx", onward), lax.ppermute(acc[1], "ctx", backward))
        if step == 0:
            mixed, mixed_low, total, middle, middle_low = finish(
                *acc, pa, pb, ta, tb, x, full_output, gain_two
            )
        else:
            acc = combine(acc, (pa, pb), (ta, tb))

    incoming = cotangent.reshape(micros, ROWS, D)
    layer_output, back_mid_normed, gradient_gate, gradient_up, gradient_down = feed(
        middle_low, incoming, middle, full_gate, full_up, full_down
    )
    da, db, back_middle, back_attn, gain_part = prepare(
        back_mid_normed, middle, incoming, gain_two, full_output, mixed, total
    )

    def scatter(part):
        return lax.psum_scatter(part, "fsdp", scatter_dimension=0, tiled=True)

    slopes = [(da, db)]
    for _ in range(count - 1):
        da, db = slopes[-1]
        slopes.append((lax.ppermute(da, "ctx", onward), lax.ppermute(db, "ctx", backward)))

    slopes[1], back_attn = lax.optimization_barrier((slopes[1], back_attn))
    gradient_output = jnp.einsum(
        "tc,td->cd", mixed_low.reshape(rows, D), back_attn.reshape(rows, D), preferred_element_type=F32
    ).astype(BF16)
    early = [
        scatter(part).reshape(own_rows, -1)
        for part in (gradient_down, gradient_gate, gradient_up, gradient_output)
    ]
    early_width = sum(part.shape[1] for part in early)
    slopes[-1], early[0] = lax.optimization_barrier((slopes[-1], early[0]))
    for step in range(1, count - 1):
        slopes[step], slopes[step + 1] = lax.optimization_barrier((slopes[step], slopes[step + 1]))
    middle_step = count // 2 + 1
    first_sums = key_gradients(meta, keys, values, queries, slopes, range(middle_step))
    slopes[middle_step - 2], first_sums = lax.optimization_barrier((slopes[middle_step - 2], first_sums))
    acc = ()
    for step in range(count):
        part = unattend(
            meta, *queries[step], *slopes[step], keys, values, memory_keys, memory_values, step, count, cap
        )
        if step == 0:
            own = part
            continue
        if acc:
            acc = (lax.ppermute(acc[0], "ctx", onward), lax.ppermute(acc[1], "ctx", backward))
        acc = combine(acc, part)
    back_key, back_value = key_gradients(
        meta, keys, values, queries, slopes, range(middle_step, count), first_sums, (cosine, sine)
    )
    ra, rb = lax.ppermute(acc[0], "ctx", onward), lax.ppermute(acc[1], "ctx", backward)
    early_sum, late_sum, gain_changes, input_gradient = tail(
        (ra, rb),
        own,
        (cosine, sine),
        gain_one,
        gain_part,
        to_chunks(early, count),
        back_key,
        back_value,
        normed_turned,
        (full_query, pair_weights),
        x,
        back_middle,
        count,
        shards,
    )
    early = from_chunks(early_sum, own_rows, early_width).astype(F32)
    three = from_chunks(late_sum, D // shards, 3 * D).astype(F32)
    units = gate_weight.shape[1]
    gain_changes = lax.dynamic_slice_in_dim(
        gain_changes, lax.axis_index("fsdp") * own_rows, own_rows, axis=1
    )
    return (
        layer_output.reshape(tokens.shape),
        input_gradient.reshape(tokens.shape),
        three[:, :D],
        three[:, D : 2 * D],
        three[:, 2 * D :],
        early[:, 3 * units :],
        early[:, units : 2 * units],
        early[:, 2 * units : 3 * units],
        early[:, :units].reshape(down_weight.shape),
        gain_changes[0],
        gain_changes[1],
    )


def solution(mesh):
    split = P("fsdp", "ctx", None, None, None)
    shard = P("fsdp", None)
    return jax.shard_map(
        body,
        mesh=mesh,
        in_specs=(
            split,
            split,
            *([shard] * 7),
            P("fsdp"),
            P("fsdp"),
            P("fsdp", "ctx", None),
            P("fsdp", "ctx", None),
            P("fsdp", "ctx", None, None, None, None),
            P("fsdp"),
        ),
        out_specs=(split, split, *([shard] * 7), P("fsdp"), P("fsdp")),
        check_vma=False,
    )
```
